512 devices in a mesh: dom: 128 (over x, y, z_hi), feat: 4 (over z_lo, core).
Axes of the slice: x: 4, y: 8, z: 8 (z_hi: 4, z_lo: 2; z = z_hi * 2 + z_lo), core: 2. Of those that a mesh axis runs over, the one named last changes fastest.
Arguments:
- node_state: bfloat16 [131072, 512], P('dom', 'feat'), may hold values from -6 to 6
- w_dst: bfloat16 [2, 512, 512], P(None, None, 'feat'), may hold values from -0.25 to 0.25
- w_src: bfloat16 [2, 512, 512], P(None, None, 'feat'), may hold values from -0.25 to 0.25
- w_msg: bfloat16 [2, 512, 512], replicated, may hold values from -0.25 to 0.25
- w_node_in: bfloat16 [2, 1024, 512], P(None, None, 'feat'), may hold values from -0.1875 to 0.1875
- w_node_out: bfloat16 [2, 512, 512], P(None, None, 'feat'), may hold values from -0.25 to 0.25
- msg_vectors: float32 [2, 2, 512], replicated, may hold values from -3 to 3
- msg_gain: float32 [2, 512], replicated, may hold values from 0.1 to 1.9
- node_vectors: float32 [2, 4, 512], P(None, None, 'feat'), may hold values from -3 to 3
- node_gain: float32 [2, 512], P(None, 'feat'), may hold values from 0.1 to 1.9
- nbr_blocks: int32 [1024, 6], P('dom'), may hold values from 0 to 1023, as said below
- edge_count: int32 [1024, 6], P('dom'), may hold values from 1 to 128, as said below
- edge_src: int32 [1024, 6, 128], P('dom'), may hold values from 0 to 127
- edge_dst: int32 [1024, 6, 128], P('dom'), may hold values from 0 to 127
Outputs:
- new_state: bfloat16 [131072, 512], P('dom', 'feat')
The draws below stay inside these ranges and needn't reach their ends.
Inputs may be any that keep to these rules, and one draw needn't show every extreme that they name: `nbr_blocks`: each row names 6 different blocks within 8 blocks of its own block b; its first entry is b. `edge_count`: the first entry of every row is 128.
All inputs are finite; a program needn't handle non-finite values.
Results may differ from the reference program's by a relative error of at most 0.017.
Values may be sent and summed in bfloat16 or wider, within the bound.
No kernel may reach another device: no remote copies, remote signals or barrier semaphores. Data moves between devices by JAX's collectives and lax.ppermute only.
A program may use at most 64 MiB of HBM per device.

```python
import jax
import jax.numpy as jnp
from jax import lax

D = 512
BLK = 128
K = 6
EC = 128
LAYERS = 2
NB = 8
NBLOCKS = 1024
NODES = 131072


def draw_nbr_blocks(key, part):
    key = jax.random.fold_in(key, 11)
    window_len = 2 * NB + 1
    offsets = jnp.arange(window_len, dtype=jnp.int32) - NB
    block_ids = jnp.arange(NBLOCKS, dtype=jnp.int32)
    targets = block_ids[:, None] + offsets[None, :]
    inside = (targets >= 0) & (targets < NBLOCKS)
    lane_ids = jnp.broadcast_to(jnp.arange(window_len, dtype=jnp.int32)[None, :], (NBLOCKS, window_len))
    scores = jax.random.randint(key, (NBLOCKS, window_len), 0, 1 << 16) * window_len + lane_ids + window_len
    scores = jnp.where(inside, scores, lane_ids)
    scores = jnp.where(offsets[None, :] == 0, scores + (1 << 17) * window_len, scores)
    chosen = lax.top_k(scores, K)[1]
    return jnp.take_along_axis(targets, chosen, axis=1).astype(jnp.int32)


def draw_edge_count(key, part):
    key = jax.random.fold_in(key, 23)
    counts = jax.random.randint(key, (NBLOCKS, K), 1, EC + 1)
    first_slot = jnp.arange(K, dtype=jnp.int32)[None, :] == 0
    return jnp.where(first_slot, EC, counts).astype(jnp.int32)


def touch_ends(array, key, low, largest):
    longest = array.shape.index(max(array.shape))
    spots = []
    for shift in (0, 1):
        where = [jax.random.randint(jax.random.fold_in(key, axis), (), 0, length) for axis, length in enumerate(array.shape)]
        where[longest] = (where[longest] + shift) % array.shape[longest]
        spots.append(tuple(where))
    return array.at[spots[0]].set(low).at[spots[1]].set(largest)


def level_of(rng, extent, split, low, high):
    factor_of, own = 1.0, jax.random.fold_in(rng, 6)
    for axis_at, blocks in split:
        steps = jnp.exp(jax.random.uniform(jax.random.fold_in(own, axis_at), (blocks,), jnp.float32, low / len(split), high / len(split)))
        factor_of = factor_of * jnp.repeat(steps, extent[axis_at] // blocks).reshape([-1 if axis == axis_at else 1 for axis in range(len(extent))])
    return factor_of


def scatter_about(key, dims, scale, bound, cuts=(), kind=jnp.bfloat16):
    gain = level_of(key, dims, cuts, -0.22, 0.18) if cuts else 1.0
    entries = jax.random.normal(key, dims, jnp.float32) * scale * gain
    return jnp.minimum(jnp.maximum(entries, -bound), bound).astype(kind)


def setup_inputs(seed: int = 0) -> dict:
    seeds = jax.random.split(jax.random.key(seed), 15)
    return {
        "node_state": scatter_about(seeds[0], (NODES, D), 1.0, 6.0, ((0, 128), (1, 4))),
        "w_dst": scatter_about(seeds[1], (LAYERS, D, D), D ** -0.5, 0.25, ((2, 4),)),
        "w_src": scatter_about(seeds[2], (LAYERS, D, D), D ** -0.5, 0.25, ((2, 4),)),
        "w_msg": scatter_about(seeds[3], (LAYERS, D, D), D ** -0.5, 0.25),
        "w_node_in": scatter_about(seeds[4], (LAYERS, 2 * D, D), (2 * D) ** -0.5, 0.1875, ((2, 4),)),
        "w_node_out": scatter_about(seeds[5], (LAYERS, D, D), D ** -0.5, 0.25, ((2, 4),)),
        "msg_vectors": scatter_about(seeds[6], (LAYERS, 2, D), 0.5, 3.0, (), jnp.float32),
        "msg_gain": jnp.clip(1.0 + 0.18 * jax.random.normal(seeds[7], (LAYERS, D), jnp.float32), 0.1, 1.9),
        "node_vectors": scatter_about(seeds[8], (LAYERS, 4, D), 0.5, 3.0, ((2, 4),), jnp.float32),
        "node_gain": jnp.clip(1.0 + 0.18 * jax.random.normal(seeds[9], (LAYERS, D), jnp.float32), 0.1, 1.9),
        "nbr_blocks": draw_nbr_blocks(jax.random.fold_in(seeds[14], 71), 0),
        "edge_count": draw_edge_count(jax.random.fold_in(seeds[14], 71), 0),
        "edge_src": touch_ends(jax.random.randint(seeds[12], (NBLOCKS, K, EC), 0, BLK), jax.random.fold_in(seeds[12], 1), 0, BLK - 1).astype(jnp.int32),
        "edge_dst": touch_ends(jax.random.randint(seeds[13], (NBLOCKS, K, EC), 0, BLK), jax.random.fold_in(seeds[13], 1), 0, BLK - 1).astype(jnp.int32),
    }


epsilon = 1e-05

def normalize(values, gain_vec, shift_vec):
    centre = lax.optimization_barrier(jnp.mean(values, axis=-1, keepdims=True))
    shifted = values - centre
    spread = lax.optimization_barrier(jnp.mean(shifted * shifted, axis=-1, keepdims=True))
    return shifted * lax.rsqrt(spread + epsilon) * gain_vec + shift_vec

def reference(node_state, w_dst, w_src, w_msg, w_node_in, w_node_out, msg_vectors, msg_gain, node_vectors, node_gain, nbr_blocks, edge_count, edge_src, edge_dst):
    slot_count = K * EC
    group_count = NBLOCKS // NB
    src_rows = (nbr_blocks[:, :, None] * BLK + edge_src).reshape(group_count, NB, slot_count)
    dst_local = edge_dst.reshape(group_count, NB, slot_count)
    edge_live = (jnp.arange(EC, dtype=jnp.int32)[None, None, :] < edge_count[:, :, None]).reshape(group_count, NB, slot_count)
    group_ids = jnp.arange(group_count, dtype=jnp.int32)
    positions = jnp.arange(BLK, dtype=jnp.int32)
    latent = node_state
    for layer_index in range(LAYERS):
        dst_terms = (jnp.dot(latent, w_dst[layer_index], preferred_element_type=jnp.float32) + node_vectors[layer_index, 0]).astype(jnp.bfloat16)
        src_terms = jnp.dot(latent, w_src[layer_index], preferred_element_type=jnp.float32).astype(jnp.bfloat16)
        weight_msg = w_msg[layer_index].astype(jnp.float32)

        def group_sum(inputs):
            group_id, senders, receivers, live_flags = inputs
            block_rows = (group_id * NB + jnp.arange(NB, dtype=jnp.int32)) * BLK
            dst_rows = receivers + block_rows[:, None]
            edge_hidden = jax.nn.relu(dst_terms[dst_rows].astype(jnp.float32) + src_terms[senders].astype(jnp.float32)).astype(jnp.bfloat16)
            message = jnp.einsum('bed,df->bef', edge_hidden.astype(jnp.float32), weight_msg) + msg_vectors[layer_index, 0]
            normed = normalize(message, msg_gain[layer_index], msg_vectors[layer_index, 1])
            one_hot = ((receivers[:, None, :] == positions[None, :, None]) & live_flags[:, None, :]).astype(jnp.float32)
            summed = jnp.einsum('bne,bed->bnd', one_hot, normed, precision=lax.Precision.HIGHEST)
            return summed.reshape(NB * BLK, D)
        aggregate = lax.map(group_sum, (group_ids, src_rows, dst_local, edge_live)).reshape(NODES, D).astype(jnp.bfloat16)
        pre_act = jnp.dot(latent, w_node_in[layer_index, :D], preferred_element_type=jnp.float32)
        pre_act = pre_act + jnp.dot(aggregate, w_node_in[layer_index, D:], preferred_element_type=jnp.float32)
        node_hidden = jax.nn.relu(pre_act + node_vectors[layer_index, 1]).astype(jnp.bfloat16)
        node_out = jnp.dot(node_hidden, w_node_out[layer_index], preferred_element_type=jnp.float32) + node_vectors[layer_index, 2]
        latent = (latent.astype(jnp.float32) + normalize(node_out, node_gain[layer_index], node_vectors[layer_index, 3])).astype(jnp.bfloat16)
    return latent
```

```python
import jax
import jax.numpy as jnp
from jax import lax
from jax.experimental import pallas as pl
from jax.experimental.pallas import tpu as pltpu
from jax.sharding import PartitionSpec as P

LAYERS = 2
EPSILON = 1e-05
BOTH = ("dom", "feat")
F32 = jnp.float32
BF16 = jnp.bfloat16
VECTOR_ROWS = 16


def dot(a, b):
    return jnp.dot(a, b, preferred_element_type=F32)


def exchange(value, mask):
    total = lax.axis_size(BOTH)
    return lax.ppermute(value, BOTH, [(i, i ^ mask) for i in range(total)])


def shifted(value, step):
    total = lax.axis_size(BOTH)
    return lax.ppermute(value, BOTH, [(i, i - step) for i in range(total) if 0 <= i - step < total])


def prepare_kernel(count_ref, src_ref, dst_ref, dst_row_ref, gather_ref, collect_ref):
    blocks, slots, edges, _ = gather_ref.shape
    lanes = lax.broadcasted_iota(jnp.int32, (edges, edges), 1)
    rows = lax.broadcasted_iota(jnp.int32, (edges, edges), 0)
    for j in range(blocks):
        for k in range(slots):
            to = dst_ref[j][:, k : k + 1] == lanes
            frm = src_ref[j][:, k : k + 1] == lanes
            gather_ref[j, k, :, :edges] = to.astype(F32).astype(BF16)
            gather_ref[j, k, :, edges:] = frm.astype(F32).astype(BF16)
            live = (dst_row_ref[j, k : k + 1, :] == rows) & (lanes < count_ref[j, k])
            collect_ref[j, :, k * edges : (k + 1) * edges] = live.astype(F32).astype(BF16)


def layer_kernel(layer, first, *refs):
    (place_ref, nbr_ref, h_ref, m4, m2, p2, p4, mate, mates, w0, w1, w2, w3, vec_in, wmsg_ref, mvec_ref,
     mgain_ref, gather_ref, collect_ref) = refs[:19]
    if first:
        out_ref, vec_ref, window, receive, hidden, normed, agg = refs[19:]
    else:
        out_ref, window, receive, hidden, normed, agg = refs[19:]
    f = place_ref[0]
    side = place_ref[1]
    base = place_ref[2]
    shards = (w0, w1, w2, w3)
    blocks, slots, edges, _ = gather_ref.shape
    width = wmsg_ref.shape[-1]
    part = width // 4

    def cols(lo, hi):
        return jnp.concatenate([w[lo:hi, :] for w in shards], axis=1)

    def wide(ref):
        return jnp.concatenate([ref[i] for i in range(4)], axis=1)

    if first:
        end = 5 * width
        for m, w in enumerate(shards):
            rows = w[end : end + 3 * VECTOR_ROWS, :].astype(F32)
            vec_ref[m] = (
                rows[:VECTOR_ROWS] + rows[VECTOR_ROWS : 2 * VECTOR_ROWS] + rows[2 * VECTOR_ROWS :]
            )
        vectors = vec_ref
    else:
        vectors = vec_in

    def vector(i):
        row = layer * 5 + i
        return jnp.concatenate([vectors[m, row : row + 1, :] for m in range(4)], axis=1)

    own = wide(h_ref)
    w_src = cols(0, width)
    pieces = [(h_ref, 5), (m4, 1), (m2, 3), (p2, 7), (p4, 9)]
    for ref, at in pieces:
        window[pl.ds(2 * at * edges, 2 * edges), :] = dot(wide(ref), w_src).astype(BF16)
    over = 1 - 2 * side
    for i, s in enumerate((None, -4, -2, 2, 4)):
        at = 5 + (0 if s is None else s) + over
        ref = mate if s is None else mates.at[i - 1]
        window[pl.ds(pl.multiple_of(2 * at * edges, 2 * edges), 2 * edges), :] = dot(wide(ref), w_src).astype(BF16)
    receive[...] = (dot(own, cols(width, 2 * width)) + vector(0)).astype(BF16)

    w_msg = jnp.concatenate([wmsg_ref[f ^ m] for m in range(4)], axis=0)
    bias = mvec_ref[layer, 0:1, :]
    offset = mvec_ref[layer, 1:2, :]
    gain = mgain_ref[layer : layer + 1, :]
    for j in range(blocks):
        to = receive[j * edges : (j + 1) * edges, :]
        for k in range(slots):
            at = (nbr_ref[2 * f + j, k] - base) * edges
            frm = window[pl.ds(pl.multiple_of(at, edges), edges), :]
            terms = dot(gather_ref[j, k], jnp.concatenate([to, frm], axis=0))
            hidden[k * edges : (k + 1) * edges, :] = jnp.maximum(terms, 0.0).astype(BF16)
        for k in range(0, slots, 2):
            rows = slice(k * edges, (k + 2) * edges)
            message = dot(hidden[rows, :], w_msg) + bias
            centred = message - jnp.mean(message, axis=1, keepdims=True)
            spread = jnp.mean(centred * centred, axis=1, keepdims=True)
            normed[rows, :] = (centred * lax.rsqrt(spread + EPSILON)).astype(BF16)
        collect = collect_ref[j]
        degree = jnp.sum(collect.astype(F32), axis=1, keepdims=True)
        total = dot(collect, normed[...]) * gain + degree * offset
        agg[j * edges : (j + 1) * edges, :] = total.astype(BF16)

    pre = dot(own, cols(2 * width, 3 * width)) + dot(agg[...], cols(3 * width, 4 * width)) + vector(1)
    inner = jnp.maximum(pre, 0.0).astype(BF16)

    def out_rows(w):
        at = 4 * width
        return jnp.concatenate(
            [w[pl.ds(pl.multiple_of(at + (f ^ m) * part, part), part), :] for m in range(4)], axis=0
        )

    w_out = jnp.concatenate([out_rows(w) for w in shards], axis=1)
    node = dot(inner, w_out) + vector(2)
    centred = node - jnp.mean(node, axis=1, keepdims=True)
    spread = jnp.mean(centred * centred, axis=1, keepdims=True)
    change = centred * lax.rsqrt(spread + EPSILON) * vector(4) + vector(3)
    for m in range(4):
        piece = change[:, m * part : (m + 1) * part]
        out_ref[f ^ m] = (h_ref[f ^ m].astype(F32) + piece).astype(BF16)


def per_device(
    node_state,
    w_dst,
    w_src,
    w_msg,
    w_node_in,
    w_node_out,
    msg_vectors,
    msg_gain,
    node_vectors,
    node_gain,
    nbr_blocks,
    edge_count,
    edge_src,
    edge_dst,
):
    width = w_msg.shape[1]
    part = width // 4
    block_count, slots = nbr_blocks.shape
    edges = edge_src.shape[2]
    mine = block_count // 4
    rows = mine * edges
    feat = lax.axis_index("feat")
    chain = lax.axis_index("dom") * 4 + feat
    place = jnp.stack([feat, feat % 2, mine * (chain - 5)]).astype(jnp.int32)

    vec = jnp.concatenate([node_vectors, node_gain[:, None, :]], axis=1).reshape(LAYERS * 5, part)
    vec = jnp.pad(vec, ((0, VECTOR_ROWS - LAYERS * 5), (0, 0)))
    high = lax.reduce_precision(vec, 8, 7)
    middle = lax.reduce_precision(vec - high, 8, 7)
    low = vec - high - middle
    packs = []
    for layer in range(LAYERS):
        group = [w_src[layer], w_dst[layer], w_node_in[layer], w_node_out[layer]]
        if layer == 0:
            group += [high.astype(BF16), middle.astype(BF16), low.astype(BF16)]
        packs.append(jnp.concatenate(group, axis=0))

    def spread_weights(pack):
        across = exchange(pack, 2)
        return pack, exchange(pack, 1), across, exchange(across, 1)

    src = lax.dynamic_slice_in_dim(edge_src, feat * mine, mine, 0)
    dst = lax.dynamic_slice_in_dim(edge_dst, feat * mine, mine, 0)
    count = lax.dynamic_slice_in_dim(edge_count, feat * mine, mine, 0)
    vmem = pl.BlockSpec(memory_space=pltpu.VMEM)
    smem = pl.BlockSpec(memory_space=pltpu.SMEM)
    gather, collect = pl.pallas_call(
        prepare_kernel,
        out_shape=(
            jax.ShapeDtypeStruct((mine, slots, edges, 2 * edges), BF16),
            jax.ShapeDtypeStruct((mine, edges, slots * edges), BF16),
        ),
        in_specs=[smem, vmem, vmem, vmem],
        out_specs=(vmem, vmem),
        name="one_hots",
    )(count, jnp.swapaxes(src, 1, 2), jnp.swapaxes(dst, 1, 2), dst)

    latent = lax.all_to_all(node_state.reshape(4, rows, part), "feat", split_axis=0, concat_axis=0, tiled=True)
    weights = spread_weights(packs[0])
    vectors = jnp.zeros((8, 128), F32)
    for layer in range(LAYERS):
        near = [shifted(latent, s) for s in (-4, -2, 2, 4)]
        mate = exchange(latent, 1)
        mates = exchange(jnp.stack(near), 1)
        if layer == 0:
            later, mates = lax.optimization_barrier((packs[1], mates))
        out_shape = [jax.ShapeDtypeStruct((4, rows, part), BF16)]
        if layer == 0:
            out_shape.append(jax.ShapeDtypeStruct((4, VECTOR_ROWS, part), F32))
        result = pl.pallas_call(
            lambda *refs, layer=layer: layer_kernel(layer, layer == 0, *refs),
            out_shape=out_shape,
            in_specs=[smem, smem] + [vmem] * 17,
            out_specs=[vmem] * len(out_shape),
            scratch_shapes=[
                pltpu.VMEM((22 * edges, width), BF16),
                pltpu.VMEM((rows, width), BF16),
                pltpu.VMEM((slots * edges, width), BF16),
                pltpu.VMEM((slots * edges, width), BF16),
                pltpu.VMEM((rows, width), BF16),
            ],
            compiler_params=pltpu.CompilerParams(vmem_limit_bytes=48 * 1024 * 1024),
            name=f"layer{layer}",
        )(
            place, nbr_blocks, latent, *near, mate, mates, *weights, vectors,
            w_msg[layer].reshape(4, part, width), msg_vectors, msg_gain, gather, collect,
        )
        if layer == 0:
            latent, vectors = result
            weights = spread_weights(later)
        else:
            latent = result[0]
    out = lax.all_to_all(latent, "feat", split_axis=0, concat_axis=0, tiled=True)
    return out.reshape(4 * rows, part)


def solution(mesh):
    placed = (
        P("dom", "feat"),
        P(None, None, "feat"),
        P(None, None, "feat"),
        P(),
        P(None, None, "feat"),
        P(None, None, "feat"),
        P(),
        P(),
        P(None, None, "feat"),
        P(None, "feat"),
        P("dom", None),
        P("dom", None),
        P("dom", None, None),
        P("dom", None, None),
    )
    return jax.shard_map(
        per_device, mesh=mesh, in_specs=placed, out_specs=P("dom", "feat"), check_vma=False
    )
```

```python
import jax
import jax.numpy as jnp
from jax import lax
from jax.experimental import pallas as pl
from jax.experimental.pallas import tpu as pltpu
from jax.sharding import PartitionSpec as P

LAYERS = 2
EPSILON = 1e-05
BOTH = ("dom", "feat")
F32 = jnp.float32
BF16 = jnp.bfloat16
VECTOR_ROWS = 16
ORDER = (0, 2, 1, 3)
FLIPPED = (1, 0, 3, 2)
STRAIGHT = (0, 1, 2, 3)
UNROLL = 4
LIST = 32
VMEM = pl.BlockSpec(memory_space=pltpu.VMEM)
SMEM = pl.BlockSpec(memory_space=pltpu.SMEM)


def dot(a, b):
    return jnp.dot(a, b, preferred_element_type=F32)


def exchange(value, mask):
    total = lax.axis_size(BOTH)
    return lax.ppermute(value, BOTH, [(i, i ^ mask) for i in range(total)])


def pass_on(value):
    total = lax.axis_size(BOTH)
    pairs = [(i, i + (2 if i % 2 == 0 else -2)) for i in range(total)]
    return lax.ppermute(value, BOTH, [(i, t) for i, t in pairs if 0 <= t < total])


def prepare_kernel(place_ref, nbr_ref, count_ref, src_ref, dst_ref, dst_row_ref, gather_ref, collect_ref, degree_ref, meta_ref):
    last, edges, _ = gather_ref.shape
    slots = nbr_ref.shape[1]
    blocks = last // slots
    core, first, base = place_ref[1], place_ref[2], place_ref[3]
    lanes = lax.broadcasted_iota(jnp.int32, (edges, edges), 1)
    rows = lax.broadcasted_iota(jnp.int32, (edges, edges), 0)
    for i in range(LIST):
        meta_ref[0, i] = last - 1
        meta_ref[1, i] = last - 1
        meta_ref[2, i] = 0
    near, far = jnp.int32(0), jnp.int32(0)
    for j in range(blocks):
        to = dst_ref[first + j]
        frm = src_ref[first + j]
        to_row = dst_row_ref[first + j]
        degree = jnp.zeros((edges, edges), F32)
        for k in range(slots):
            s = j * slots + k
            gather_ref[s, :, :edges] = (to[:, k : k + 1] == lanes).astype(F32).astype(BF16)
            gather_ref[s, :, edges:] = (frm[:, k : k + 1] == lanes).astype(F32).astype(BF16)
            live = ((to_row[k : k + 1, :] == rows) & (lanes < count_ref[first + j, k])).astype(F32)
            collect_ref[s] = live.astype(BF16)
            degree = degree + live
            place = nbr_ref[first + j, k] - base
            step = (place + 2 * blocks) // blocks - 2
            hops = jnp.abs(step)
            meta_ref[2, s] = hops * blocks + place - step * blocks
            mine = jnp.where(step == 0, core == j // (blocks // 2), (step > 0) == (core == 1))
            is_far = mine & (hops == 2)
            is_near = mine & (hops < 2)

            @pl.when(is_near)
            def _():
                meta_ref[0, near] = s

            @pl.when(is_far)
            def _():
                meta_ref[1, far] = s

            near = near + is_near.astype(jnp.int32)
            far = far + is_far.astype(jnp.int32)
        degree_ref[j * edges : (j + 1) * edges, :] = jnp.broadcast_to(
            jnp.sum(degree, axis=1, keepdims=True), (edges, edges)
        )
    meta_ref[3, 0] = near
    meta_ref[3, 1] = far
    gather_ref[last - 1] = jnp.zeros(gather_ref.shape[1:], BF16)
    collect_ref[last - 1] = jnp.zeros(collect_ref.shape[1:], BF16)


def wide(ref, order=STRAIGHT):
    return jnp.concatenate([ref[i] for i in order], axis=1)


def weight(shards, f, half, base, mixed):
    part = shards[0].shape[-1]
    rows = []
    for i in range(4):
        g = f ^ ORDER[i] if mixed else i
        cols = []
        for m, w in enumerate(shards):
            at = g // 2 if m < 2 else (g // 2) ^ half
            start = base + (g % 2) * part
            if mixed:
                start = pl.multiple_of(start, part)
            cols.append(w[at, pl.ds(start, part), :])
        rows.append(jnp.concatenate(cols, axis=1))
    return jnp.concatenate(rows, axis=0)


def vector(vectors, layer, i):
    row = layer * 5 + i
    return jnp.concatenate([vectors[m, row : row + 1, :] for m in range(4)], axis=1)


def run_edges(which, shift, layer, f, meta_ref, receive, window, gather_ref, collect_ref, wmsg_ref, mvec_ref, hidden, normed, acc):
    slots = 6
    edges = gather_ref.shape[1]
    w_msg = jnp.concatenate([wmsg_ref[f ^ m] for m in range(4)], axis=0)
    bias = mvec_ref[layer, 0:1, :]

    def body(step, carry):
        ids = [meta_ref[which, step * UNROLL + u] for u in range(UNROLL)]
        blocks = [jnp.minimum(s // slots, 3) for s in ids]
        for u, (s, j) in enumerate(zip(ids, blocks)):
            at = meta_ref[2, s] - shift
            if which == 1:
                at = jnp.maximum(at, 0)
            to = receive[pl.ds(pl.multiple_of(j * edges, edges), edges), :]
            frm = window[pl.ds(pl.multiple_of(at * edges, edges), edges), :]
            terms = dot(gather_ref[s], jnp.concatenate([to, frm], axis=0))
            hidden[u * edges : (u + 1) * edges, :] = jnp.maximum(terms, 0.0).astype(BF16)
        for v in range(0, UNROLL, 2):
            rows = slice(v * edges, (v + 2) * edges)
            message = dot(hidden[rows, :], w_msg) + bias
            centred = message - jnp.mean(message, axis=1, keepdims=True)
            spread = jnp.mean(centred * centred, axis=1, keepdims=True)
            normed[rows, :] = (centred * lax.rsqrt(spread + EPSILON)).astype(BF16)
        for u, (s, j) in enumerate(zip(ids, blocks)):
            rows = pl.ds(pl.multiple_of(j * edges, edges), edges)
            acc[rows, :] = acc[rows, :] + dot(collect_ref[s], normed[u * edges : (u + 1) * edges, :])
        return carry

    lax.fori_loop(0, (meta_ref[3, which] + UNROLL - 1) // UNROLL, body, 0)


def near_kernel(layer, first, place_ref, meta_ref, h_ref, next_ref, w0, w1, w2, w3, *refs):
    if first:
        wmsg_ref, mvec_ref, gather_ref, collect_ref, acc, receive, vectors, window, hidden, normed = refs
    else:
        vectors, wmsg_ref, mvec_ref, gather_ref, collect_ref, acc, receive, window, hidden, normed = refs
    f, half = place_ref[0], place_ref[4]
    shards = (w0, w1, w2, w3)
    edges = gather_ref.shape[1]
    if first:
        end = w0.shape[1] - 3 * VECTOR_ROWS
        for m, w in enumerate(shards):
            rows = w[0, end : end + 3 * VECTOR_ROWS, :].astype(F32)
            vectors[m] = rows[:VECTOR_ROWS] + rows[VECTOR_ROWS : 2 * VECTOR_ROWS] + rows[2 * VECTOR_ROWS :]
    w_src = weight(shards, f, half, 0, True)
    own = wide(h_ref)
    block = own.shape[0]
    window[:block, :] = dot(own, w_src).astype(BF16)
    window[block:, :] = dot(wide(next_ref, FLIPPED), w_src).astype(BF16)
    receive[...] = (dot(own, weight(shards, f, half, 2 * edges, True)) + vector(vectors, layer, 0)).astype(BF16)
    acc[...] = jnp.zeros_like(acc)
    run_edges(0, 0, layer, f, meta_ref, receive, window, gather_ref, collect_ref, wmsg_ref, mvec_ref, hidden, normed, acc)


def far_kernel(layer, place_ref, meta_ref, after_ref, w0, w1, w2, w3, wmsg_ref, mvec_ref, gather_ref, collect_ref, acc_in, receive, out_ref, window, hidden, normed, acc):
    f, half = place_ref[0], place_ref[4]
    edges = gather_ref.shape[1]
    window[...] = dot(wide(after_ref), weight((w0, w1, w2, w3), f, half, 0, True)).astype(BF16)
    acc[...] = acc_in[...]
    run_edges(1, 8, layer, f, meta_ref, receive, window, gather_ref, collect_ref, wmsg_ref, mvec_ref, hidden, normed, acc)
    out_ref[...] = acc[...].astype(BF16)


def node_kernel(layer, final, place_ref, h_ref, part_a, part_b, degree_ref, w0, w1, w2, w3, vectors, mvec_ref, mgain_ref, *outs):
    f, half = place_ref[0], place_ref[4]
    shards = (w0, w1, w2, w3)
    part = h_ref.shape[-1]
    step = 2 * part
    total = part_a[...].astype(F32) + part_b[...].astype(F32)
    agg = total * mgain_ref[layer : layer + 1, :] + degree_ref[:, 0:1] * mvec_ref[layer, 1:2, :]
    pre = dot(wide(h_ref), weight(shards, f, half, 2 * step, True))
    pre = pre + dot(agg.astype(BF16), weight(shards, f, half, 3 * step, False)) + vector(vectors, layer, 1)
    inner = jnp.maximum(pre, 0.0).astype(BF16)
    inner = jnp.concatenate([inner[:, m * part : (m + 1) * part] for m in ORDER], axis=1)
    node = dot(inner, weight(shards, f, half, 4 * step, True)) + vector(vectors, layer, 2)
    centred = node - jnp.mean(node, axis=1, keepdims=True)
    spread = jnp.mean(centred * centred, axis=1, keepdims=True)
    change = centred * lax.rsqrt(spread + EPSILON) * vector(vectors, layer, 4) + vector(vectors, layer, 3)
    for i, m in enumerate(ORDER):
        if final and m not in (0, 2):
            continue
        new = (h_ref[i].astype(F32) + change[:, m * part : (m + 1) * part]).astype(BF16)
        if final:
            outs[m // 2][...] = new
        else:
            outs[0][i] = new


def join_kernel(place_ref, own_ref, other_ref, out_ref):
    rows = own_ref.shape[0]
    side = place_ref[5]
    out_ref[pl.ds(pl.multiple_of(side * rows, rows), rows), :] = own_ref[...]
    out_ref[pl.ds(pl.multiple_of((1 - side) * rows, rows), rows), :] = other_ref[...]


def call(kernel, name, inputs, spaces, outs, out_spaces, scratch=()):
    return pl.pallas_call(
        kernel,
        out_shape=outs,
        in_specs=spaces,
        out_specs=out_spaces,
        scratch_shapes=list(scratch),
        compiler_params=pltpu.CompilerParams(vmem_limit_bytes=32 * 1024 * 1024),
        name=name,
    )(*inputs)


def per_device(
    node_state,
    w_dst,
    w_src,
    w_msg,
    w_node_in,
    w_node_out,
    msg_vectors,
    msg_gain,
    node_vectors,
    node_gain,
    nbr_blocks,
    edge_count,
    edge_src,
    edge_dst,
):
    width = w_msg.shape[1]
    part = width // 4
    block_count, slots = nbr_blocks.shape
    edges = edge_src.shape[2]
    mine = block_count // 2
    rows = mine * edges
    feat = lax.axis_index("feat")
    dom = lax.axis_index("dom")
    side = feat // 2
    half = (dom // 4) % 2
    place = jnp.stack(
        [feat, feat % 2, side * mine, dom * block_count + side * mine, half, side]
    ).astype(jnp.int32)

    vec = jnp.concatenate([node_vectors, node_gain[:, None, :]], axis=1).reshape(LAYERS * 5, part)
    vec = jnp.pad(vec, ((0, VECTOR_ROWS - LAYERS * 5), (0, 0)))
    high = lax.reduce_precision(vec, 8, 7)
    middle = lax.reduce_precision(vec - high, 8, 7)
    low = vec - high - middle
    thirds = jnp.concatenate([high, middle, low], axis=0).astype(BF16)
    packs = []
    for layer in range(LAYERS):
        group = [
            w.reshape(2, width // 2, part)
            for w in (
                w_src[layer], w_dst[layer], w_node_in[layer, :width], w_node_in[layer, width:], w_node_out[layer],
            )
        ]
        if layer == 0:
            group.append(jnp.broadcast_to(thirds[None], (2,) + thirds.shape))
        packs.append(jnp.concatenate(group, axis=1))

    def spread_weights(pack, share):
        beside = exchange(pack, 1)
        across = exchange(share, 2)
        across = jnp.stack([across, exchange(across, 16)])
        return pack, beside, across, exchange(across, 1)

    def share_of(pack):
        return lax.dynamic_index_in_dim(pack, half, 0, keepdims=False)

    halves = node_state.reshape(2, rows, part)
    own = lax.dynamic_index_in_dim(halves, side, 0, keepdims=False)
    other = lax.dynamic_index_in_dim(halves, 1 - side, 0, keepdims=False)
    pair = jnp.stack([own, exchange(other, 2)])
    latent = jnp.concatenate([pair, exchange(pair, 1)], axis=0)
    weights = spread_weights(packs[0], share_of(packs[0]))

    all_slots = mine * slots + 1
    gather, collect, degree, meta = call(
        prepare_kernel,
        "one_hots",
        (place, nbr_blocks, edge_count, jnp.swapaxes(edge_src, 1, 2), jnp.swapaxes(edge_dst, 1, 2), edge_dst),
        [SMEM] * 3 + [VMEM] * 3,
        (
            jax.ShapeDtypeStruct((all_slots, edges, 2 * edges), BF16),
            jax.ShapeDtypeStruct((all_slots, edges, edges), BF16),
            jax.ShapeDtypeStruct((rows, edges), F32),
            jax.ShapeDtypeStruct((4, LIST), jnp.int32),
        ),
        (VMEM, VMEM, VMEM, SMEM),
    )

    vectors = None
    for layer in range(LAYERS):
        final = layer == LAYERS - 1
        after = pass_on(latent)
        beyond = pass_on(after)
        if not final:
            beyond, share = lax.optimization_barrier((beyond, share_of(packs[layer + 1])))
        messages = w_msg[layer].reshape(4, part, width)
        outs = [jax.ShapeDtypeStruct((rows, width), F32), jax.ShapeDtypeStruct((rows, width), BF16)]
        inputs = [place, meta, latent, after, *weights]
        if layer == 0:
            outs.append(jax.ShapeDtypeStruct((4, VECTOR_ROWS, part), F32))
        else:
            inputs.append(vectors)
        inputs += [messages, msg_vectors, gather, collect]
        result = call(
            lambda *refs, layer=layer: near_kernel(layer, layer == 0, *refs),
            f"near{layer}",
            inputs,
            [SMEM, SMEM] + [VMEM] * (len(inputs) - 2),
            outs,
            [VMEM] * len(outs),
            [
                pltpu.VMEM((2 * rows, width), BF16),
                pltpu.VMEM((UNROLL * edges, width), BF16),
                pltpu.VMEM((UNROLL * edges, width), BF16),
            ],
        )
        acc, receive = result[0], result[1]
        if layer == 0:
            vectors = result[2]
        partial = call(
            lambda *refs, layer=layer: far_kernel(layer, *refs),
            f"far{layer}",
            [place, meta, beyond, *weights, messages, msg_vectors, gather, collect, acc, receive],
            [SMEM, SMEM] + [VMEM] * 11,
            jax.ShapeDtypeStruct((rows, width), BF16),
            VMEM,
            [
                pltpu.VMEM((rows, width), BF16),
                pltpu.VMEM((UNROLL * edges, width), BF16),
                pltpu.VMEM((UNROLL * edges, width), BF16),
                pltpu.VMEM((rows, width), F32),
            ],
        )
        theirs = exchange(partial, 1)
        if final:
            outs = [jax.ShapeDtypeStruct((rows, part), BF16)] * 2
        else:
            outs = [jax.ShapeDtypeStruct((4, rows, part), BF16)]
        result = call(
            lambda *refs, layer=layer, final=final: node_kernel(layer, final, *refs),
            f"node{layer}",
            [place, latent, partial, theirs, degree, *weights, vectors, msg_vectors, msg_gain],
            [SMEM] + [VMEM] * 11,
            outs,
            [VMEM] * len(outs),
        )
        if final:
            return call(
                join_kernel,
                "join",
                [place, result[0], exchange(result[1], 2)],
                [SMEM, VMEM, VMEM],
                jax.ShapeDtypeStruct((2 * rows, part), BF16),
                VMEM,
            )
        latent = result[0]
        weights = spread_weights(packs[layer + 1], share)


def solution(mesh):
    placed = (
        P("dom", "feat"),
        P(None, None, "feat"),
        P(None, None, "feat"),
        P(),
        P(None, None, "feat"),
        P(None, None, "feat"),
        P(),
        P(),
        P(None, None, "feat"),
        P(None, "feat"),
        P("dom", None),
        P("dom", None),
        P("dom", None, None),
        P("dom", None, None),
    )
    return jax.shard_map(
        per_device, mesh=mesh, in_specs=placed, out_specs=P("dom", "feat"), check_vma=False
    )
```

```python
import jax
import jax.numpy as jnp
from jax import lax
from jax.experimental import pallas as pl
from jax.experimental.pallas import tpu as pltpu
from jax.sharding import PartitionSpec as P

LAYERS = 2
EPSILON = 1e-05
BOTH = ("dom", "feat")
F32 = jnp.float32
BF16 = jnp.bfloat16
VECTOR_ROWS = 16
ORDER = (0, 2, 1, 3)
FLIPPED = (1, 0, 3, 2)
STRAIGHT = (0, 1, 2, 3)
UNROLL = 4
LIST = 32
VMEM = pl.BlockSpec(memory_space=pltpu.VMEM)
SMEM = pl.BlockSpec(memory_space=pltpu.SMEM)


def dot(a, b):
    return jnp.dot(a, b, preferred_element_type=F32)


def exchange(value, mask):
    total = lax.axis_size(BOTH)
    return lax.ppermute(value, BOTH, [(i, i ^ mask) for i in range(total)])


def pass_on(value):
    total = lax.axis_size(BOTH)
    pairs = [(i, i + (2 if i % 2 == 0 else -2)) for i in range(total)]
    return lax.ppermute(value, BOTH, [(i, t) for i, t in pairs if 0 <= t < total])


def from_other_side(value):
    total = lax.axis_size(BOTH)
    pairs = []
    for i in range(total):
        column, low = divmod(i, 16)
        z, core = divmod(low, 2)
        z = (z + (1 if z % 2 else -1)) % 8
        pairs.append((i, column * 16 + z * 2 + core))
    return lax.ppermute(value, BOTH, pairs)


def prepare_kernel(place_ref, nbr_ref, count_ref, src_ref, dst_ref, gather_ref, collect_ref, degree_ref, meta_ref, turned):
    last, edges, _ = gather_ref.shape
    slots = nbr_ref.shape[1]
    blocks = last // slots
    core, first, base = place_ref[1], place_ref[2], place_ref[3]
    lanes = lax.broadcasted_iota(jnp.int32, (edges, edges), 1)
    rows = lax.broadcasted_iota(jnp.int32, (edges, edges), 0)
    for i in range(LIST):
        meta_ref[0, i] = last - 1
        meta_ref[1, i] = last - 1
        meta_ref[2, i] = 0
    near, far = jnp.int32(0), jnp.int32(0)
    turned[...] = jnp.zeros_like(turned)
    for j in range(blocks):
        turned[0:slots, :] = src_ref[first + j].astype(F32)
        turned[8 : 8 + slots, :] = dst_ref[first + j].astype(F32)
        columns = turned[...].T.astype(jnp.int32)
        to_row = dst_ref[first + j]
        degree = jnp.zeros((edges, edges), F32)
        for k in range(slots):
            s = j * slots + k
            gather_ref[s, :, :edges] = (columns[:, 8 + k : 9 + k] == lanes).astype(F32).astype(BF16)
            gather_ref[s, :, edges:] = (columns[:, k : k + 1] == lanes).astype(F32).astype(BF16)
            live = ((to_row[k : k + 1, :] == rows) & (lanes < count_ref[first + j, k])).astype(F32)
            collect_ref[s] = live.astype(BF16)
            degree = degree + live
            place = nbr_ref[first + j, k] - base
            step = (place + 2 * blocks) // blocks - 2
            hops = jnp.abs(step)
            meta_ref[2, s] = hops * blocks + place - step * blocks
            mine = jnp.where(step == 0, core == j // (blocks // 2), (step > 0) == (core == 1))
            is_far = mine & (hops == 2)
            is_near = mine & (hops < 2)

            @pl.when(is_near)
            def _():
                meta_ref[0, near] = s

            @pl.when(is_far)
            def _():
                meta_ref[1, far] = s

            near = near + is_near.astype(jnp.int32)
            far = far + is_far.astype(jnp.int32)
        degree_ref[j * edges : (j + 1) * edges, :] = jnp.broadcast_to(
            jnp.sum(degree, axis=1, keepdims=True), (edges, edges)
        )
    meta_ref[3, 0] = near
    meta_ref[3, 1] = far
    gather_ref[last - 1] = jnp.zeros(gather_ref.shape[1:], BF16)
    collect_ref[last - 1] = jnp.zeros(collect_ref.shape[1:], BF16)


def first_pack_kernel(src_ref, dst_ref, vec_ref, gain_ref, out_ref):
    width = src_ref.shape[1]
    out_ref[:width, :] = src_ref[0]
    out_ref[width : 2 * width, :] = dst_ref[0]
    rest = jnp.concatenate(
        [part for layer in range(LAYERS) for part in (vec_ref[layer], gain_ref[layer : layer + 1, :])]
        + [jnp.zeros((VECTOR_ROWS - 5 * LAYERS, src_ref.shape[2]), F32)],
        axis=0,
    )
    for i in range(3):
        at = 2 * width + i * VECTOR_ROWS
        piece = rest.astype(BF16)
        out_ref[at : at + VECTOR_ROWS, :] = piece
        rest = rest - piece.astype(F32)


def other_packs_kernel(src_ref, dst_ref, in_ref, out_w_ref, node_ref, next_ref):
    width = src_ref.shape[1]
    node_ref[: 2 * width, :] = in_ref[0]
    node_ref[2 * width :, :] = out_w_ref[0]
    next_ref[:width, :] = src_ref[1]
    next_ref[width : 2 * width, :] = dst_ref[1]
    next_ref[2 * width : 4 * width, :] = in_ref[1]
    next_ref[4 * width :, :] = out_w_ref[1]


def wide(ref, order=STRAIGHT):
    return jnp.concatenate([ref[i] for i in order], axis=1)


def weight(shards, f, base, mixed):
    own, across, beside = shards
    part = own.shape[-1]
    rows = []
    for i in range(4):
        at = pl.ds(pl.multiple_of(base + (f ^ ORDER[i]) * part, part) if mixed else base + i * part, part)
        rows.append(jnp.concatenate([own[at, :], beside[0, at, :], across[at, :], beside[1, at, :]], axis=1))
    return jnp.concatenate(rows, axis=0)


def vector(vectors, layer, i):
    row = layer * 5 + i
    return jnp.concatenate([vectors[m, row : row + 1, :] for m in range(4)], axis=1)


def run_edges(which, shift, layer, f, meta_ref, receive, window, gather_ref, collect_ref, wmsg_ref, mvec_ref, hidden, normed, acc):
    slots = 6
    edges = gather_ref.shape[1]
    w_msg = jnp.concatenate([wmsg_ref[4 * layer + (f ^ m)] for m in range(4)], axis=0)
    bias = mvec_ref[layer, 0:1, :]

    def body(step, carry):
        ids = [meta_ref[which, step * UNROLL + u] for u in range(UNROLL)]
        blocks = [jnp.minimum(s // slots, 3) for s in ids]
        for u, (s, j) in enumerate(zip(ids, blocks)):
            at = meta_ref[2, s] - shift
            if which == 1:
                at = jnp.maximum(at, 0)
            to = receive[pl.ds(pl.multiple_of(j * edges, edges), edges), :]
            frm = window[pl.ds(pl.multiple_of(at * edges, edges), edges), :]
            terms = dot(gather_ref[s], jnp.concatenate([to, frm], axis=0))
            hidden[u * edges : (u + 1) * edges, :] = jnp.maximum(terms, 0.0).astype(BF16)
        for v in range(0, UNROLL, 2):
            rows = slice(v * edges, (v + 2) * edges)
            message = dot(hidden[rows, :], w_msg) + bias
            centred = message - jnp.mean(message, axis=1, keepdims=True)
            spread = jnp.mean(centred * centred, axis=1, keepdims=True)
            normed[rows, :] = (centred * lax.rsqrt(spread + EPSILON)).astype(BF16)
        for u, (s, j) in enumerate(zip(ids, blocks)):
            rows = pl.ds(pl.multiple_of(j * edges, edges), edges)
            acc[rows, :] = acc[rows, :] + dot(collect_ref[s], normed[u * edges : (u + 1) * edges, :])
        return carry

    lax.fori_loop(0, (meta_ref[3, which] + UNROLL - 1) // UNROLL, body, 0)


def near_kernel(layer, first, place_ref, meta_ref, h_ref, next_ref, w_own, w_across, w_beside, *refs):
    if first:
        wmsg_ref, mvec_ref, gather_ref, collect_ref, acc, receive, vectors, window, hidden, normed = refs
    else:
        vectors, wmsg_ref, mvec_ref, gather_ref, collect_ref, acc, receive, window, hidden, normed = refs
    f = place_ref[0]
    shards = (w_own, w_across, w_beside)
    if first:
        end = w_own.shape[0] - 3 * VECTOR_ROWS
        for m, w in enumerate((w_own, w_beside.at[0], w_across, w_beside.at[1])):
            rows = w[end : end + 3 * VECTOR_ROWS, :].astype(F32)
            vectors[m] = rows[:VECTOR_ROWS] + rows[VECTOR_ROWS : 2 * VECTOR_ROWS] + rows[2 * VECTOR_ROWS :]
    w_src = weight(shards, f, 0, True)
    own = wide(h_ref)
    block, width = own.shape
    window[:block, :] = dot(own, w_src).astype(BF16)
    window[block:, :] = dot(wide(next_ref, FLIPPED), w_src).astype(BF16)
    receive[...] = (dot(own, weight(shards, f, width, True)) + vector(vectors, layer, 0)).astype(BF16)
    acc[...] = jnp.zeros_like(acc)
    run_edges(0, 0, layer, f, meta_ref, receive, window, gather_ref, collect_ref, wmsg_ref, mvec_ref, hidden, normed, acc)


def far_kernel(layer, place_ref, meta_ref, after_ref, w_own, w_across, w_beside, wmsg_ref, mvec_ref, gather_ref, collect_ref, acc_in, receive, out_ref, window, hidden, normed, acc):
    f = place_ref[0]
    window[...] = dot(wide(after_ref), weight((w_own, w_across, w_beside), f, 0, True)).astype(BF16)
    acc[...] = acc_in[...]
    run_edges(1, 8, layer, f, meta_ref, receive, window, gather_ref, collect_ref, wmsg_ref, mvec_ref, hidden, normed, acc)
    out_ref[...] = acc[...].astype(BF16)


def node_kernel(layer, final, place_ref, h_ref, part_a, part_b, degree_ref, w_own, w_across, w_beside, vectors, mvec_ref, mgain_ref, *outs):
    f = place_ref[0]
    shards = (w_own, w_across, w_beside)
    part = h_ref.shape[-1]
    width = 4 * part
    base = w_own.shape[0] - 3 * width
    total = part_a[...].astype(F32) + part_b[...].astype(F32)
    agg = total * mgain_ref[layer : layer + 1, :] + degree_ref[:, 0:1] * mvec_ref[layer, 1:2, :]
    pre = dot(wide(h_ref), weight(shards, f, base, True))
    pre = pre + dot(agg.astype(BF16), weight(shards, f, base + width, False)) + vector(vectors, layer, 1)
    inner = jnp.maximum(pre, 0.0).astype(BF16)
    inner = jnp.concatenate([inner[:, m * part : (m + 1) * part] for m in ORDER], axis=1)
    node = dot(inner, weight(shards, f, base + 2 * width, True)) + vector(vectors, layer, 2)
    centred = node - jnp.mean(node, axis=1, keepdims=True)
    spread = jnp.mean(centred * centred, axis=1, keepdims=True)
    change = centred * lax.rsqrt(spread + EPSILON) * vector(vectors, layer, 4) + vector(vectors, layer, 3)
    for i, m in enumerate(ORDER):
        if final and m not in (0, 2):
            continue
        new = (h_ref[i].astype(F32) + change[:, m * part : (m + 1) * part]).astype(BF16)
        if final:
            outs[m // 2][...] = new
        else:
            outs[0][i] = new


def join_kernel(place_ref, own_ref, other_ref, out_ref):
    rows = own_ref.shape[0]
    side = place_ref[4]
    out_ref[pl.ds(pl.multiple_of(side * rows, rows), rows), :] = own_ref[...]
    out_ref[pl.ds(pl.multiple_of((1 - side) * rows, rows), rows), :] = other_ref[...]


def call(kernel, name, inputs, spaces, outs, out_spaces, scratch=(), us=2):
    return pl.pallas_call(
        kernel,
        out_shape=outs,
        in_specs=spaces,
        out_specs=out_spaces,
        scratch_shapes=list(scratch),
        compiler_params=pltpu.CompilerParams(vmem_limit_bytes=32 * 1024 * 1024),
        cost_estimate=pl.CostEstimate(flops=int(us * 1e9), bytes_accessed=1 << 20, transcendentals=0),
        name=name,
    )(*inputs)


def per_device(
    node_state,
    w_dst,
    w_src,
    w_msg,
    w_node_in,
    w_node_out,
    msg_vectors,
    msg_gain,
    node_vectors,
    node_gain,
    nbr_blocks,
    edge_count,
    edge_src,
    edge_dst,
):
    width = w_msg.shape[1]
    part = width // 4
    block_count, slots = nbr_blocks.shape
    edges = edge_src.shape[2]
    mine = block_count // 2
    rows = mine * edges
    feat = lax.axis_index("feat")
    dom = lax.axis_index("dom")
    side = feat // 2
    place = jnp.stack([feat, feat % 2, side * mine, dom * block_count + side * mine, side]).astype(jnp.int32)
    barrier = lax.optimization_barrier

    halves = node_state.reshape(2, rows, part)
    own = lax.dynamic_index_in_dim(halves, side, 0, keepdims=False)
    other = lax.dynamic_index_in_dim(halves, 1 - side, 0, keepdims=False)
    across = exchange(other, 2)
    first = call(
        first_pack_kernel,
        "first_pack",
        (w_src, w_dst, node_vectors, node_gain),
        [VMEM] * 4,
        jax.ShapeDtypeStruct((2 * width + 3 * VECTOR_ROWS, part), BF16),
        VMEM,
        us=1,
    )
    first_across = exchange(first, 2)
    node_pack, next_pack = call(
        other_packs_kernel,
        "other_packs",
        (w_src, w_dst, w_node_in, w_node_out),
        [VMEM] * 4,
        (jax.ShapeDtypeStruct((3 * width, part), BF16), jax.ShapeDtypeStruct((5 * width, part), BF16)),
        (VMEM, VMEM),
        us=2,
    )
    pair = jnp.stack([own, across])
    latent = jnp.concatenate([pair, exchange(pair, 1)], axis=0)
    node_share, nbr_blocks = barrier((node_pack, nbr_blocks, latent))[:2]
    node_across = exchange(node_share, 2)

    all_slots = mine * slots + 1
    gather, collect, degree, meta = call(
        prepare_kernel,
        "one_hots",
        (place, nbr_blocks, edge_count, edge_src, edge_dst),
        [SMEM] * 3 + [VMEM] * 2,
        (
            jax.ShapeDtypeStruct((all_slots, edges, 2 * edges), BF16),
            jax.ShapeDtypeStruct((all_slots, edges, edges), BF16),
            jax.ShapeDtypeStruct((rows, edges), F32),
            jax.ShapeDtypeStruct((4, LIST), jnp.int32),
        ),
        (VMEM, VMEM, VMEM, SMEM),
        [pltpu.VMEM((edges, edges), F32)],
        us=3,
    )
    edge_weights = (first, first_across, exchange(jnp.stack([first, first_across]), 1))

    vectors = None
    messages = w_msg.reshape(LAYERS * 4, part, width)
    for layer in range(LAYERS):
        final = layer == LAYERS - 1
        after = pass_on(latent)
        beyond = pass_on(after)
        if layer == 0:
            next_share = barrier((next_pack, after))[0]
            next_across = from_other_side(next_share)
        outs = [jax.ShapeDtypeStruct((rows, width), F32), jax.ShapeDtypeStruct((rows, width), BF16)]
        inputs = [place, meta, latent, after, *edge_weights]
        if layer == 0:
            outs.append(jax.ShapeDtypeStruct((4, VECTOR_ROWS, part), F32))
        else:
            inputs.append(vectors)
        inputs += [messages, msg_vectors, gather, collect]
        result = call(
            lambda *refs, layer=layer: near_kernel(layer, layer == 0, *refs),
            f"near{layer}",
            inputs,
            [SMEM, SMEM] + [VMEM] * (len(inputs) - 2),
            outs,
            [VMEM] * len(outs),
            [
                pltpu.VMEM((2 * rows, width), BF16),
                pltpu.VMEM((UNROLL * edges, width), BF16),
                pltpu.VMEM((UNROLL * edges, width), BF16),
            ],
            us=5,
        )
        acc, receive = result[0], result[1]
        if layer == 0:
            vectors = result[2]
        partial = call(
            lambda *refs, layer=layer: far_kernel(layer, *refs),
            f"far{layer}",
            [place, meta, beyond, *edge_weights, messages, msg_vectors, gather, collect, acc, receive],
            [SMEM, SMEM] + [VMEM] * 10,
            jax.ShapeDtypeStruct((rows, width), BF16),
            VMEM,
            [
                pltpu.VMEM((rows, width), BF16),
                pltpu.VMEM((UNROLL * edges, width), BF16),
                pltpu.VMEM((UNROLL * edges, width), BF16),
                pltpu.VMEM((rows, width), F32),
            ],
            us=3,
        )
        theirs = exchange(partial, 1)
        if layer == 0:
            node_weights = (node_pack, node_across, exchange(jnp.stack([node_pack, node_across]), 1))
        if final:
            outs = [jax.ShapeDtypeStruct((rows, part), BF16)] * 2
        else:
            outs = [jax.ShapeDtypeStruct((4, rows, part), BF16)]
        result = call(
            lambda *refs, layer=layer, final=final: node_kernel(layer, final, *refs),
            f"node{layer}",
            [place, latent, partial, theirs, degree, *node_weights, vectors, msg_vectors, msg_gain],
            [SMEM] + [VMEM] * 10,
            outs,
            [VMEM] * len(outs),
        )
        if final:
            return call(
                join_kernel,
                "join",
                [place, result[0], exchange(result[1], 2)],
                [SMEM, VMEM, VMEM],
                jax.ShapeDtypeStruct((2 * rows, part), BF16),
                VMEM,
            )
        latent = result[0]
        next_across = barrier((next_across, latent))[0]
        edge_weights = (next_pack, next_across, exchange(jnp.stack([next_pack, next_across]), 1))
        node_weights = edge_weights


def solution(mesh):
    placed = (
        P("dom", "feat"),
        P(None, None, "feat"),
        P(None, None, "feat"),
        P(),
        P(None, None, "feat"),
        P(None, None, "feat"),
        P(),
        P(),
        P(None, None, "feat"),
        P(None, "feat"),
        P("dom", None),
        P("dom", None),
        P("dom", None, None),
        P("dom", None, None),
    )
    return jax.shard_map(
        per_device, mesh=mesh, in_specs=placed, out_specs=P("dom", "feat"), check_vma=False
    )
```

```python
import jax
import jax.numpy as jnp
from jax import lax
from jax.experimental import pallas as pl
from jax.experimental.pallas import tpu as pltpu
from jax.sharding import PartitionSpec as P

LAYERS = 2
EPSILON = 1e-05
BOTH = ("dom", "feat")
F32 = jnp.float32
BF16 = jnp.bfloat16
VECTOR_ROWS = 16
ORDER = (0, 2, 1, 3)
STRAIGHT = (0, 1, 2, 3)
FROM_NEXT = (3, 2, 1, 0)
FROM_BEYOND = (2, 3, 0, 1)
UNROLL = 4
LIST = 32
VMEM = pl.BlockSpec(memory_space=pltpu.VMEM)
SMEM = pl.BlockSpec(memory_space=pltpu.SMEM)


def dot(a, b):
    return jnp.dot(a, b, preferred_element_type=F32)


def exchange(value, mask):
    total = lax.axis_size(BOTH)
    return lax.ppermute(value, BOTH, [(i, i ^ mask) for i in range(total)])


def swap_with(value, chips):
    total = lax.axis_size(BOTH)
    step = 2 * chips + 1
    pairs = [(i, i + (step if i % 2 == 0 else -step)) for i in range(total)]
    return lax.ppermute(value, BOTH, [(i, t) for i, t in pairs if 0 <= t < total])


def from_other_side(value):
    total = lax.axis_size(BOTH)
    pairs = []
    for i in range(total):
        column, low = divmod(i, 16)
        z, core = divmod(low, 2)
        z = (z + (1 if z % 2 else -1)) % 8
        pairs.append((i, column * 16 + z * 2 + core))
    return lax.ppermute(value, BOTH, pairs)


def prepare_kernel(place_ref, nbr_ref, count_ref, src_ref, dst_ref, gather_ref, collect_ref, degree_ref, meta_ref, turned):
    last, edges, _ = gather_ref.shape
    slots = nbr_ref.shape[1]
    blocks = last // slots
    core, first, base = place_ref[1], place_ref[2], place_ref[3]
    lanes = lax.broadcasted_iota(jnp.int32, (edges, edges), 1)
    rows = lax.broadcasted_iota(jnp.int32, (edges, edges), 0)
    for i in range(LIST):
        meta_ref[0, i] = last - 1
        meta_ref[1, i] = last - 1
        meta_ref[2, i] = 0
    near, far = jnp.int32(0), jnp.int32(0)
    turned[...] = jnp.zeros_like(turned)
    for j in range(blocks):
        turned[0:slots, :] = src_ref[first + j].astype(F32)
        turned[8 : 8 + slots, :] = dst_ref[first + j].astype(F32)
        columns = turned[...].T.astype(jnp.int32)
        to_row = dst_ref[first + j]
        degree = jnp.zeros((edges, edges), F32)
        for k in range(slots):
            s = j * slots + k
            gather_ref[s, :, :edges] = (columns[:, 8 + k : 9 + k] == lanes).astype(F32).astype(BF16)
            gather_ref[s, :, edges:] = (columns[:, k : k + 1] == lanes).astype(F32).astype(BF16)
            live = ((to_row[k : k + 1, :] == rows) & (lanes < count_ref[first + j, k])).astype(F32)
            collect_ref[s] = live.astype(BF16)
            degree = degree + live
            place = nbr_ref[first + j, k] - base
            step = (place + 2 * blocks) // blocks - 2
            hops = jnp.abs(step)
            meta_ref[2, s] = hops * blocks + place - step * blocks
            mine = jnp.where(step == 0, core == j // (blocks // 2), (step > 0) == (core == 0))
            is_far = mine & (hops == 2)
            is_near = mine & (hops < 2)

            @pl.when(is_near)
            def _():
                meta_ref[0, near] = s

            @pl.when(is_far)
            def _():
                meta_ref[1, far] = s

            near = near + is_near.astype(jnp.int32)
            far = far + is_far.astype(jnp.int32)
        degree_ref[j * edges : (j + 1) * edges, :] = jnp.broadcast_to(
            jnp.sum(degree, axis=1, keepdims=True), (edges, edges)
        )
    meta_ref[3, 0] = near
    meta_ref[3, 1] = far
    gather_ref[last - 1] = jnp.zeros(gather_ref.shape[1:], BF16)
    collect_ref[last - 1] = jnp.zeros(collect_ref.shape[1:], BF16)


def pack_kernel(src_ref, dst_ref, in_ref, out_w_ref, vec_ref, gain_ref, first_ref, next_ref):
    width = src_ref.shape[1]
    for layer, ref in enumerate((first_ref, next_ref)):
        ref[: 2 * width, :] = in_ref[layer]
        ref[2 * width : 3 * width, :] = out_w_ref[layer]
        ref[3 * width : 4 * width, :] = src_ref[layer]
        ref[4 * width : 5 * width, :] = dst_ref[layer]
    rest = jnp.concatenate(
        [part for layer in range(LAYERS) for part in (vec_ref[layer], gain_ref[layer : layer + 1, :])]
        + [jnp.zeros((VECTOR_ROWS - 5 * LAYERS, src_ref.shape[2]), F32)],
        axis=0,
    )
    for i in range(3):
        at = 5 * width + i * VECTOR_ROWS
        piece = rest.astype(BF16)
        first_ref[at : at + VECTOR_ROWS, :] = piece
        rest = rest - piece.astype(F32)
    first_ref[5 * width + 3 * VECTOR_ROWS :, :] = jnp.zeros((VECTOR_ROWS, src_ref.shape[2]), BF16)


def wide(ref, order=STRAIGHT):
    return jnp.concatenate([ref[i] for i in order], axis=1)


def weight(shards, f, mixed):
    own, across, beside = shards
    part = own.shape[-1]
    rows = []
    for i in range(4):
        at = pl.ds(pl.multiple_of((f ^ ORDER[i]) * part, part) if mixed else i * part, part)
        rows.append(jnp.concatenate([own[at, :], beside[0, at, :], across[at, :], beside[1, at, :]], axis=1))
    return jnp.concatenate(rows, axis=0)


def vector(vectors, layer, i):
    row = layer * 5 + i
    return jnp.concatenate([vectors[m, row : row + 1, :] for m in range(4)], axis=1)


def run_edges(which, shift, layer, f, meta_ref, receive, window, gather_ref, collect_ref, wmsg_ref, mvec_ref, hidden, normed, acc):
    slots = 6
    edges = gather_ref.shape[1]
    w_msg = jnp.concatenate([wmsg_ref[f ^ m] for m in range(4)], axis=0)
    bias = mvec_ref[layer, 0:1, :]

    def body(step, carry):
        ids = [meta_ref[which, step * UNROLL + u] for u in range(UNROLL)]
        blocks = [jnp.minimum(s // slots, 3) for s in ids]
        for u, (s, j) in enumerate(zip(ids, blocks)):
            at = meta_ref[2, s] - shift
            if which == 1:
                at = jnp.maximum(at, 0)
            to = receive[pl.ds(pl.multiple_of(j * edges, edges), edges), :]
            frm = window[pl.ds(pl.multiple_of(at * edges, edges), edges), :]
            terms = dot(gather_ref[s], jnp.concatenate([to, frm], axis=0))
            hidden[u * edges : (u + 1) * edges, :] = jnp.maximum(terms, 0.0).astype(BF16)
        for v in range(0, UNROLL, 2):
            rows = slice(v * edges, (v + 2) * edges)
            message = dot(hidden[rows, :], w_msg) + bias
            centred = message - jnp.mean(message, axis=1, keepdims=True)
            spread = jnp.mean(centred * centred, axis=1, keepdims=True)
            normed[rows, :] = (centred * lax.rsqrt(spread + EPSILON)).astype(BF16)
        for u, (s, j) in enumerate(zip(ids, blocks)):
            rows = pl.ds(pl.multiple_of(j * edges, edges), edges)
            acc[rows, :] = acc[rows, :] + dot(collect_ref[s], normed[u * edges : (u + 1) * edges, :])
        return carry

    lax.fori_loop(0, (meta_ref[3, which] + UNROLL - 1) // UNROLL, body, 0)


def near_kernel(layer, first, place_ref, meta_ref, h_ref, next_ref, wmsg_ref, mvec_ref, gather_ref, collect_ref, *refs):
    source, target, refs = refs[:3], refs[3:6], refs[6:]
    if first:
        own_rows, across_rows, beside_rows, acc, receive, vectors, window, hidden, normed = refs
        for m, w in enumerate((own_rows, beside_rows.at[0], across_rows, beside_rows.at[1])):
            rows = w[...].astype(F32)
            vectors[m] = rows[:VECTOR_ROWS] + rows[VECTOR_ROWS : 2 * VECTOR_ROWS] + rows[2 * VECTOR_ROWS : 3 * VECTOR_ROWS]
    else:
        vectors, acc, receive, window, hidden, normed = refs
    f = place_ref[0]
    w_src = weight(source, f, True)
    own = wide(h_ref)
    block = own.shape[0]
    window[:block, :] = dot(own, w_src).astype(BF16)
    window[block:, :] = dot(wide(next_ref, FROM_NEXT), w_src).astype(BF16)
    receive[...] = (dot(own, weight(target, f, True)) + vector(vectors, layer, 0)).astype(BF16)
    acc[...] = jnp.zeros_like(acc)
    run_edges(0, 0, layer, f, meta_ref, receive, window, gather_ref, collect_ref, wmsg_ref, mvec_ref, hidden, normed, acc)


def far_kernel(layer, place_ref, meta_ref, after_ref, wmsg_ref, mvec_ref, gather_ref, collect_ref, acc_in, receive, w_own, w_across, w_beside, out_ref, window, hidden, normed, acc):
    f = place_ref[0]
    window[...] = dot(wide(after_ref, FROM_BEYOND), weight((w_own, w_across, w_beside), f, True)).astype(BF16)
    acc[...] = acc_in[...]
    run_edges(1, 8, layer, f, meta_ref, receive, window, gather_ref, collect_ref, wmsg_ref, mvec_ref, hidden, normed, acc)
    out_ref[...] = acc[...].astype(BF16)


def node_kernel(layer, final, place_ref, h_ref, part_a, part_b, degree_ref, vectors, mvec_ref, mgain_ref, *refs):
    f = place_ref[0]
    w_latent, w_sum, w_out, outs = refs[:3], refs[3:6], refs[6:9], refs[9:]
    part = h_ref.shape[-1]
    total = part_a[...].astype(F32) + part_b[...].astype(F32)
    agg = total * mgain_ref[layer : layer + 1, :] + degree_ref[:, 0:1] * mvec_ref[layer, 1:2, :]
    pre = dot(wide(h_ref), weight(w_latent, f, True))
    pre = pre + dot(agg.astype(BF16), weight(w_sum, f, False)) + vector(vectors, layer, 1)
    inner = jnp.maximum(pre, 0.0).astype(BF16)
    inner = jnp.concatenate([inner[:, m * part : (m + 1) * part] for m in ORDER], axis=1)
    node = dot(inner, weight(w_out, f, True)) + vector(vectors, layer, 2)
    centred = node - jnp.mean(node, axis=1, keepdims=True)
    spread = jnp.mean(centred * centred, axis=1, keepdims=True)
    change = centred * lax.rsqrt(spread + EPSILON) * vector(vectors, layer, 4) + vector(vectors, layer, 3)
    for i, m in enumerate(ORDER):
        if final and m not in (0, 2):
            continue
        new = (h_ref[i].astype(F32) + change[:, m * part : (m + 1) * part]).astype(BF16)
        if final:
            outs[m // 2][...] = new
        else:
            outs[0][i] = new


def join_kernel(place_ref, own_ref, other_ref, out_ref):
    rows = own_ref.shape[0]
    side = place_ref[4]
    out_ref[pl.ds(pl.multiple_of(side * rows, rows), rows), :] = own_ref[...]
    out_ref[pl.ds(pl.multiple_of((1 - side) * rows, rows), rows), :] = other_ref[...]


def rows_of(weights, at, count):
    specs = [pl.BlockSpec((count, w.shape[-1]), lambda i: (at, 0)) for w in weights[:2]]
    return weights, specs + [pl.BlockSpec((2, count, weights[2].shape[-1]), lambda i: (0, at, 0))]


def call(kernel, name, inputs, spaces, outs, out_spaces, scratch=(), us=2):
    return pl.pallas_call(
        kernel,
        out_shape=outs,
        grid=(1,),
        in_specs=spaces,
        out_specs=out_spaces,
        scratch_shapes=list(scratch),
        compiler_params=pltpu.CompilerParams(vmem_limit_bytes=32 * 1024 * 1024),
        cost_estimate=pl.CostEstimate(flops=int(us * 1e9), bytes_accessed=1 << 20, transcendentals=0),
        name=name,
    )(*inputs)


def per_device(
    node_state,
    w_dst,
    w_src,
    w_msg,
    w_node_in,
    w_node_out,
    msg_vectors,
    msg_gain,
    node_vectors,
    node_gain,
    nbr_blocks,
    edge_count,
    edge_src,
    edge_dst,
):
    width = w_msg.shape[1]
    part = width // 4
    block_count, slots = nbr_blocks.shape
    edges = edge_src.shape[2]
    mine = block_count // 2
    rows = mine * edges
    feat = lax.axis_index("feat")
    dom = lax.axis_index("dom")
    side = feat // 2
    place = jnp.stack([feat, feat % 2, side * mine, dom * block_count + side * mine, side]).astype(jnp.int32)
    barrier = lax.optimization_barrier

    halves = node_state.reshape(2, rows, part)
    own = lax.dynamic_index_in_dim(halves, side, 0, keepdims=False)
    other = lax.dynamic_index_in_dim(halves, 1 - side, 0, keepdims=False)
    across = exchange(other, 2)
    pack, next_pack = call(
        pack_kernel,
        "packs",
        (w_src, w_dst, w_node_in, w_node_out, node_vectors, node_gain),
        [VMEM] * 6,
        (
            jax.ShapeDtypeStruct((5 * width + 4 * VECTOR_ROWS, part), BF16),
            jax.ShapeDtypeStruct((5 * width, part), BF16),
        ),
        (VMEM, VMEM),
    )
    pack_across = exchange(pack, 2)
    next_across = from_other_side(next_pack)
    pair = jnp.stack([own, across])
    latent = jnp.concatenate([pair, exchange(pair, 1)], axis=0)

    all_slots = mine * slots + 1
    nbr_blocks = barrier((nbr_blocks, latent))[0]
    gather, collect, degree, meta = call(
        prepare_kernel,
        "one_hots",
        (place, nbr_blocks, edge_count, edge_src, edge_dst),
        [SMEM] * 3 + [VMEM] * 2,
        (
            jax.ShapeDtypeStruct((all_slots, edges, 2 * edges), BF16),
            jax.ShapeDtypeStruct((all_slots, edges, edges), BF16),
            jax.ShapeDtypeStruct((rows, edges), F32),
            jax.ShapeDtypeStruct((4, LIST), jnp.int32),
        ),
        (VMEM, VMEM, VMEM, SMEM),
        [pltpu.VMEM((edges, edges), F32)],
        us=3,
    )
    vectors = None
    messages = w_msg.reshape(LAYERS * 4, part, width)
    for layer in range(LAYERS):
        final = layer == LAYERS - 1
        after = swap_with(latent, 1)
        beyond = swap_with(latent, 2)
        if layer == 0:
            pack_across, next_across, after, meta = barrier((pack_across, next_across, after, meta))
            weights = (pack, pack_across, exchange(jnp.stack([pack, pack_across]), 1))
        message_spec = pl.BlockSpec((4, part, width), lambda i, layer=layer: (layer, 0, 0))
        edge_inputs = [messages, msg_vectors, gather, collect]
        edge_specs = [message_spec, VMEM, VMEM, VMEM]
        source, source_specs = rows_of(weights, 3, width)
        target, target_specs = rows_of(weights, 4, width)
        outs = [jax.ShapeDtypeStruct((rows, width), F32), jax.ShapeDtypeStruct((rows, width), BF16)]
        if layer == 0:
            outs.append(jax.ShapeDtypeStruct((4, VECTOR_ROWS, part), F32))
            extra, extra_specs = rows_of(weights, 5 * width // (4 * VECTOR_ROWS), 4 * VECTOR_ROWS)
        else:
            extra, extra_specs = (vectors,), [VMEM]
        result = call(
            lambda *refs, layer=layer: near_kernel(layer, layer == 0, *refs),
            f"near{layer}",
            [place, meta, latent, after, *edge_inputs, *source, *target, *extra],
            [SMEM, SMEM, VMEM, VMEM, *edge_specs, *source_specs, *target_specs, *extra_specs],
            outs,
            [VMEM] * len(outs),
            [
                pltpu.VMEM((2 * rows, width), BF16),
                pltpu.VMEM((UNROLL * edges, width), BF16),
                pltpu.VMEM((UNROLL * edges, width), BF16),
            ],
            us=5,
        )
        acc, receive = result[0], result[1]
        if layer == 0:
            vectors = result[2]
            acc, next_across = barrier((acc, next_across))
            beside = exchange(jnp.stack([next_pack, next_across]), 1)
            beyond, beside, acc = barrier((beyond, beside, acc))
            next_weights = (next_pack, next_across, beside)
        else:
            beyond, acc = barrier((beyond, acc))
        partial = call(
            lambda *refs, layer=layer: far_kernel(layer, *refs),
            f"far{layer}",
            [place, meta, beyond, *edge_inputs, acc, receive, *source],
            [SMEM, SMEM, VMEM, *edge_specs, VMEM, VMEM, *source_specs],
            jax.ShapeDtypeStruct((rows, width), BF16),
            VMEM,
            [
                pltpu.VMEM((rows, width), BF16),
                pltpu.VMEM((UNROLL * edges, width), BF16),
                pltpu.VMEM((UNROLL * edges, width), BF16),
                pltpu.VMEM((rows, width), F32),
            ],
            us=3,
        )
        theirs = exchange(partial, 1)
        if final:
            outs = [jax.ShapeDtypeStruct((rows, part), BF16)] * 2
        else:
            outs = [jax.ShapeDtypeStruct((4, rows, part), BF16)]
        matrices = [rows_of(weights, i, width) for i in range(3)]
        result = call(
            lambda *refs, layer=layer, final=final: node_kernel(layer, final, *refs),
            f"node{layer}",
            [place, latent, partial, theirs, degree, vectors, msg_vectors, msg_gain] + [w for group, _ in matrices for w in group],
            [SMEM] + [VMEM] * 7 + [spec for _, specs in matrices for spec in specs],
            outs,
            [VMEM] * len(outs),
        )
        if final:
            return call(
                join_kernel,
                "join",
                [place, result[0], exchange(result[1], 2)],
                [SMEM, VMEM, VMEM],
                jax.ShapeDtypeStruct((2 * rows, part), BF16),
                VMEM,
            )
        latent = result[0]
        weights = next_weights


def solution(mesh):
    placed = (
        P("dom", "feat"),
        P(None, None, "feat"),
        P(None, None, "feat"),
        P(),
        P(None, None, "feat"),
        P(None, None, "feat"),
        P(),
        P(),
        P(None, None, "feat"),
        P(None, "feat"),
        P("dom", None),
        P("dom", None),
        P("dom", None, None),
        P("dom", None, None),
    )
    return jax.shard_map(
        per_device, mesh=mesh, in_specs=placed, out_specs=P("dom", "feat"), check_vma=False
    )
```

```python
import jax
import jax.numpy as jnp
from jax import lax
from jax.experimental import pallas as pl
from jax.experimental.pallas import tpu as pltpu
from jax.sharding import PartitionSpec as P

LAYERS = 2
EPSILON = 1e-05
BOTH = ("dom", "feat")
F32 = jnp.float32
BF16 = jnp.bfloat16
VECTOR_ROWS = 16
ORDER = (0, 2, 1, 3)
STRAIGHT = (0, 1, 2, 3)
FROM_NEXT = (3, 2, 1, 0)
FROM_BEYOND = (2, 3, 0, 1)
UNROLL = 4
LIST = 32
VMEM = pl.BlockSpec(memory_space=pltpu.VMEM)
SMEM = pl.BlockSpec(memory_space=pltpu.SMEM)
ANY = pl.BlockSpec(memory_space=pl.ANY)


def dot(a, b):
    return jnp.dot(a, b, preferred_element_type=F32)


def exchange(value, mask):
    total = lax.axis_size(BOTH)
    return lax.ppermute(value, BOTH, [(i, i ^ mask) for i in range(total)])


def swap_with(value, chips):
    total = lax.axis_size(BOTH)
    step = 2 * chips + 1
    pairs = [(i, i + (step if i % 2 == 0 else -step)) for i in range(total)]
    return lax.ppermute(value, BOTH, [(i, t) for i, t in pairs if 0 <= t < total])


def from_other_side(value):
    total = lax.axis_size(BOTH)
    pairs = []
    for i in range(total):
        column, low = divmod(i, 16)
        z, core = divmod(low, 2)
        z = (z + (1 if z % 2 else -1)) % 8
        pairs.append((i, column * 16 + z * 2 + core))
    return lax.ppermute(value, BOTH, pairs)


def prepare_kernel(place_ref, nbr_ref, count_ref, src_ref, dst_ref, gather_ref, collect_ref, degree_ref, meta_ref, turned):
    last, edges, _ = gather_ref.shape
    slots = nbr_ref.shape[1]
    blocks = last // slots
    core, first, base = place_ref[1], place_ref[2], place_ref[3]
    lanes = lax.broadcasted_iota(jnp.int32, (edges, edges), 1)
    rows = lax.broadcasted_iota(jnp.int32, (edges, edges), 0)
    for i in range(LIST):
        meta_ref[0, i] = last - 1
        meta_ref[1, i] = last - 1
        meta_ref[2, i] = 0
    near, far = jnp.int32(0), jnp.int32(0)
    turned[...] = jnp.zeros_like(turned)
    for j in range(blocks):
        turned[0:slots, :] = src_ref[first + j].astype(F32)
        turned[8 : 8 + slots, :] = dst_ref[first + j].astype(F32)
        columns = turned[...].T.astype(jnp.int32)
        to_row = dst_ref[first + j]
        degree = jnp.zeros((edges, edges), F32)
        for k in range(slots):
            s = j * slots + k
            gather_ref[s, :, :edges] = (columns[:, 8 + k : 9 + k] == lanes).astype(F32).astype(BF16)
            gather_ref[s, :, edges:] = (columns[:, k : k + 1] == lanes).astype(F32).astype(BF16)
            live = ((to_row[k : k + 1, :] == rows) & (lanes < count_ref[first + j, k])).astype(F32)
            collect_ref[s] = live.astype(BF16)
            degree = degree + live
            place = nbr_ref[first + j, k] - base
            step = (place + 2 * blocks) // blocks - 2
            hops = jnp.abs(step)
            meta_ref[2, s] = hops * blocks + place - step * blocks
            mine = jnp.where(step == 0, core == j // (blocks // 2), (step > 0) == (core == 0))
            is_far = mine & (hops == 2)
            is_near = mine & (hops < 2)

            @pl.when(is_near)
            def _():
                meta_ref[0, near] = s

            @pl.when(is_far)
            def _():
                meta_ref[1, far] = s

            near = near + is_near.astype(jnp.int32)
            far = far + is_far.astype(jnp.int32)
        degree_ref[j * edges : (j + 1) * edges, :] = jnp.broadcast_to(
            jnp.sum(degree, axis=1, keepdims=True), (edges, edges)
        )
    meta_ref[3, 0] = near
    meta_ref[3, 1] = far
    gather_ref[last - 1] = jnp.zeros(gather_ref.shape[1:], BF16)
    collect_ref[last - 1] = jnp.zeros(collect_ref.shape[1:], BF16)


def pack_kernel(src_ref, dst_ref, in_ref, out_w_ref, vec_ref, gain_ref, first_ref, next_ref, rows, sems):
    width = src_ref.shape[1]
    copies = []
    for layer, ref in enumerate((first_ref, next_ref)):
        for source, at in ((in_ref, 0), (out_w_ref, 2), (src_ref, 3), (dst_ref, 4)):
            count = source.shape[1]
            copies.append(
                pltpu.make_async_copy(
                    source.at[layer], ref.at[pl.ds(at * width, count), :], sems.at[len(copies)]
                )
            )
    for copy in copies:
        copy.start()
    rest = jnp.concatenate(
        [part for layer in range(LAYERS) for part in (vec_ref[layer], gain_ref[layer : layer + 1, :])]
        + [jnp.zeros((VECTOR_ROWS - 5 * LAYERS, src_ref.shape[2]), F32)],
        axis=0,
    )
    for i in range(3):
        piece = rest.astype(BF16)
        rows[i * VECTOR_ROWS : (i + 1) * VECTOR_ROWS, :] = piece
        rest = rest - piece.astype(F32)
    rows[3 * VECTOR_ROWS :, :] = jnp.zeros((VECTOR_ROWS, src_ref.shape[2]), BF16)
    last = pltpu.make_async_copy(
        rows, first_ref.at[pl.ds(5 * width, 4 * VECTOR_ROWS), :], sems.at[len(copies)]
    )
    last.start()
    for copy in copies:
        copy.wait()
    last.wait()


def wide(ref, order=STRAIGHT):
    return jnp.concatenate([ref[i] for i in order], axis=1)


def weight(shards, f, mixed):
    part = shards[0].shape[-1]
    rows = []
    for i in range(4):
        at = pl.ds(pl.multiple_of((f ^ ORDER[i]) * part, part) if mixed else i * part, part)
        rows.append(jnp.concatenate([w[at, :] for w in shards], axis=1))
    return jnp.concatenate(rows, axis=0)


def vector(vectors, layer, i):
    row = layer * 5 + i
    return jnp.concatenate([vectors[m, row : row + 1, :] for m in range(4)], axis=1)


def run_edges(which, shift, layer, f, meta_ref, receive, window, gather_ref, collect_ref, wmsg_ref, mvec_ref, hidden, normed, acc):
    slots = 6
    edges = gather_ref.shape[1]
    w_msg = jnp.concatenate([wmsg_ref[f ^ m] for m in range(4)], axis=0)
    bias = mvec_ref[layer, 0:1, :]

    def body(step, carry):
        ids = [meta_ref[which, step * UNROLL + u] for u in range(UNROLL)]
        blocks = [jnp.minimum(s // slots, 3) for s in ids]
        for u, (s, j) in enumerate(zip(ids, blocks)):
            at = meta_ref[2, s] - shift
            if which == 1:
                at = jnp.maximum(at, 0)
            to = receive[pl.ds(pl.multiple_of(j * edges, edges), edges), :]
            frm = window[pl.ds(pl.multiple_of(at * edges, edges), edges), :]
            terms = dot(gather_ref[s], jnp.concatenate([to, frm], axis=0))
            hidden[u * edges : (u + 1) * edges, :] = jnp.maximum(terms, 0.0).astype(BF16)
        for v in range(0, UNROLL, 2):
            rows = slice(v * edges, (v + 2) * edges)
            message = dot(hidden[rows, :], w_msg) + bias
            centred = message - jnp.mean(message, axis=1, keepdims=True)
            spread = jnp.mean(centred * centred, axis=1, keepdims=True)
            normed[rows, :] = (centred * lax.rsqrt(spread + EPSILON)).astype(BF16)
        for u, (s, j) in enumerate(zip(ids, blocks)):
            rows = pl.ds(pl.multiple_of(j * edges, edges), edges)
            acc[rows, :] = acc[rows, :] + dot(collect_ref[s], normed[u * edges : (u + 1) * edges, :])
        return carry

    lax.fori_loop(0, (meta_ref[3, which] + UNROLL - 1) // UNROLL, body, 0)


def near_kernel(layer, first, place_ref, meta_ref, h_ref, next_ref, wmsg_ref, mvec_ref, gather_ref, collect_ref, *refs):
    source, target, refs = refs[:4], refs[4:8], refs[8:]
    if first:
        shards, (acc, receive, vectors, window, hidden, normed) = refs[:4], refs[4:]
        for m, w in enumerate(shards):
            rows = w[...].astype(F32)
            vectors[m] = rows[:VECTOR_ROWS] + rows[VECTOR_ROWS : 2 * VECTOR_ROWS] + rows[2 * VECTOR_ROWS : 3 * VECTOR_ROWS]
    else:
        vectors, acc, receive, window, hidden, normed = refs
    f = place_ref[0]
    w_src = weight(source, f, True)
    own = wide(h_ref)
    block = own.shape[0]
    window[:block, :] = dot(own, w_src).astype(BF16)
    window[block:, :] = dot(wide(next_ref, FROM_NEXT), w_src).astype(BF16)
    receive[...] = (dot(own, weight(target, f, True)) + vector(vectors, layer, 0)).astype(BF16)
    acc[...] = jnp.zeros_like(acc)
    run_edges(0, 0, layer, f, meta_ref, receive, window, gather_ref, collect_ref, wmsg_ref, mvec_ref, hidden, normed, acc)


def far_kernel(layer, place_ref, meta_ref, after_ref, wmsg_ref, mvec_ref, gather_ref, collect_ref, acc_in, receive, w0, w1, w2, w3, out_ref, window, hidden, normed, acc):
    f = place_ref[0]
    window[...] = dot(wide(after_ref, FROM_BEYOND), weight((w0, w1, w2, w3), f, True)).astype(BF16)
    acc[...] = acc_in[...]
    run_edges(1, 8, layer, f, meta_ref, receive, window, gather_ref, collect_ref, wmsg_ref, mvec_ref, hidden, normed, acc)
    out_ref[...] = acc[...].astype(BF16)


def node_kernel(layer, final, place_ref, h_ref, part_a, part_b, degree_ref, vectors, mvec_ref, mgain_ref, *refs):
    f = place_ref[0]
    w_latent, w_sum, w_out, outs = refs[:4], refs[4:8], refs[8:12], refs[12:]
    part = h_ref.shape[-1]
    total = part_a[...].astype(F32) + part_b[...].astype(F32)
    agg = total * mgain_ref[layer : layer + 1, :] + degree_ref[:, 0:1] * mvec_ref[layer, 1:2, :]
    pre = dot(wide(h_ref), weight(w_latent, f, True))
    pre = pre + dot(agg.astype(BF16), weight(w_sum, f, False)) + vector(vectors, layer, 1)
    inner = jnp.maximum(pre, 0.0).astype(BF16)
    inner = jnp.concatenate([inner[:, m * part : (m + 1) * part] for m in ORDER], axis=1)
    node = dot(inner, weight(w_out, f, True)) + vector(vectors, layer, 2)
    centred = node - jnp.mean(node, axis=1, keepdims=True)
    spread = jnp.mean(centred * centred, axis=1, keepdims=True)
    change = centred * lax.rsqrt(spread + EPSILON) * vector(vectors, layer, 4) + vector(vectors, layer, 3)
    for i, m in enumerate(ORDER):
        if final and m not in (0, 2):
            continue
        new = (h_ref[i].astype(F32) + change[:, m * part : (m + 1) * part]).astype(BF16)
        if final:
            outs[m // 2][...] = new
        else:
            outs[0][i] = new


def join_kernel(place_ref, own_ref, other_ref, out_ref):
    rows = own_ref.shape[0]
    side = place_ref[4]
    out_ref[pl.ds(pl.multiple_of(side * rows, rows), rows), :] = own_ref[...]
    out_ref[pl.ds(pl.multiple_of((1 - side) * rows, rows), rows), :] = other_ref[...]


def rows_of(weights, at, count):
    return weights, [pl.BlockSpec((count, w.shape[-1]), lambda i: (at, 0)) for w in weights]


def call(kernel, name, inputs, spaces, outs, out_spaces, scratch=(), us=2):
    return pl.pallas_call(
        kernel,
        out_shape=outs,
        grid=(1,),
        in_specs=spaces,
        out_specs=out_spaces,
        scratch_shapes=list(scratch),
        compiler_params=pltpu.CompilerParams(vmem_limit_bytes=32 * 1024 * 1024),
        cost_estimate=pl.CostEstimate(flops=int(us * 1e9), bytes_accessed=1 << 20, transcendentals=0),
        name=name,
    )(*inputs)


def per_device(
    node_state,
    w_dst,
    w_src,
    w_msg,
    w_node_in,
    w_node_out,
    msg_vectors,
    msg_gain,
    node_vectors,
    node_gain,
    nbr_blocks,
    edge_count,
    edge_src,
    edge_dst,
):
    width = w_msg.shape[1]
    part = width // 4
    block_count, slots = nbr_blocks.shape
    edges = edge_src.shape[2]
    mine = block_count // 2
    rows = mine * edges
    feat = lax.axis_index("feat")
    dom = lax.axis_index("dom")
    side = feat // 2
    place = jnp.stack([feat, feat % 2, side * mine, dom * block_count + side * mine, side]).astype(jnp.int32)
    barrier = lax.optimization_barrier

    halves = node_state.reshape(2, rows, part)
    own = lax.dynamic_index_in_dim(halves, side, 0, keepdims=False)
    other = lax.dynamic_index_in_dim(halves, 1 - side, 0, keepdims=False)
    pack, next_pack = call(
        pack_kernel,
        "packs",
        (w_src, w_dst, w_node_in, w_node_out, node_vectors, node_gain),
        [ANY] * 4 + [VMEM] * 2,
        (
            jax.ShapeDtypeStruct((5 * width + 4 * VECTOR_ROWS, part), BF16),
            jax.ShapeDtypeStruct((5 * width, part), BF16),
        ),
        (ANY, ANY),
        [pltpu.VMEM((4 * VECTOR_ROWS, part), BF16), pltpu.SemaphoreType.DMA((9,))],
    )
    across = exchange(other, 2)
    pack_across = exchange(pack, 2)
    next_share, across = barrier((next_pack, across))
    next_across = from_other_side(next_share)
    beside = exchange(pack, 1)
    next_share, beside = barrier((next_pack, beside))
    next_beside = exchange(next_share, 1)
    pair = barrier((jnp.stack([own, across]), pack))[0]
    latent = jnp.concatenate([pair, exchange(pair, 1)], axis=0)

    all_slots = mine * slots + 1
    nbr_blocks = barrier((nbr_blocks, latent))[0]
    gather, collect, degree, meta = call(
        prepare_kernel,
        "one_hots",
        (place, nbr_blocks, edge_count, edge_src, edge_dst),
        [SMEM] * 3 + [VMEM] * 2,
        (
            jax.ShapeDtypeStruct((all_slots, edges, 2 * edges), BF16),
            jax.ShapeDtypeStruct((all_slots, edges, edges), BF16),
            jax.ShapeDtypeStruct((rows, edges), F32),
            jax.ShapeDtypeStruct((4, LIST), jnp.int32),
        ),
        (VMEM, VMEM, VMEM, SMEM),
        [pltpu.VMEM((edges, edges), F32)],
        us=3,
    )
    vectors = None
    messages = w_msg.reshape(LAYERS * 4, part, width)
    for layer in range(LAYERS):
        final = layer == LAYERS - 1
        after = swap_with(latent, 1)
        beyond = swap_with(latent, 2)
        if layer == 0:
            pack_across, next_across, next_beside, after, beyond, meta = barrier(
                (pack_across, next_across, next_beside, after, beyond, meta)
            )
            weights = (pack, beside, pack_across, exchange(pack_across, 1))
        message_spec = pl.BlockSpec((4, part, width), lambda i, layer=layer: (layer, 0, 0))
        edge_inputs = [messages, msg_vectors, gather, collect]
        edge_specs = [message_spec, VMEM, VMEM, VMEM]
        source, source_specs = rows_of(weights, 3, width)
        target, target_specs = rows_of(weights, 4, width)
        outs = [jax.ShapeDtypeStruct((rows, width), F32), jax.ShapeDtypeStruct((rows, width), BF16)]
        if layer == 0:
            outs.append(jax.ShapeDtypeStruct((4, VECTOR_ROWS, part), F32))
            extra, extra_specs = rows_of(weights, 5 * width // (4 * VECTOR_ROWS), 4 * VECTOR_ROWS)
        else:
            extra, extra_specs = (vectors,), [VMEM]
        result = call(
            lambda *refs, layer=layer: near_kernel(layer, layer == 0, *refs),
            f"near{layer}",
            [place, meta, latent, after, *edge_inputs, *source, *target, *extra],
            [SMEM, SMEM, VMEM, VMEM, *edge_specs, *source_specs, *target_specs, *extra_specs],
            outs,
            [VMEM] * len(outs),
            [
                pltpu.VMEM((2 * rows, width), BF16),
                pltpu.VMEM((UNROLL * edges, width), BF16),
                pltpu.VMEM((UNROLL * edges, width), BF16),
            ],
            us=5,
        )
        acc, receive = result[0], result[1]
        if layer == 0:
            vectors = result[2]
            next_weights = (next_pack, next_beside, next_across, exchange(next_across, 1))
        else:
            beyond, acc = barrier((beyond, acc))
        partial = call(
            lambda *refs, layer=layer: far_kernel(layer, *refs),
            f"far{layer}",
            [place, meta, beyond, *edge_inputs, acc, receive, *source],
            [SMEM, SMEM, VMEM, *edge_specs, VMEM, VMEM, *source_specs],
            jax.ShapeDtypeStruct((rows, width), BF16),
            VMEM,
            [
                pltpu.VMEM((rows, width), BF16),
                pltpu.VMEM((UNROLL * edges, width), BF16),
                pltpu.VMEM((UNROLL * edges, width), BF16),
                pltpu.VMEM((rows, width), F32),
            ],
            us=3,
        )
        theirs = exchange(partial, 1)
        if final:
            outs = [jax.ShapeDtypeStruct((rows, part), BF16)] * 2
        else:
            outs = [jax.ShapeDtypeStruct((4, rows, part), BF16)]
        matrices = [rows_of(weights, i, width) for i in range(3)]
        result = call(
            lambda *refs, layer=layer, final=final: node_kernel(layer, final, *refs),
            f"node{layer}",
            [place, latent, partial, theirs, degree, vectors, msg_vectors, msg_gain] + [w for group, _ in matrices for w in group],
            [SMEM] + [VMEM] * 7 + [spec for _, specs in matrices for spec in specs],
            outs,
            [VMEM] * len(outs),
        )
        if final:
            return call(
                join_kernel,
                "join",
                [place, result[0], exchange(result[1], 2)],
                [SMEM, VMEM, VMEM],
                jax.ShapeDtypeStruct((2 * rows, part), BF16),
                VMEM,
            )
        latent = result[0]
        weights = next_weights


def solution(mesh):
    placed = (
        P("dom", "feat"),
        P(None, None, "feat"),
        P(None, None, "feat"),
        P(),
        P(None, None, "feat"),
        P(None, None, "feat"),
        P(),
        P(),
        P(None, None, "feat"),
        P(None, "feat"),
        P("dom", None),
        P("dom", None),
        P("dom", None, None),
        P("dom", None, None),
    )
    return jax.shard_map(
        per_device, mesh=mesh, in_specs=placed, out_specs=P("dom", "feat"), check_vma=False
    )
```

```python
import jax
import jax.numpy as jnp
from jax import lax
from jax.experimental import pallas as pl
from jax.experimental.pallas import tpu as pltpu
from jax.sharding import PartitionSpec as P

LAYERS = 2
EPSILON = 1e-05
BOTH = ("dom", "feat")
F32 = jnp.float32
BF16 = jnp.bfloat16
VECTOR_ROWS = 16
ORDER = (0, 2, 1, 3)
STRAIGHT = (0, 1, 2, 3)
FROM_NEXT = (3, 2, 1, 0)
FROM_BEYOND = (2, 3, 0, 1)
UNROLL = 4
LIST = 32
VMEM = pl.BlockSpec(memory_space=pltpu.VMEM)
SMEM = pl.BlockSpec(memory_space=pltpu.SMEM)
HBM = pl.BlockSpec(memory_space=pltpu.HBM)


def dot(a, b):
    return jnp.dot(a, b, preferred_element_type=F32)


def exchange(value, mask):
    total = lax.axis_size(BOTH)
    return lax.ppermute(value, BOTH, [(i, i ^ mask) for i in range(total)])


def swap_with(value, chips):
    total = lax.axis_size(BOTH)
    step = 2 * chips + 1
    pairs = [(i, i + (step if i % 2 == 0 else -step)) for i in range(total)]
    return lax.ppermute(value, BOTH, [(i, t) for i, t in pairs if 0 <= t < total])


def from_other_side(value):
    total = lax.axis_size(BOTH)
    pairs = []
    for i in range(total):
        column, low = divmod(i, 16)
        z, core = divmod(low, 2)
        z = (z + (1 if z % 2 else -1)) % 8
        pairs.append((i, column * 16 + z * 2 + core))
    return lax.ppermute(value, BOTH, pairs)


def prepare_kernel(place_ref, nbr_ref, count_ref, src_ref, dst_ref, gather_ref, collect_ref, degree_ref, meta_ref, turned):
    last, edges, _ = gather_ref.shape
    slots = nbr_ref.shape[1]
    blocks = last // slots
    core, first, base = place_ref[1], place_ref[2], place_ref[3]
    lanes = lax.broadcasted_iota(jnp.int32, (edges, edges), 1)
    rows = lax.broadcasted_iota(jnp.int32, (edges, edges), 0)
    for i in range(LIST):
        meta_ref[0, i] = last - 1
        meta_ref[1, i] = last - 1
        meta_ref[2, i] = 0
    near, far = jnp.int32(0), jnp.int32(0)
    turned[...] = jnp.zeros_like(turned)
    for j in range(blocks):
        turned[0:slots, :] = src_ref[first + j].astype(F32)
        turned[8 : 8 + slots, :] = dst_ref[first + j].astype(F32)
        columns = turned[...].T.astype(jnp.int32)
        to_row = dst_ref[first + j]
        degree = jnp.zeros((edges, edges), F32)
        for k in range(slots):
            s = j * slots + k
            gather_ref[s, :, :edges] = (columns[:, 8 + k : 9 + k] == lanes).astype(F32).astype(BF16)
            gather_ref[s, :, edges:] = (columns[:, k : k + 1] == lanes).astype(F32).astype(BF16)
            live = ((to_row[k : k + 1, :] == rows) & (lanes < count_ref[first + j, k])).astype(F32)
            collect_ref[s] = live.astype(BF16)
            degree = degree + live
            place = nbr_ref[first + j, k] - base
            step = (place + 2 * blocks) // blocks - 2
            hops = jnp.abs(step)
            meta_ref[2, s] = hops * blocks + place - step * blocks
            mine = jnp.where(step == 0, core == j // (blocks // 2), (step > 0) == (core == 0))
            is_far = mine & (hops == 2)
            is_near = mine & (hops < 2)

            @pl.when(is_near)
            def _():
                meta_ref[0, near] = s

            @pl.when(is_far)
            def _():
                meta_ref[1, far] = s

            near = near + is_near.astype(jnp.int32)
            far = far + is_far.astype(jnp.int32)
        degree_ref[j * edges : (j + 1) * edges, :] = jnp.broadcast_to(
            jnp.sum(degree, axis=1, keepdims=True), (edges, edges)
        )
    meta_ref[3, 0] = near
    meta_ref[3, 1] = far
    gather_ref[last - 1] = jnp.zeros(gather_ref.shape[1:], BF16)
    collect_ref[last - 1] = jnp.zeros(collect_ref.shape[1:], BF16)


def pack_kernel(src_ref, dst_ref, in_ref, out_w_ref, vec_ref, gain_ref, first_ref, next_ref, rows, sems):
    width = src_ref.shape[1]
    copies = []
    for layer, ref in enumerate((first_ref, next_ref)):
        for source, at in ((in_ref, 0), (out_w_ref, 2), (src_ref, 3), (dst_ref, 4)):
            count = source.shape[1]
            copies.append(
                pltpu.make_async_copy(
                    source.at[layer], ref.at[pl.ds(at * width, count), :], sems.at[len(copies)]
                )
            )
    for copy in copies:
        copy.start()
    rest = jnp.concatenate(
        [part for layer in range(LAYERS) for part in (vec_ref[layer], gain_ref[layer : layer + 1, :])]
        + [jnp.zeros((VECTOR_ROWS - 5 * LAYERS, src_ref.shape[2]), F32)],
        axis=0,
    )
    for i in range(3):
        piece = rest.astype(BF16)
        rows[i * VECTOR_ROWS : (i + 1) * VECTOR_ROWS, :] = piece
        rest = rest - piece.astype(F32)
    rows[3 * VECTOR_ROWS :, :] = jnp.zeros((VECTOR_ROWS, src_ref.shape[2]), BF16)
    last = pltpu.make_async_copy(
        rows, first_ref.at[pl.ds(5 * width, 4 * VECTOR_ROWS), :], sems.at[len(copies)]
    )
    last.start()
    for copy in copies:
        copy.wait()
    last.wait()


def wide(ref, order=STRAIGHT):
    return jnp.concatenate([ref[i] for i in order], axis=1)


def weight(shards, f, mixed):
    part = shards[0].shape[-1]
    rows = []
    for i in range(4):
        at = pl.ds(pl.multiple_of((f ^ ORDER[i]) * part, part) if mixed else i * part, part)
        rows.append(jnp.concatenate([w[at, :] for w in shards], axis=1))
    return jnp.concatenate(rows, axis=0)


def vector(vectors, layer, i):
    row = layer * 5 + i
    return jnp.concatenate([vectors[m, row : row + 1, :] for m in range(4)], axis=1)


def run_edges(which, shift, layer, f, meta_ref, receive, window, gather_ref, collect_ref, wmsg_ref, mvec_ref, hidden, normed, acc):
    slots = 6
    edges = gather_ref.shape[1]
    w_msg = jnp.concatenate([wmsg_ref[f ^ m] for m in range(4)], axis=0)
    bias = mvec_ref[layer, 0:1, :]

    def body(step, carry):
        ids = [meta_ref[which, step * UNROLL + u] for u in range(UNROLL)]
        blocks = [jnp.minimum(s // slots, 3) for s in ids]
        for u, (s, j) in enumerate(zip(ids, blocks)):
            at = meta_ref[2, s] - shift
            if which == 1:
                at = jnp.maximum(at, 0)
            to = receive[pl.ds(pl.multiple_of(j * edges, edges), edges), :]
            frm = window[pl.ds(pl.multiple_of(at * edges, edges), edges), :]
            terms = dot(gather_ref[s], jnp.concatenate([to, frm], axis=0))
            hidden[u * edges : (u + 1) * edges, :] = jnp.maximum(terms, 0.0).astype(BF16)
        for v in range(0, UNROLL, 2):
            rows = slice(v * edges, (v + 2) * edges)
            message = dot(hidden[rows, :], w_msg) + bias
            centred = message - jnp.mean(message, axis=1, keepdims=True)
            spread = jnp.mean(centred * centred, axis=1, keepdims=True)
            normed[rows, :] = (centred * lax.rsqrt(spread + EPSILON)).astype(BF16)
        for u, (s, j) in enumerate(zip(ids, blocks)):
            rows = pl.ds(pl.multiple_of(j * edges, edges), edges)
            acc[rows, :] = acc[rows, :] + dot(collect_ref[s], normed[u * edges : (u + 1) * edges, :])
        return carry

    lax.fori_loop(0, (meta_ref[3, which] + UNROLL - 1) // UNROLL, body, 0)


def near_kernel(layer, first, place_ref, meta_ref, h_ref, next_ref, wmsg_ref, mvec_ref, gather_ref, collect_ref, *refs):
    source, target, refs = refs[:4], refs[4:8], refs[8:]
    if first:
        shards, (acc, receive, vectors, window, hidden, normed) = refs[:4], refs[4:]
        for m, w in enumerate(shards):
            rows = w[...].astype(F32)
            vectors[m] = rows[:VECTOR_ROWS] + rows[VECTOR_ROWS : 2 * VECTOR_ROWS] + rows[2 * VECTOR_ROWS : 3 * VECTOR_ROWS]
    else:
        vectors, acc, receive, window, hidden, normed = refs
    f = place_ref[0]
    w_src = weight(source, f, True)
    own = wide(h_ref)
    block = own.shape[0]
    window[:block, :] = dot(own, w_src).astype(BF16)
    window[block:, :] = dot(wide(next_ref, FROM_NEXT), w_src).astype(BF16)
    receive[...] = (dot(own, weight(target, f, True)) + vector(vectors, layer, 0)).astype(BF16)
    acc[...] = jnp.zeros_like(acc)
    run_edges(0, 0, layer, f, meta_ref, receive, window, gather_ref, collect_ref, wmsg_ref, mvec_ref, hidden, normed, acc)


def far_kernel(layer, place_ref, meta_ref, after_ref, wmsg_ref, mvec_ref, gather_ref, collect_ref, acc_in, receive, w0, w1, w2, w3, out_ref, window, hidden, normed, acc):
    f = place_ref[0]
    window[...] = dot(wide(after_ref, FROM_BEYOND), weight((w0, w1, w2, w3), f, True)).astype(BF16)
    acc[...] = acc_in[...]
    run_edges(1, 8, layer, f, meta_ref, receive, window, gather_ref, collect_ref, wmsg_ref, mvec_ref, hidden, normed, acc)
    out_ref[...] = acc[...].astype(BF16)


def node_kernel(layer, final, place_ref, h_ref, part_a, part_b, degree_ref, vectors, mvec_ref, mgain_ref, *refs):
    f = place_ref[0]
    w_latent, w_sum, w_out, outs = refs[:4], refs[4:8], refs[8:12], refs[12:]
    part = h_ref.shape[-1]
    total = part_a[...].astype(F32) + part_b[...].astype(F32)
    agg = total * mgain_ref[layer : layer + 1, :] + degree_ref[:, 0:1] * mvec_ref[layer, 1:2, :]
    pre = dot(wide(h_ref), weight(w_latent, f, True))
    pre = pre + dot(agg.astype(BF16), weight(w_sum, f, False)) + vector(vectors, layer, 1)
    inner = jnp.maximum(pre, 0.0).astype(BF16)
    inner = jnp.concatenate([inner[:, m * part : (m + 1) * part] for m in ORDER], axis=1)
    node = dot(inner, weight(w_out, f, True)) + vector(vectors, layer, 2)
    centred = node - jnp.mean(node, axis=1, keepdims=True)
    spread = jnp.mean(centred * centred, axis=1, keepdims=True)
    change = centred * lax.rsqrt(spread + EPSILON) * vector(vectors, layer, 4) + vector(vectors, layer, 3)
    for i, m in enumerate(ORDER):
        if final and m not in (0, 2):
            continue
        new = (h_ref[i].astype(F32) + change[:, m * part : (m + 1) * part]).astype(BF16)
        if final:
            outs[m // 2][...] = new
        else:
            outs[0][i] = new


def join_kernel(place_ref, own_ref, other_ref, out_ref):
    rows = own_ref.shape[0]
    side = place_ref[4]
    out_ref[pl.ds(pl.multiple_of(side * rows, rows), rows), :] = own_ref[...]
    out_ref[pl.ds(pl.multiple_of((1 - side) * rows, rows), rows), :] = other_ref[...]


def rows_of(weights, at, count):
    return weights, [pl.BlockSpec((count, w.shape[-1]), lambda i: (at, 0)) for w in weights]


def call(kernel, name, inputs, spaces, outs, out_spaces, scratch=(), us=2, mib=32):
    return pl.pallas_call(
        kernel,
        out_shape=outs,
        grid=(1,),
        in_specs=spaces,
        out_specs=out_spaces,
        scratch_shapes=list(scratch),
        compiler_params=pltpu.CompilerParams(vmem_limit_bytes=mib * 1024 * 1024),
        cost_estimate=pl.CostEstimate(flops=int(us * 1e9), bytes_accessed=1 << 20, transcendentals=0),
        name=name,
    )(*inputs)


def per_device(
    node_state,
    w_dst,
    w_src,
    w_msg,
    w_node_in,
    w_node_out,
    msg_vectors,
    msg_gain,
    node_vectors,
    node_gain,
    nbr_blocks,
    edge_count,
    edge_src,
    edge_dst,
):
    width = w_msg.shape[1]
    part = width // 4
    block_count, slots = nbr_blocks.shape
    edges = edge_src.shape[2]
    mine = block_count // 2
    rows = mine * edges
    feat = lax.axis_index("feat")
    dom = lax.axis_index("dom")
    side = feat // 2
    place = jnp.stack([feat, feat % 2, side * mine, dom * block_count + side * mine, side]).astype(jnp.int32)
    barrier = lax.optimization_barrier

    halves = node_state.reshape(2, rows, part)
    own = lax.dynamic_index_in_dim(halves, side, 0, keepdims=False)
    other = lax.dynamic_index_in_dim(halves, 1 - side, 0, keepdims=False)
    pack, next_pack = call(
        pack_kernel,
        "packs",
        (w_src, w_dst, w_node_in, w_node_out, node_vectors, node_gain),
        [HBM] * 4 + [VMEM] * 2,
        (
            jax.ShapeDtypeStruct((5 * width + 4 * VECTOR_ROWS, part), BF16),
            jax.ShapeDtypeStruct((5 * width, part), BF16),
        ),
        (HBM, HBM),
        [pltpu.VMEM((4 * VECTOR_ROWS, part), BF16), pltpu.SemaphoreType.DMA((9,))],
        mib=60,
    )
    other = barrier((other, pack))[0]
    across = exchange(other, 2)
    pack_across = exchange(pack, 2)
    next_across = from_other_side(next_pack)
    beside = exchange(pack, 1)
    next_beside = exchange(next_pack, 1)

    all_slots = mine * slots + 1
    gather, collect, degree, meta = call(
        prepare_kernel,
        "one_hots",
        (place, nbr_blocks, edge_count, edge_src, edge_dst),
        [SMEM] * 3 + [VMEM] * 2,
        (
            jax.ShapeDtypeStruct((all_slots, edges, 2 * edges), BF16),
            jax.ShapeDtypeStruct((all_slots, edges, edges), BF16),
            jax.ShapeDtypeStruct((rows, edges), F32),
            jax.ShapeDtypeStruct((4, LIST), jnp.int32),
        ),
        (VMEM, VMEM, VMEM, SMEM),
        [pltpu.VMEM((edges, edges), F32)],
        us=3,
    )
    pair = jnp.stack([own, across])
    pair, pack_across, next_across, beside, next_beside, meta = barrier(
        (pair, pack_across, next_across, beside, next_beside, meta)
    )
    latent = jnp.concatenate([pair, exchange(pair, 1)], axis=0)
    pack_across = barrier((pack_across, latent))[0]
    weights = (pack, beside, pack_across, exchange(pack_across, 1))

    vectors = None
    messages = w_msg.reshape(LAYERS * 4, part, width)
    for layer in range(LAYERS):
        final = layer == LAYERS - 1
        after = swap_with(latent, 1)
        beyond = swap_with(latent, 2)
        message_spec = pl.BlockSpec((4, part, width), lambda i, layer=layer: (layer, 0, 0))
        edge_inputs = [messages, msg_vectors, gather, collect]
        edge_specs = [message_spec, VMEM, VMEM, VMEM]
        source, source_specs = rows_of(weights, 3, width)
        target, target_specs = rows_of(weights, 4, width)
        outs = [jax.ShapeDtypeStruct((rows, width), F32), jax.ShapeDtypeStruct((rows, width), BF16)]
        if layer == 0:
            outs.append(jax.ShapeDtypeStruct((4, VECTOR_ROWS, part), F32))
            extra, extra_specs = rows_of(weights, 5 * width // (4 * VECTOR_ROWS), 4 * VECTOR_ROWS)
        else:
            extra, extra_specs = (vectors,), [VMEM]
        result = call(
            lambda *refs, layer=layer: near_kernel(layer, layer == 0, *refs),
            f"near{layer}",
            [place, meta, latent, after, *edge_inputs, *source, *target, *extra],
            [SMEM, SMEM, VMEM, VMEM, *edge_specs, *source_specs, *target_specs, *extra_specs],
            outs,
            [VMEM] * len(outs),
            [
                pltpu.VMEM((2 * rows, width), BF16),
                pltpu.VMEM((UNROLL * edges, width), BF16),
                pltpu.VMEM((UNROLL * edges, width), BF16),
            ],
            us=5,
        )
        acc, receive = result[0], result[1]
        if layer == 0:
            vectors = result[2]
            next_across = barrier((next_across, acc))[0]
            next_weights = (next_pack, next_beside, next_across, exchange(next_across, 1))
        beyond, acc = barrier((beyond, acc))
        partial = call(
            lambda *refs, layer=layer: far_kernel(layer, *refs),
            f"far{layer}",
            [place, meta, beyond, *edge_inputs, acc, receive, *source],
            [SMEM, SMEM, VMEM, *edge_specs, VMEM, VMEM, *source_specs],
            jax.ShapeDtypeStruct((rows, width), BF16),
            VMEM,
            [
                pltpu.VMEM((rows, width), BF16),
                pltpu.VMEM((UNROLL * edges, width), BF16),
                pltpu.VMEM((UNROLL * edges, width), BF16),
                pltpu.VMEM((rows, width), F32),
            ],
            us=3,
        )
        theirs = exchange(partial, 1)
        if final:
            outs = [jax.ShapeDtypeStruct((rows, part), BF16)] * 2
        else:
            outs = [jax.ShapeDtypeStruct((4, rows, part), BF16)]
        matrices = [rows_of(weights, i, width) for i in range(3)]
        result = call(
            lambda *refs, layer=layer, final=final: node_kernel(layer, final, *refs),
            f"node{layer}",
            [place, latent, partial, theirs, degree, vectors, msg_vectors, msg_gain] + [w for group, _ in matrices for w in group],
            [SMEM] + [VMEM] * 7 + [spec for _, specs in matrices for spec in specs],
            outs,
            [VMEM] * len(outs),
        )
        if final:
            return call(
                join_kernel,
                "join",
                [place, result[0], exchange(result[1], 2)],
                [SMEM, VMEM, VMEM],
                jax.ShapeDtypeStruct((2 * rows, part), BF16),
                VMEM,
            )
        latent = result[0]
        weights = next_weights


def solution(mesh):
    placed = (
        P("dom", "feat"),
        P(None, None, "feat"),
        P(None, None, "feat"),
        P(),
        P(None, None, "feat"),
        P(None, None, "feat"),
        P(),
        P(),
        P(None, None, "feat"),
        P(None, "feat"),
        P("dom", None),
        P("dom", None),
        P("dom", None, None),
        P("dom", None, None),
    )
    return jax.shard_map(
        per_device, mesh=mesh, in_specs=placed, out_specs=P("dom", "feat"), check_vma=False
    )
```

```python
import jax
import jax.numpy as jnp
from jax import lax
from jax.experimental import pallas as pl
from jax.experimental.pallas import tpu as pltpu
from jax.sharding import PartitionSpec as P

LAYERS = 2
EPSILON = 1e-05
BOTH = ("dom", "feat")
F32 = jnp.float32
BF16 = jnp.bfloat16
VECTOR_ROWS = 16
ORDER = (0, 2, 1, 3)
STRAIGHT = (0, 1, 2, 3)
FROM_NEXT = (3, 2, 1, 0)
FROM_BEYOND = (2, 3, 0, 1)
UNROLL = 4
LIST = 32
VMEM = pl.BlockSpec(memory_space=pltpu.VMEM)
SMEM = pl.BlockSpec(memory_space=pltpu.SMEM)
HBM = pl.BlockSpec(memory_space=pltpu.HBM)


def dot(a, b):
    return jnp.dot(a, b, preferred_element_type=F32)


def exchange(value, mask):
    total = lax.axis_size(BOTH)
    return lax.ppermute(value, BOTH, [(i, i ^ mask) for i in range(total)])


def swap_with(value, chips):
    total = lax.axis_size(BOTH)
    step = 2 * chips + 1
    pairs = [(i, i + (step if i % 2 == 0 else -step)) for i in range(total)]
    return lax.ppermute(value, BOTH, [(i, t) for i, t in pairs if 0 <= t < total])


def from_other_side(value):
    total = lax.axis_size(BOTH)
    pairs = []
    for i in range(total):
        column, low = divmod(i, 16)
        z, core = divmod(low, 2)
        z = (z + (1 if z % 2 else -1)) % 8
        pairs.append((i, column * 16 + z * 2 + core))
    return lax.ppermute(value, BOTH, pairs)


def prepare_kernel(place_ref, nbr_ref, count_ref, src_ref, dst_ref, gather_ref, collect_ref, degree_ref, meta_ref, turned):
    last, edges, _ = gather_ref.shape
    slots = nbr_ref.shape[1]
    blocks = last // slots
    core, first, base = place_ref[1], place_ref[2], place_ref[3]
    lanes = lax.broadcasted_iota(jnp.int32, (edges, edges), 1)
    rows = lax.broadcasted_iota(jnp.int32, (edges, edges), 0)
    for i in range(LIST):
        meta_ref[0, i] = last - 1
        meta_ref[1, i] = last - 1
        meta_ref[2, i] = 0
    near, far = jnp.int32(0), jnp.int32(0)
    turned[...] = jnp.zeros_like(turned)
    for j in range(blocks):
        turned[0:slots, :] = src_ref[first + j].astype(F32)
        turned[8 : 8 + slots, :] = dst_ref[first + j].astype(F32)
        columns = turned[...].T.astype(jnp.int32)
        to_row = dst_ref[first + j]
        degree = jnp.zeros((edges, edges), F32)
        for k in range(slots):
            s = j * slots + k
            gather_ref[s, :, :edges] = (columns[:, 8 + k : 9 + k] == lanes).astype(F32).astype(BF16)
            gather_ref[s, :, edges:] = (columns[:, k : k + 1] == lanes).astype(F32).astype(BF16)
            live = ((to_row[k : k + 1, :] == rows) & (lanes < count_ref[first + j, k])).astype(F32)
            collect_ref[s] = live.astype(BF16)
            degree = degree + live
            place = nbr_ref[first + j, k] - base
            step = (place + 2 * blocks) // blocks - 2
            hops = jnp.abs(step)
            meta_ref[2, s] = hops * blocks + place - step * blocks
            mine = jnp.where(step == 0, core == j // (blocks // 2), (step > 0) == (core == 0))
            is_far = mine & (hops == 2)
            is_near = mine & (hops < 2)

            @pl.when(is_near)
            def _():
                meta_ref[0, near] = s

            @pl.when(is_far)
            def _():
                meta_ref[1, far] = s

            near = near + is_near.astype(jnp.int32)
            far = far + is_far.astype(jnp.int32)
        degree_ref[j * edges : (j + 1) * edges, :] = jnp.broadcast_to(
            jnp.sum(degree, axis=1, keepdims=True), (edges, edges)
        )
    meta_ref[3, 0] = near
    meta_ref[3, 1] = far
    gather_ref[last - 1] = jnp.zeros(gather_ref.shape[1:], BF16)
    collect_ref[last - 1] = jnp.zeros(collect_ref.shape[1:], BF16)


def pack_kernel(src_ref, dst_ref, in_ref, out_w_ref, vec_ref, gain_ref, first_ref, next_ref, rows, sems):
    width = src_ref.shape[1]
    copies = []
    for layer, ref in enumerate((first_ref, next_ref)):
        for source, at in ((in_ref, 0), (out_w_ref, 2), (src_ref, 3), (dst_ref, 4)):
            count = source.shape[1]
            copies.append(
                pltpu.make_async_copy(
                    source.at[layer], ref.at[pl.ds(at * width, count), :], sems.at[len(copies)]
                )
            )
    for copy in copies:
        copy.start()
    rest = jnp.concatenate(
        [part for layer in range(LAYERS) for part in (vec_ref[layer], gain_ref[layer : layer + 1, :])]
        + [jnp.zeros((VECTOR_ROWS - 5 * LAYERS, src_ref.shape[2]), F32)],
        axis=0,
    )
    for i in range(3):
        piece = rest.astype(BF16)
        rows[i * VECTOR_ROWS : (i + 1) * VECTOR_ROWS, :] = piece
        rest = rest - piece.astype(F32)
    rows[3 * VECTOR_ROWS :, :] = jnp.zeros((VECTOR_ROWS, src_ref.shape[2]), BF16)
    last = pltpu.make_async_copy(
        rows, first_ref.at[pl.ds(5 * width, 4 * VECTOR_ROWS), :], sems.at[len(copies)]
    )
    last.start()
    for copy in copies:
        copy.wait()
    last.wait()


def wide(ref, order=STRAIGHT):
    return jnp.concatenate([ref[i] for i in order], axis=1)


def weight(shards, f, mixed):
    part = shards[0].shape[-1]
    rows = []
    for i in range(4):
        at = pl.ds(pl.multiple_of((f ^ ORDER[i]) * part, part) if mixed else i * part, part)
        rows.append(jnp.concatenate([w[at, :] for w in shards], axis=1))
    return jnp.concatenate(rows, axis=0)


def vector(vectors, layer, i):
    row = layer * 5 + i
    return jnp.concatenate([vectors[m, row : row + 1, :] for m in range(4)], axis=1)


def run_edges(which, shift, layer, f, meta_ref, receive, window, gather_ref, collect_ref, wmsg_ref, mvec_ref, hidden, normed, acc):
    slots = 6
    edges = gather_ref.shape[1]
    w_msg = jnp.concatenate([wmsg_ref[f ^ m] for m in range(4)], axis=0)
    bias = mvec_ref[layer, 0:1, :]

    def body(step, carry):
        ids = [meta_ref[which, step * UNROLL + u] for u in range(UNROLL)]
        blocks = [jnp.minimum(s // slots, 3) for s in ids]
        for u, (s, j) in enumerate(zip(ids, blocks)):
            at = meta_ref[2, s] - shift
            if which == 1:
                at = jnp.maximum(at, 0)
            to = receive[pl.ds(pl.multiple_of(j * edges, edges), edges), :]
            frm = window[pl.ds(pl.multiple_of(at * edges, edges), edges), :]
            terms = dot(gather_ref[s], jnp.concatenate([to, frm], axis=0))
            hidden[u * edges : (u + 1) * edges, :] = jnp.maximum(terms, 0.0).astype(BF16)
        for v in range(0, UNROLL, 2):
            rows = slice(v * edges, (v + 2) * edges)
            message = dot(hidden[rows, :], w_msg) + bias
            centred = message - jnp.mean(message, axis=1, keepdims=True)
            spread = jnp.mean(centred * centred, axis=1, keepdims=True)
            normed[rows, :] = (centred * lax.rsqrt(spread + EPSILON)).astype(BF16)
        for u, (s, j) in enumerate(zip(ids, blocks)):
            rows = pl.ds(pl.multiple_of(j * edges, edges), edges)
            acc[rows, :] = acc[rows, :] + dot(collect_ref[s], normed[u * edges : (u + 1) * edges, :])
        return carry

    lax.fori_loop(0, (meta_ref[3, which] + UNROLL - 1) // UNROLL, body, 0)


def near_kernel(layer, first, place_ref, meta_ref, h_ref, next_ref, wmsg_ref, mvec_ref, gather_ref, collect_ref, *refs):
    source, target, refs = refs[:4], refs[4:8], refs[8:]
    if first:
        shards, (acc, receive, vectors, window, hidden, normed) = refs[:4], refs[4:]
        for m, w in enumerate(shards):
            rows = w[...].astype(F32)
            vectors[m] = rows[:VECTOR_ROWS] + rows[VECTOR_ROWS : 2 * VECTOR_ROWS] + rows[2 * VECTOR_ROWS : 3 * VECTOR_ROWS]
    else:
        vectors, acc, receive, window, hidden, normed = refs
    f = place_ref[0]
    w_src = weight(source, f, True)
    own = wide(h_ref)
    block = own.shape[0]
    window[:block, :] = dot(own, w_src).astype(BF16)
    window[block:, :] = dot(wide(next_ref, FROM_NEXT), w_src).astype(BF16)
    receive[...] = (dot(own, weight(target, f, True)) + vector(vectors, layer, 0)).astype(BF16)
    acc[...] = jnp.zeros_like(acc)
    run_edges(0, 0, layer, f, meta_ref, receive, window, gather_ref, collect_ref, wmsg_ref, mvec_ref, hidden, normed, acc)


def far_kernel(layer, place_ref, meta_ref, after_ref, wmsg_ref, mvec_ref, gather_ref, collect_ref, acc_in, receive, w0, w1, w2, w3, out_ref, window, hidden, normed, acc):
    f = place_ref[0]
    window[...] = dot(wide(after_ref, FROM_BEYOND), weight((w0, w1, w2, w3), f, True)).astype(BF16)
    acc[...] = acc_in[...]
    run_edges(1, 8, layer, f, meta_ref, receive, window, gather_ref, collect_ref, wmsg_ref, mvec_ref, hidden, normed, acc)
    out_ref[...] = acc[...].astype(BF16)


def node_kernel(layer, final, place_ref, h_ref, part_a, part_b, degree_ref, vectors, mvec_ref, mgain_ref, *refs):
    f = place_ref[0]
    w_latent, w_sum, w_out, outs = refs[:4], refs[4:8], refs[8:12], refs[12:]
    part = h_ref.shape[-1]
    total = part_a[...].astype(F32) + part_b[...].astype(F32)
    agg = total * mgain_ref[layer : layer + 1, :] + degree_ref[:, 0:1] * mvec_ref[layer, 1:2, :]
    pre = dot(wide(h_ref), weight(w_latent, f, True))
    pre = pre + dot(agg.astype(BF16), weight(w_sum, f, False)) + vector(vectors, layer, 1)
    inner = jnp.maximum(pre, 0.0).astype(BF16)
    inner = jnp.concatenate([inner[:, m * part : (m + 1) * part] for m in ORDER], axis=1)
    node = dot(inner, weight(w_out, f, True)) + vector(vectors, layer, 2)
    centred = node - jnp.mean(node, axis=1, keepdims=True)
    spread = jnp.mean(centred * centred, axis=1, keepdims=True)
    change = centred * lax.rsqrt(spread + EPSILON) * vector(vectors, layer, 4) + vector(vectors, layer, 3)
    for i, m in enumerate(ORDER):
        if final and m not in (0, 2):
            continue
        new = (h_ref[i].astype(F32) + change[:, m * part : (m + 1) * part]).astype(BF16)
        if final:
            outs[m // 2][...] = new
        else:
            outs[0][i] = new


def join_kernel(place_ref, own_ref, other_ref, out_ref):
    rows = own_ref.shape[0]
    side = place_ref[4]
    out_ref[pl.ds(pl.multiple_of(side * rows, rows), rows), :] = own_ref[...]
    out_ref[pl.ds(pl.multiple_of((1 - side) * rows, rows), rows), :] = other_ref[...]


def rows_of(weights, at, count):
    return weights, [pl.BlockSpec((count, w.shape[-1]), lambda i: (at, 0)) for w in weights]


def call(kernel, name, inputs, spaces, outs, out_spaces, scratch=(), us=2, mib=32):
    return pl.pallas_call(
        kernel,
        out_shape=outs,
        grid=(1,),
        in_specs=spaces,
        out_specs=out_spaces,
        scratch_shapes=list(scratch),
        compiler_params=pltpu.CompilerParams(vmem_limit_bytes=mib * 1024 * 1024),
        cost_estimate=pl.CostEstimate(flops=int(us * 1e9), bytes_accessed=1 << 20, transcendentals=0),
        name=name,
    )(*inputs)


def per_device(
    node_state,
    w_dst,
    w_src,
    w_msg,
    w_node_in,
    w_node_out,
    msg_vectors,
    msg_gain,
    node_vectors,
    node_gain,
    nbr_blocks,
    edge_count,
    edge_src,
    edge_dst,
):
    width = w_msg.shape[1]
    part = width // 4
    block_count, slots = nbr_blocks.shape
    edges = edge_src.shape[2]
    mine = block_count // 2
    rows = mine * edges
    feat = lax.axis_index("feat")
    dom = lax.axis_index("dom")
    side = feat // 2
    place = jnp.stack([feat, feat % 2, side * mine, dom * block_count + side * mine, side]).astype(jnp.int32)
    barrier = lax.optimization_barrier

    halves = node_state.reshape(2, rows, part)
    own = lax.dynamic_index_in_dim(halves, side, 0, keepdims=False)
    other = lax.dynamic_index_in_dim(halves, 1 - side, 0, keepdims=False)
    pack, next_pack = call(
        pack_kernel,
        "packs",
        (w_src, w_dst, w_node_in, w_node_out, node_vectors, node_gain),
        [VMEM] * 6,
        (
            jax.ShapeDtypeStruct((5 * width + 4 * VECTOR_ROWS, part), BF16),
            jax.ShapeDtypeStruct((5 * width, part), BF16),
        ),
        (HBM, HBM),
        [pltpu.VMEM((4 * VECTOR_ROWS, part), BF16), pltpu.SemaphoreType.DMA((9,))],
        mib=60,
    )
    across = exchange(other, 2)
    pack_across = exchange(pack, 2)
    beside = exchange(pack, 1)
    next_share, beside = barrier((next_pack, beside))
    next_across = from_other_side(next_share)
    next_beside = exchange(next_share, 1)

    all_slots = mine * slots + 1
    gather, collect, degree, meta = call(
        prepare_kernel,
        "one_hots",
        (place, nbr_blocks, edge_count, edge_src, edge_dst),
        [SMEM] * 3 + [VMEM] * 2,
        (
            jax.ShapeDtypeStruct((all_slots, edges, 2 * edges), BF16),
            jax.ShapeDtypeStruct((all_slots, edges, edges), BF16),
            jax.ShapeDtypeStruct((rows, edges), F32),
            jax.ShapeDtypeStruct((4, LIST), jnp.int32),
        ),
        (VMEM, VMEM, VMEM, SMEM),
        [pltpu.VMEM((edges, edges), F32)],
        us=3,
    )
    pair = jnp.stack([own, across])
    pair, pack_across, next_across, beside, next_beside, meta = barrier(
        (pair, pack_across, next_across, beside, next_beside, meta)
    )
    latent = jnp.concatenate([pair, exchange(pair, 1)], axis=0)
    pack_across = barrier((pack_across, latent))[0]
    weights = (pack, beside, pack_across, exchange(pack_across, 1))

    vectors = None
    messages = w_msg.reshape(LAYERS * 4, part, width)
    for layer in range(LAYERS):
        final = layer == LAYERS - 1
        after = swap_with(latent, 1)
        beyond = swap_with(latent, 2)
        message_spec = pl.BlockSpec((4, part, width), lambda i, layer=layer: (layer, 0, 0))
        edge_inputs = [messages, msg_vectors, gather, collect]
        edge_specs = [message_spec, VMEM, VMEM, VMEM]
        source, source_specs = rows_of(weights, 3, width)
        target, target_specs = rows_of(weights, 4, width)
        outs = [jax.ShapeDtypeStruct((rows, width), F32), jax.ShapeDtypeStruct((rows, width), BF16)]
        if layer == 0:
            outs.append(jax.ShapeDtypeStruct((4, VECTOR_ROWS, part), F32))
            extra, extra_specs = rows_of(weights, 5 * width // (4 * VECTOR_ROWS), 4 * VECTOR_ROWS)
        else:
            extra, extra_specs = (vectors,), [VMEM]
        result = call(
            lambda *refs, layer=layer: near_kernel(layer, layer == 0, *refs),
            f"near{layer}",
            [place, meta, latent, after, *edge_inputs, *source, *target, *extra],
            [SMEM, SMEM, VMEM, VMEM, *edge_specs, *source_specs, *target_specs, *extra_specs],
            outs,
            [VMEM] * len(outs),
            [
                pltpu.VMEM((2 * rows, width), BF16),
                pltpu.VMEM((UNROLL * edges, width), BF16),
                pltpu.VMEM((UNROLL * edges, width), BF16),
            ],
            us=5,
        )
        acc, receive = result[0], result[1]
        if layer == 0:
            vectors = result[2]
            next_across = barrier((next_across, acc))[0]
            next_weights = (next_pack, next_beside, next_across, exchange(next_across, 1))
        beyond, acc = barrier((beyond, acc))
        partial = call(
            lambda *refs, layer=layer: far_kernel(layer, *refs),
            f"far{layer}",
            [place, meta, beyond, *edge_inputs, acc, receive, *source],
            [SMEM, SMEM, VMEM, *edge_specs, VMEM, VMEM, *source_specs],
            jax.ShapeDtypeStruct((rows, width), BF16),
            VMEM,
            [
                pltpu.VMEM((rows, width), BF16),
                pltpu.VMEM((UNROLL * edges, width), BF16),
                pltpu.VMEM((UNROLL * edges, width), BF16),
                pltpu.VMEM((rows, width), F32),
            ],
            us=3,
        )
        theirs = exchange(partial, 1)
        if final:
            outs = [jax.ShapeDtypeStruct((rows, part), BF16)] * 2
        else:
            outs = [jax.ShapeDtypeStruct((4, rows, part), BF16)]
        matrices = [rows_of(weights, i, width) for i in range(3)]
        result = call(
            lambda *refs, layer=layer, final=final: node_kernel(layer, final, *refs),
            f"node{layer}",
            [place, latent, partial, theirs, degree, vectors, msg_vectors, msg_gain] + [w for group, _ in matrices for w in group],
            [SMEM] + [VMEM] * 7 + [spec for _, specs in matrices for spec in specs],
            outs,
            [VMEM] * len(outs),
        )
        if final:
            return call(
                join_kernel,
                "join",
                [place, result[0], exchange(result[1], 2)],
                [SMEM, VMEM, VMEM],
                jax.ShapeDtypeStruct((2 * rows, part), BF16),
                VMEM,
            )
        latent = result[0]
        weights = next_weights


def solution(mesh):
    placed = (
        P("dom", "feat"),
        P(None, None, "feat"),
        P(None, None, "feat"),
        P(),
        P(None, None, "feat"),
        P(None, None, "feat"),
        P(),
        P(),
        P(None, None, "feat"),
        P(None, "feat"),
        P("dom", None),
        P("dom", None),
        P("dom", None, None),
        P("dom", None, None),
    )
    return jax.shard_map(
        per_device, mesh=mesh, in_specs=placed, out_specs=P("dom", "feat"), check_vma=False
    )
```

```python
import jax
import jax.numpy as jnp
from jax import lax
from jax.experimental import pallas as pl
from jax.experimental.pallas import tpu as pltpu
from jax.sharding import PartitionSpec as P

LAYERS = 2
EPSILON = 1e-05
BOTH = ("dom", "feat")
F32 = jnp.float32
BF16 = jnp.bfloat16
VECTOR_ROWS = 16
ORDER = (0, 2, 1, 3)
STRAIGHT = (0, 1, 2, 3)
FROM_NEXT = (3, 2, 1, 0)
FROM_BEYOND = (2, 3, 0, 1)
UNROLL = 4
LIST = 32
VMEM = pl.BlockSpec(memory_space=pltpu.VMEM)
SMEM = pl.BlockSpec(memory_space=pltpu.SMEM)
HBM = pl.BlockSpec(memory_space=pltpu.HBM)


def dot(a, b):
    return jnp.dot(a, b, preferred_element_type=F32)


def exchange(value, mask):
    total = lax.axis_size(BOTH)
    return lax.ppermute(value, BOTH, [(i, i ^ mask) for i in range(total)])


def swap_with(value, chips):
    total = lax.axis_size(BOTH)
    step = 2 * chips + 1
    pairs = [(i, i + (step if i % 2 == 0 else -step)) for i in range(total)]
    return lax.ppermute(value, BOTH, [(i, t) for i, t in pairs if 0 <= t < total])


def from_other_side(value):
    total = lax.axis_size(BOTH)
    pairs = []
    for i in range(total):
        column, low = divmod(i, 16)
        z, core = divmod(low, 2)
        z = (z + (1 if z % 2 else -1)) % 8
        pairs.append((i, column * 16 + z * 2 + core))
    return lax.ppermute(value, BOTH, pairs)


def prepare_kernel(place_ref, nbr_ref, count_ref, src_ref, dst_ref, gather_ref, collect_ref, degree_ref, meta_ref, turned):
    last, edges, _ = gather_ref.shape
    slots = nbr_ref.shape[1]
    blocks = last // slots
    core, first, base = place_ref[1], place_ref[2], place_ref[3]
    lanes = lax.broadcasted_iota(jnp.int32, (edges, edges), 1)
    rows = lax.broadcasted_iota(jnp.int32, (edges, edges), 0)
    for i in range(LIST):
        meta_ref[0, i] = last - 1
        meta_ref[1, i] = last - 1
        meta_ref[2, i] = 0
    near, far = jnp.int32(0), jnp.int32(0)
    turned[...] = jnp.zeros_like(turned)
    for j in range(blocks):
        turned[0:slots, :] = src_ref[first + j].astype(F32)
        turned[8 : 8 + slots, :] = dst_ref[first + j].astype(F32)
        columns = turned[...].T.astype(jnp.int32)
        to_row = dst_ref[first + j]
        degree = jnp.zeros((edges, edges), F32)
        for k in range(slots):
            s = j * slots + k
            gather_ref[s, :, :edges] = (columns[:, 8 + k : 9 + k] == lanes).astype(F32).astype(BF16)
            gather_ref[s, :, edges:] = (columns[:, k : k + 1] == lanes).astype(F32).astype(BF16)
            live = ((to_row[k : k + 1, :] == rows) & (lanes < count_ref[first + j, k])).astype(F32)
            collect_ref[s] = live.astype(BF16)
            degree = degree + live
            place = nbr_ref[first + j, k] - base
            step = (place + 2 * blocks) // blocks - 2
            hops = jnp.abs(step)
            meta_ref[2, s] = hops * blocks + place - step * blocks
            mine = jnp.where(step == 0, core == j // (blocks // 2), (step > 0) == (core == 0))
            is_far = mine & (hops == 2)
            is_near = mine & (hops < 2)

            @pl.when(is_near)
            def _():
                meta_ref[0, near] = s

            @pl.when(is_far)
            def _():
                meta_ref[1, far] = s

            near = near + is_near.astype(jnp.int32)
            far = far + is_far.astype(jnp.int32)
        degree_ref[j * edges : (j + 1) * edges, :] = jnp.broadcast_to(
            jnp.sum(degree, axis=1, keepdims=True), (edges, edges)
        )
    meta_ref[3, 0] = near
    meta_ref[3, 1] = far
    gather_ref[last - 1] = jnp.zeros(gather_ref.shape[1:], BF16)
    collect_ref[last - 1] = jnp.zeros(collect_ref.shape[1:], BF16)


def pack_kernel(src_ref, dst_ref, in_ref, out_w_ref, vec_ref, gain_ref, *refs):
    outs, (rows, sems) = refs[:6], refs[6:]
    width = src_ref.shape[1]
    copies = []

    def copy(source, ref, at):
        copies.append(
            pltpu.make_async_copy(source, ref.at[pl.ds(at, source.shape[0]), :], sems.at[len(copies)])
        )
        copies[-1].start()

    for layer in range(LAYERS):
        pack, edge, node = outs[3 * layer : 3 * layer + 3]
        copy(src_ref.at[layer], edge, 0)
        copy(dst_ref.at[layer], edge, width)
        copy(src_ref.at[layer], pack, 3 * width)
        copy(dst_ref.at[layer], pack, 4 * width)
        for ref in (pack, node):
            copy(in_ref.at[layer], ref, 0)
            copy(out_w_ref.at[layer], ref, 2 * width)
    rest = jnp.concatenate(
        [part for layer in range(LAYERS) for part in (vec_ref[layer], gain_ref[layer : layer + 1, :])]
        + [jnp.zeros((VECTOR_ROWS - 5 * LAYERS, src_ref.shape[2]), F32)],
        axis=0,
    )
    for i in range(3):
        piece = rest.astype(BF16)
        rows[i * VECTOR_ROWS : (i + 1) * VECTOR_ROWS, :] = piece
        rest = rest - piece.astype(F32)
    rows[3 * VECTOR_ROWS :, :] = jnp.zeros((VECTOR_ROWS, src_ref.shape[2]), BF16)
    copy(rows, outs[0], 5 * width)
    copy(rows, outs[1], 2 * width)
    for each in copies:
        each.wait()


def wide(ref, order=STRAIGHT):
    return jnp.concatenate([ref[i] for i in order], axis=1)


def weight(shards, f, mixed):
    part = shards[0].shape[-1]
    rows = []
    for i in range(4):
        at = pl.ds(pl.multiple_of((f ^ ORDER[i]) * part, part) if mixed else i * part, part)
        rows.append(jnp.concatenate([w[at, :] for w in shards], axis=1))
    return jnp.concatenate(rows, axis=0)


def vector(vectors, layer, i):
    row = layer * 5 + i
    return jnp.concatenate([vectors[m, row : row + 1, :] for m in range(4)], axis=1)


def run_edges(which, shift, layer, f, meta_ref, receive, window, gather_ref, collect_ref, wmsg_ref, mvec_ref, hidden, normed, acc):
    slots = 6
    edges = gather_ref.shape[1]
    w_msg = jnp.concatenate([wmsg_ref[f ^ m] for m in range(4)], axis=0)
    bias = mvec_ref[layer, 0:1, :]

    def body(step, carry):
        ids = [meta_ref[which, step * UNROLL + u] for u in range(UNROLL)]
        blocks = [jnp.minimum(s // slots, 3) for s in ids]
        for u, (s, j) in enumerate(zip(ids, blocks)):
            at = meta_ref[2, s] - shift
            if which == 1:
                at = jnp.maximum(at, 0)
            to = receive[pl.ds(pl.multiple_of(j * edges, edges), edges), :]
            frm = window[pl.ds(pl.multiple_of(at * edges, edges), edges), :]
            terms = dot(gather_ref[s], jnp.concatenate([to, frm], axis=0))
            hidden[u * edges : (u + 1) * edges, :] = jnp.maximum(terms, 0.0).astype(BF16)
        for v in range(0, UNROLL, 2):
            rows = slice(v * edges, (v + 2) * edges)
            message = dot(hidden[rows, :], w_msg) + bias
            centred = message - jnp.mean(message, axis=1, keepdims=True)
            spread = jnp.mean(centred * centred, axis=1, keepdims=True)
            normed[rows, :] = (centred * lax.rsqrt(spread + EPSILON)).astype(BF16)
        for u, (s, j) in enumerate(zip(ids, blocks)):
            rows = pl.ds(pl.multiple_of(j * edges, edges), edges)
            acc[rows, :] = acc[rows, :] + dot(collect_ref[s], normed[u * edges : (u + 1) * edges, :])
        return carry

    lax.fori_loop(0, (meta_ref[3, which] + UNROLL - 1) // UNROLL, body, 0)


def near_kernel(layer, first, place_ref, meta_ref, h_ref, next_ref, wmsg_ref, mvec_ref, gather_ref, collect_ref, *refs):
    source, target, refs = refs[:4], refs[4:8], refs[8:]
    if first:
        shards, (acc, receive, vectors, window, hidden, normed) = refs[:4], refs[4:]
        for m, w in enumerate(shards):
            rows = w[...].astype(F32)
            vectors[m] = rows[:VECTOR_ROWS] + rows[VECTOR_ROWS : 2 * VECTOR_ROWS] + rows[2 * VECTOR_ROWS : 3 * VECTOR_ROWS]
    else:
        vectors, acc, receive, window, hidden, normed = refs
    f = place_ref[0]
    w_src = weight(source, f, True)
    own = wide(h_ref)
    block = own.shape[0]
    window[:block, :] = dot(own, w_src).astype(BF16)
    window[block:, :] = dot(wide(next_ref, FROM_NEXT), w_src).astype(BF16)
    receive[...] = (dot(own, weight(target, f, True)) + vector(vectors, layer, 0)).astype(BF16)
    acc[...] = jnp.zeros_like(acc)
    run_edges(0, 0, layer, f, meta_ref, receive, window, gather_ref, collect_ref, wmsg_ref, mvec_ref, hidden, normed, acc)


def far_kernel(layer, place_ref, meta_ref, after_ref, wmsg_ref, mvec_ref, gather_ref, collect_ref, acc_in, receive, w0, w1, w2, w3, out_ref, window, hidden, normed, acc):
    f = place_ref[0]
    window[...] = dot(wide(after_ref, FROM_BEYOND), weight((w0, w1, w2, w3), f, True)).astype(BF16)
    acc[...] = acc_in[...]
    run_edges(1, 8, layer, f, meta_ref, receive, window, gather_ref, collect_ref, wmsg_ref, mvec_ref, hidden, normed, acc)
    out_ref[...] = acc[...].astype(BF16)


def node_kernel(layer, final, place_ref, h_ref, part_a, part_b, degree_ref, vectors, mvec_ref, mgain_ref, *refs):
    f = place_ref[0]
    w_latent, w_sum, w_out, outs = refs[:4], refs[4:8], refs[8:12], refs[12:]
    part = h_ref.shape[-1]
    total = part_a[...].astype(F32) + part_b[...].astype(F32)
    agg = total * mgain_ref[layer : layer + 1, :] + degree_ref[:, 0:1] * mvec_ref[layer, 1:2, :]
    pre = dot(wide(h_ref), weight(w_latent, f, True))
    pre = pre + dot(agg.astype(BF16), weight(w_sum, f, False)) + vector(vectors, layer, 1)
    inner = jnp.maximum(pre, 0.0).astype(BF16)
    inner = jnp.concatenate([inner[:, m * part : (m + 1) * part] for m in ORDER], axis=1)
    node = dot(inner, weight(w_out, f, True)) + vector(vectors, layer, 2)
    centred = node - jnp.mean(node, axis=1, keepdims=True)
    spread = jnp.mean(centred * centred, axis=1, keepdims=True)
    change = centred * lax.rsqrt(spread + EPSILON) * vector(vectors, layer, 4) + vector(vectors, layer, 3)
    for i, m in enumerate(ORDER):
        if final and m not in (0, 2):
            continue
        new = (h_ref[i].astype(F32) + change[:, m * part : (m + 1) * part]).astype(BF16)
        if final:
            outs[m // 2][...] = new
        else:
            outs[0][i] = new


def join_kernel(place_ref, own_ref, other_ref, out_ref):
    rows = own_ref.shape[0]
    side = place_ref[4]
    out_ref[pl.ds(pl.multiple_of(side * rows, rows), rows), :] = own_ref[...]
    out_ref[pl.ds(pl.multiple_of((1 - side) * rows, rows), rows), :] = other_ref[...]


def rows_of(weights, matrix, width):
    inputs, specs = [], []
    for w in weights:
        at = matrix
        if isinstance(w, tuple):
            w, at = (w[0], matrix - 3) if matrix > 2 else (w[1], matrix)
        inputs.append(w)
        specs.append(pl.BlockSpec((width, w.shape[-1]), lambda i, at=at: (at, 0)))
    return inputs, specs


def vectors_of(weights):
    count = 4 * VECTOR_ROWS
    inputs = [w[0] if isinstance(w, tuple) else w for w in weights]
    return inputs, [
        pl.BlockSpec((count, w.shape[-1]), lambda i, at=w.shape[0] // count - 1: (at, 0)) for w in inputs
    ]


def call(kernel, name, inputs, spaces, outs, out_spaces, scratch=(), us=2, mib=32):
    return pl.pallas_call(
        kernel,
        out_shape=outs,
        grid=(1,),
        in_specs=spaces,
        out_specs=out_spaces,
        scratch_shapes=list(scratch),
        compiler_params=pltpu.CompilerParams(vmem_limit_bytes=mib * 1024 * 1024),
        cost_estimate=pl.CostEstimate(flops=int(us * 1e9), bytes_accessed=1 << 20, transcendentals=0),
        name=name,
    )(*inputs)


def per_device(
    node_state,
    w_dst,
    w_src,
    w_msg,
    w_node_in,
    w_node_out,
    msg_vectors,
    msg_gain,
    node_vectors,
    node_gain,
    nbr_blocks,
    edge_count,
    edge_src,
    edge_dst,
):
    width = w_msg.shape[1]
    part = width // 4
    block_count, slots = nbr_blocks.shape
    edges = edge_src.shape[2]
    mine = block_count // 2
    rows = mine * edges
    feat = lax.axis_index("feat")
    dom = lax.axis_index("dom")
    side = feat // 2
    place = jnp.stack([feat, feat % 2, side * mine, dom * block_count + side * mine, side]).astype(jnp.int32)
    barrier = lax.optimization_barrier

    halves = node_state.reshape(2, rows, part)
    own = lax.dynamic_index_in_dim(halves, side, 0, keepdims=False)
    other = lax.dynamic_index_in_dim(halves, 1 - side, 0, keepdims=False)
    extra_rows = 4 * VECTOR_ROWS
    pack, edge, node, next_pack, next_edge, next_node = call(
        pack_kernel,
        "packs",
        (w_src, w_dst, w_node_in, w_node_out, node_vectors, node_gain),
        [VMEM] * 6,
        [
            jax.ShapeDtypeStruct((count, part), BF16)
            for count in (
                5 * width + extra_rows, 2 * width + extra_rows, 3 * width, 5 * width, 2 * width, 3 * width,
            )
        ],
        [HBM] * 6,
        [pltpu.VMEM((extra_rows, part), BF16), pltpu.SemaphoreType.DMA((18,))],
        mib=60,
    )
    across = exchange(other, 2)
    edge_across = exchange(edge, 2)
    beside = exchange(pack, 1)
    next_share, beside = barrier((next_pack, beside))
    next_beside = exchange(next_share, 1)

    all_slots = mine * slots + 1
    gather, collect, degree, meta = call(
        prepare_kernel,
        "one_hots",
        (place, nbr_blocks, edge_count, edge_src, edge_dst),
        [SMEM] * 3 + [VMEM] * 2,
        (
            jax.ShapeDtypeStruct((all_slots, edges, 2 * edges), BF16),
            jax.ShapeDtypeStruct((all_slots, edges, edges), BF16),
            jax.ShapeDtypeStruct((rows, edges), F32),
            jax.ShapeDtypeStruct((4, LIST), jnp.int32),
        ),
        (VMEM, VMEM, VMEM, SMEM),
        [pltpu.VMEM((edges, edges), F32)],
        us=3,
    )
    pair = jnp.stack([own, across])
    pair, edge_across, beside, next_beside, meta = barrier((pair, edge_across, beside, next_beside, meta))
    latent = jnp.concatenate([pair, exchange(pair, 1)], axis=0)
    edge_across, node_share = barrier((edge_across, node, latent))[:2]
    edge_beyond = exchange(edge_across, 1)
    node_across = from_other_side(node_share)
    weights = (pack, beside, (edge_across, None), (edge_beyond, None))

    vectors = None
    messages = w_msg.reshape(LAYERS * 4, part, width)
    for layer in range(LAYERS):
        final = layer == LAYERS - 1
        after = swap_with(latent, 1)
        beyond = swap_with(latent, 2)
        message_spec = pl.BlockSpec((4, part, width), lambda i, layer=layer: (layer, 0, 0))
        edge_inputs = [messages, msg_vectors, gather, collect]
        edge_specs = [message_spec, VMEM, VMEM, VMEM]
        source, source_specs = rows_of(weights, 3, width)
        target, target_specs = rows_of(weights, 4, width)
        outs = [jax.ShapeDtypeStruct((rows, width), F32), jax.ShapeDtypeStruct((rows, width), BF16)]
        if layer == 0:
            outs.append(jax.ShapeDtypeStruct((4, VECTOR_ROWS, part), F32))
            extra, extra_specs = vectors_of(weights)
        else:
            extra, extra_specs = (vectors,), [VMEM]
        result = call(
            lambda *refs, layer=layer: near_kernel(layer, layer == 0, *refs),
            f"near{layer}",
            [place, meta, latent, after, *edge_inputs, *source, *target, *extra],
            [SMEM, SMEM, VMEM, VMEM, *edge_specs, *source_specs, *target_specs, *extra_specs],
            outs,
            [VMEM] * len(outs),
            [
                pltpu.VMEM((2 * rows, width), BF16),
                pltpu.VMEM((UNROLL * edges, width), BF16),
                pltpu.VMEM((UNROLL * edges, width), BF16),
            ],
            us=5,
        )
        acc, receive = result[0], result[1]
        if layer == 0:
            vectors = result[2]
            node_across, next_edge, next_node, acc = barrier((node_across, next_edge, next_node, acc))
            next_edge = exchange(next_edge, 2)
            next_node = from_other_side(next_node)
            node_beyond = exchange(node_across, 1)
            beyond, node_beyond = barrier((beyond, node_beyond))
            weights = (pack, beside, (edge_across, node_across), (edge_beyond, node_beyond))
        else:
            next_node, acc = barrier((next_node, acc))
            node_beyond = exchange(next_node, 1)
            beyond, node_beyond = barrier((beyond, node_beyond))
            weights = (next_pack, next_beside, (next_edge, next_node), (edge_beyond, node_beyond))
        beyond, acc = barrier((beyond, acc))
        partial = call(
            lambda *refs, layer=layer: far_kernel(layer, *refs),
            f"far{layer}",
            [place, meta, beyond, *edge_inputs, acc, receive, *source],
            [SMEM, SMEM, VMEM, *edge_specs, VMEM, VMEM, *source_specs],
            jax.ShapeDtypeStruct((rows, width), BF16),
            VMEM,
            [
                pltpu.VMEM((rows, width), BF16),
                pltpu.VMEM((UNROLL * edges, width), BF16),
                pltpu.VMEM((UNROLL * edges, width), BF16),
                pltpu.VMEM((rows, width), F32),
            ],
            us=3,
        )
        if layer == 0:
            next_edge, next_node, partial = barrier((next_edge, next_node, partial))
            edge_beyond = exchange(next_edge, 1)
        theirs = exchange(partial, 1)
        if layer == 0:
            theirs, edge_beyond = barrier((theirs, edge_beyond))
        if final:
            outs = [jax.ShapeDtypeStruct((rows, part), BF16)] * 2
        else:
            outs = [jax.ShapeDtypeStruct((4, rows, part), BF16)]
        matrices = [rows_of(weights, i, width) for i in range(3)]
        result = call(
            lambda *refs, layer=layer, final=final: node_kernel(layer, final, *refs),
            f"node{layer}",
            [place, latent, partial, theirs, degree, vectors, msg_vectors, msg_gain] + [w for group, _ in matrices for w in group],
            [SMEM] + [VMEM] * 7 + [spec for _, specs in matrices for spec in specs],
            outs,
            [VMEM] * len(outs),
        )
        if final:
            return call(
                join_kernel,
                "join",
                [place, result[0], exchange(result[1], 2)],
                [SMEM, VMEM, VMEM],
                jax.ShapeDtypeStruct((2 * rows, part), BF16),
                VMEM,
            )
        latent = result[0]
        weights = (next_pack, next_beside, (next_edge, None), (edge_beyond, None))


def solution(mesh):
    placed = (
        P("dom", "feat"),
        P(None, None, "feat"),
        P(None, None, "feat"),
        P(),
        P(None, None, "feat"),
        P(None, None, "feat"),
        P(),
        P(),
        P(None, None, "feat"),
        P(None, "feat"),
        P("dom", None),
        P("dom", None),
        P("dom", None, None),
        P("dom", None, None),
    )
    return jax.shard_map(
        per_device, mesh=mesh, in_specs=placed, out_specs=P("dom", "feat"), check_vma=False
    )
```

```python
import jax
import jax.numpy as jnp
from jax import lax
from jax.experimental import pallas as pl
from jax.experimental.pallas import tpu as pltpu
from jax.sharding import PartitionSpec as P

LAYERS = 2
EPSILON = 1e-05
BOTH = ("dom", "feat")
F32 = jnp.float32
BF16 = jnp.bfloat16
VECTOR_ROWS = 16
ORDER = (0, 2, 1, 3)
STRAIGHT = (0, 1, 2, 3)
FROM_NEXT = (3, 2, 1, 0)
FROM_BEYOND = (2, 3, 0, 1)
UNROLL = 4
LIST = 32
VMEM = pl.BlockSpec(memory_space=pltpu.VMEM)
SMEM = pl.BlockSpec(memory_space=pltpu.SMEM)
HBM = pl.BlockSpec(memory_space=pltpu.HBM)


def dot(a, b):
    return jnp.dot(a, b, preferred_element_type=F32)


def exchange(value, mask):
    total = lax.axis_size(BOTH)
    return lax.ppermute(value, BOTH, [(i, i ^ mask) for i in range(total)])


def swap_with(value, chips):
    total = lax.axis_size(BOTH)
    step = 2 * chips + 1
    pairs = [(i, i + (step if i % 2 == 0 else -step)) for i in range(total)]
    return lax.ppermute(value, BOTH, [(i, t) for i, t in pairs if 0 <= t < total])


def from_other_side(value):
    total = lax.axis_size(BOTH)
    pairs = []
    for i in range(total):
        column, low = divmod(i, 16)
        z, core = divmod(low, 2)
        z = (z + (1 if z % 2 else -1)) % 8
        pairs.append((i, column * 16 + z * 2 + core))
    return lax.ppermute(value, BOTH, pairs)


def prepare_kernel(place_ref, nbr_ref, count_ref, src_ref, dst_ref, gather_ref, collect_ref, degree_ref, meta_ref, turned):
    last, edges, _ = gather_ref.shape
    slots = nbr_ref.shape[1]
    blocks = last // slots
    core, first, base = place_ref[1], place_ref[2], place_ref[3]
    lanes = lax.broadcasted_iota(jnp.int32, (edges, edges), 1)
    rows = lax.broadcasted_iota(jnp.int32, (edges, edges), 0)
    for i in range(LIST):
        meta_ref[0, i] = last - 1
        meta_ref[1, i] = last - 1
        meta_ref[2, i] = 0
    near, far = jnp.int32(0), jnp.int32(0)
    turned[...] = jnp.zeros_like(turned)
    for j in range(blocks):
        turned[0:slots, :] = src_ref[first + j].astype(F32)
        turned[8 : 8 + slots, :] = dst_ref[first + j].astype(F32)
        columns = turned[...].T.astype(jnp.int32)
        to_row = dst_ref[first + j]
        degree = jnp.zeros((edges, edges), F32)
        for k in range(slots):
            s = j * slots + k
            gather_ref[s, :, :edges] = (columns[:, 8 + k : 9 + k] == lanes).astype(F32).astype(BF16)
            gather_ref[s, :, edges:] = (columns[:, k : k + 1] == lanes).astype(F32).astype(BF16)
            live = ((to_row[k : k + 1, :] == rows) & (lanes < count_ref[first + j, k])).astype(F32)
            collect_ref[s] = live.astype(BF16)
            degree = degree + live
            place = nbr_ref[first + j, k] - base
            step = (place + 2 * blocks) // blocks - 2
            hops = jnp.abs(step)
            meta_ref[2, s] = hops * blocks + place - step * blocks
            mine = jnp.where(step == 0, core == j // (blocks // 2), (step > 0) == (core == 0))
            is_far = mine & (hops == 2)
            is_near = mine & (hops < 2)

            @pl.when(is_near)
            def _():
                meta_ref[0, near] = s

            @pl.when(is_far)
            def _():
                meta_ref[1, far] = s

            near = near + is_near.astype(jnp.int32)
            far = far + is_far.astype(jnp.int32)
        degree_ref[j * edges : (j + 1) * edges, :] = jnp.broadcast_to(
            jnp.sum(degree, axis=1, keepdims=True), (edges, edges)
        )
    meta_ref[3, 0] = near
    meta_ref[3, 1] = far
    gather_ref[last - 1] = jnp.zeros(gather_ref.shape[1:], BF16)
    collect_ref[last - 1] = jnp.zeros(collect_ref.shape[1:], BF16)


def pack_kernel(src_ref, dst_ref, in_ref, out_w_ref, vec_ref, gain_ref, first_ref, next_ref, rows, sems):
    width = src_ref.shape[1]
    copies = []
    for layer, ref in enumerate((first_ref, next_ref)):
        for source, at in ((in_ref, 0), (out_w_ref, 2), (src_ref, 3), (dst_ref, 4)):
            count = source.shape[1]
            copies.append(
                pltpu.make_async_copy(
                    source.at[layer], ref.at[pl.ds(at * width, count), :], sems.at[len(copies)]
                )
            )
    for copy in copies:
        copy.start()
    rest = jnp.concatenate(
        [part for layer in range(LAYERS) for part in (vec_ref[layer], gain_ref[layer : layer + 1, :])]
        + [jnp.zeros((VECTOR_ROWS - 5 * LAYERS, src_ref.shape[2]), F32)],
        axis=0,
    )
    for i in range(3):
        piece = rest.astype(BF16)
        rows[i * VECTOR_ROWS : (i + 1) * VECTOR_ROWS, :] = piece
        rest = rest - piece.astype(F32)
    rows[3 * VECTOR_ROWS :, :] = jnp.zeros((VECTOR_ROWS, src_ref.shape[2]), BF16)
    last = pltpu.make_async_copy(
        rows, first_ref.at[pl.ds(5 * width, 4 * VECTOR_ROWS), :], sems.at[len(copies)]
    )
    last.start()
    for copy in copies:
        copy.wait()
    last.wait()


def wide(ref, order=STRAIGHT):
    return jnp.concatenate([ref[i] for i in order], axis=1)


def weight(shards, f, mixed):
    part = shards[0].shape[-1]
    rows = []
    for i in range(4):
        at = pl.ds(pl.multiple_of((f ^ ORDER[i]) * part, part) if mixed else i * part, part)
        rows.append(jnp.concatenate([w[at, :] for w in shards], axis=1))
    return jnp.concatenate(rows, axis=0)


def vector(vectors, layer, i):
    row = layer * 5 + i
    return jnp.concatenate([vectors[m, row : row + 1, :] for m in range(4)], axis=1)


def run_edges(which, shift, layer, f, meta_ref, receive, window, gather_ref, collect_ref, wmsg_ref, mvec_ref, hidden, normed, acc):
    slots = 6
    edges = gather_ref.shape[1]
    w_msg = jnp.concatenate([wmsg_ref[f ^ m] for m in range(4)], axis=0)
    bias = mvec_ref[layer, 0:1, :]

    def body(step, carry):
        ids = [meta_ref[which, step * UNROLL + u] for u in range(UNROLL)]
        blocks = [jnp.minimum(s // slots, 3) for s in ids]
        for u, (s, j) in enumerate(zip(ids, blocks)):
            at = meta_ref[2, s] - shift
            if which == 1:
                at = jnp.maximum(at, 0)
            to = receive[pl.ds(pl.multiple_of(j * edges, edges), edges), :]
            frm = window[pl.ds(pl.multiple_of(at * edges, edges), edges), :]
            terms = dot(gather_ref[s], jnp.concatenate([to, frm], axis=0))
            hidden[u * edges : (u + 1) * edges, :] = jnp.maximum(terms, 0.0).astype(BF16)
        for v in range(0, UNROLL, 2):
            rows = slice(v * edges, (v + 2) * edges)
            message = dot(hidden[rows, :], w_msg) + bias
            centred = message - jnp.mean(message, axis=1, keepdims=True)
            spread = jnp.mean(centred * centred, axis=1, keepdims=True)
            normed[rows, :] = (centred * lax.rsqrt(spread + EPSILON)).astype(BF16)
        for u, (s, j) in enumerate(zip(ids, blocks)):
            rows = pl.ds(pl.multiple_of(j * edges, edges), edges)
            acc[rows, :] = acc[rows, :] + dot(collect_ref[s], normed[u * edges : (u + 1) * edges, :])
        return carry

    lax.fori_loop(0, (meta_ref[3, which] + UNROLL - 1) // UNROLL, body, 0)


def near_kernel(layer, first, place_ref, meta_ref, h_ref, next_ref, wmsg_ref, mvec_ref, gather_ref, collect_ref, *refs):
    source, target, refs = refs[:4], refs[4:8], refs[8:]
    if first:
        shards, (acc, receive, vectors, window, hidden, normed) = refs[:4], refs[4:]
        for m, w in enumerate(shards):
            rows = w[...].astype(F32)
            vectors[m] = rows[:VECTOR_ROWS] + rows[VECTOR_ROWS : 2 * VECTOR_ROWS] + rows[2 * VECTOR_ROWS : 3 * VECTOR_ROWS]
    else:
        vectors, acc, receive, window, hidden, normed = refs
    f = place_ref[0]
    w_src = weight(source, f, True)
    own = wide(h_ref)
    block = own.shape[0]
    window[:block, :] = dot(own, w_src).astype(BF16)
    window[block:, :] = dot(wide(next_ref, FROM_NEXT), w_src).astype(BF16)
    receive[...] = (dot(own, weight(target, f, True)) + vector(vectors, layer, 0)).astype(BF16)
    acc[...] = jnp.zeros_like(acc)
    run_edges(0, 0, layer, f, meta_ref, receive, window, gather_ref, collect_ref, wmsg_ref, mvec_ref, hidden, normed, acc)


def far_kernel(layer, place_ref, meta_ref, after_ref, wmsg_ref, mvec_ref, gather_ref, collect_ref, acc_in, receive, w0, w1, w2, w3, out_ref, window, hidden, normed, acc):
    f = place_ref[0]
    window[...] = dot(wide(after_ref, FROM_BEYOND), weight((w0, w1, w2, w3), f, True)).astype(BF16)
    acc[...] = acc_in[...]
    run_edges(1, 8, layer, f, meta_ref, receive, window, gather_ref, collect_ref, wmsg_ref, mvec_ref, hidden, normed, acc)
    out_ref[...] = acc[...].astype(BF16)


def node_kernel(layer, final, place_ref, h_ref, part_a, part_b, degree_ref, vectors, mvec_ref, mgain_ref, *refs):
    f = place_ref[0]
    w_latent, w_sum, w_out, outs = refs[:4], refs[4:8], refs[8:12], refs[12:]
    part = h_ref.shape[-1]
    total = part_a[...].astype(F32) + part_b[...].astype(F32)
    agg = total * mgain_ref[layer : layer + 1, :] + degree_ref[:, 0:1] * mvec_ref[layer, 1:2, :]
    pre = dot(wide(h_ref), weight(w_latent, f, True))
    pre = pre + dot(agg.astype(BF16), weight(w_sum, f, False)) + vector(vectors, layer, 1)
    inner = jnp.maximum(pre, 0.0).astype(BF16)
    inner = jnp.concatenate([inner[:, m * part : (m + 1) * part] for m in ORDER], axis=1)
    node = dot(inner, weight(w_out, f, True)) + vector(vectors, layer, 2)
    centred = node - jnp.mean(node, axis=1, keepdims=True)
    spread = jnp.mean(centred * centred, axis=1, keepdims=True)
    change = centred * lax.rsqrt(spread + EPSILON) * vector(vectors, layer, 4) + vector(vectors, layer, 3)
    for i, m in enumerate(ORDER):
        if final and m not in (0, 2):
            continue
        new = (h_ref[i].astype(F32) + change[:, m * part : (m + 1) * part]).astype(BF16)
        if final:
            outs[m // 2][...] = new
        else:
            outs[0][i] = new


def join_kernel(place_ref, own_ref, other_ref, out_ref):
    rows = own_ref.shape[0]
    side = place_ref[4]
    out_ref[pl.ds(pl.multiple_of(side * rows, rows), rows), :] = own_ref[...]
    out_ref[pl.ds(pl.multiple_of((1 - side) * rows, rows), rows), :] = other_ref[...]


def rows_of(weights, at, count):
    return weights, [pl.BlockSpec((count, w.shape[-1]), lambda i: (at, 0)) for w in weights]


def call(kernel, name, inputs, spaces, outs, out_spaces, scratch=(), us=2, mib=32):
    return pl.pallas_call(
        kernel,
        out_shape=outs,
        grid=(1,),
        in_specs=spaces,
        out_specs=out_spaces,
        scratch_shapes=list(scratch),
        compiler_params=pltpu.CompilerParams(vmem_limit_bytes=mib * 1024 * 1024),
        cost_estimate=pl.CostEstimate(flops=int(us * 1e9), bytes_accessed=1 << 20, transcendentals=0),
        name=name,
    )(*inputs)


def per_device(
    node_state,
    w_dst,
    w_src,
    w_msg,
    w_node_in,
    w_node_out,
    msg_vectors,
    msg_gain,
    node_vectors,
    node_gain,
    nbr_blocks,
    edge_count,
    edge_src,
    edge_dst,
):
    width = w_msg.shape[1]
    part = width // 4
    block_count, slots = nbr_blocks.shape
    edges = edge_src.shape[2]
    mine = block_count // 2
    rows = mine * edges
    feat = lax.axis_index("feat")
    dom = lax.axis_index("dom")
    side = feat // 2
    place = jnp.stack([feat, feat % 2, side * mine, dom * block_count + side * mine, side]).astype(jnp.int32)
    barrier = lax.optimization_barrier

    halves = node_state.reshape(2, rows, part)
    own = lax.dynamic_index_in_dim(halves, side, 0, keepdims=False)
    other = lax.dynamic_index_in_dim(halves, 1 - side, 0, keepdims=False)
    pack, next_pack = call(
        pack_kernel,
        "packs",
        (w_src, w_dst, w_node_in, w_node_out, node_vectors, node_gain),
        [VMEM] * 6,
        (
            jax.ShapeDtypeStruct((5 * width + 4 * VECTOR_ROWS, part), BF16),
            jax.ShapeDtypeStruct((5 * width, part), BF16),
        ),
        (HBM, HBM),
        [pltpu.VMEM((4 * VECTOR_ROWS, part), BF16), pltpu.SemaphoreType.DMA((9,))],
        mib=60,
    )
    across = exchange(other, 2)
    pack_across = exchange(pack, 2)
    beside = exchange(pack, 1)
    next_share, beside = barrier((next_pack, beside))
    next_across = from_other_side(next_share)
    next_beside = exchange(next_share, 1)

    all_slots = mine * slots + 1
    gather, collect, degree, meta = call(
        prepare_kernel,
        "one_hots",
        (place, nbr_blocks, edge_count, edge_src, edge_dst),
        [SMEM] * 3 + [VMEM] * 2,
        (
            jax.ShapeDtypeStruct((all_slots, edges, 2 * edges), BF16),
            jax.ShapeDtypeStruct((all_slots, edges, edges), BF16),
            jax.ShapeDtypeStruct((rows, edges), F32),
            jax.ShapeDtypeStruct((4, LIST), jnp.int32),
        ),
        (VMEM, VMEM, VMEM, SMEM),
        [pltpu.VMEM((edges, edges), F32)],
        us=3,
    )
    pair = jnp.stack([own, across])
    latent = jnp.concatenate([pair, exchange(pair, 1)], axis=0)
    latent, pack_across, next_across, beside, next_beside, meta = barrier(
        (latent, pack_across, next_across, beside, next_beside, meta)
    )
    weights = (pack, beside, pack_across, exchange(pack_across, 1))

    vectors = None
    messages = w_msg.reshape(LAYERS * 4, part, width)
    for layer in range(LAYERS):
        final = layer == LAYERS - 1
        after = swap_with(latent, 1)
        beyond = swap_with(latent, 2)
        message_spec = pl.BlockSpec((4, part, width), lambda i, layer=layer: (layer, 0, 0))
        edge_inputs = [messages, msg_vectors, gather, collect]
        edge_specs = [message_spec, VMEM, VMEM, VMEM]
        source, source_specs = rows_of(weights, 3, width)
        target, target_specs = rows_of(weights, 4, width)
        outs = [jax.ShapeDtypeStruct((rows, width), F32), jax.ShapeDtypeStruct((rows, width), BF16)]
        if layer == 0:
            outs.append(jax.ShapeDtypeStruct((4, VECTOR_ROWS, part), F32))
            extra, extra_specs = rows_of(weights, 5 * width // (4 * VECTOR_ROWS), 4 * VECTOR_ROWS)
        else:
            extra, extra_specs = (vectors,), [VMEM]
        result = call(
            lambda *refs, layer=layer: near_kernel(layer, layer == 0, *refs),
            f"near{layer}",
            [place, meta, latent, after, *edge_inputs, *source, *target, *extra],
            [SMEM, SMEM, VMEM, VMEM, *edge_specs, *source_specs, *target_specs, *extra_specs],
            outs,
            [VMEM] * len(outs),
            [
                pltpu.VMEM((2 * rows, width), BF16),
                pltpu.VMEM((UNROLL * edges, width), BF16),
                pltpu.VMEM((UNROLL * edges, width), BF16),
            ],
            us=5,
        )
        acc, receive = result[0], result[1]
        if layer == 0:
            vectors = result[2]
            next_across = barrier((next_across, acc))[0]
            next_weights = (next_pack, next_beside, next_across, exchange(next_across, 1))
        beyond, acc = barrier((beyond, acc))
        partial = call(
            lambda *refs, layer=layer: far_kernel(layer, *refs),
            f"far{layer}",
            [place, meta, beyond, *edge_inputs, acc, receive, *source],
            [SMEM, SMEM, VMEM, *edge_specs, VMEM, VMEM, *source_specs],
            jax.ShapeDtypeStruct((rows, width), BF16),
            VMEM,
            [
                pltpu.VMEM((rows, width), BF16),
                pltpu.VMEM((UNROLL * edges, width), BF16),
                pltpu.VMEM((UNROLL * edges, width), BF16),
                pltpu.VMEM((rows, width), F32),
            ],
            us=3,
        )
        theirs = exchange(partial, 1)
        if final:
            outs = [jax.ShapeDtypeStruct((rows, part), BF16)] * 2
        else:
            outs = [jax.ShapeDtypeStruct((4, rows, part), BF16)]
        matrices = [rows_of(weights, i, width) for i in range(3)]
        result = call(
            lambda *refs, layer=layer, final=final: node_kernel(layer, final, *refs),
            f"node{layer}",
            [place, latent, partial, theirs, degree, vectors, msg_vectors, msg_gain] + [w for group, _ in matrices for w in group],
            [SMEM] + [VMEM] * 7 + [spec for _, specs in matrices for spec in specs],
            outs,
            [VMEM] * len(outs),
        )
        if final:
            return call(
                join_kernel,
                "join",
                [place, result[0], exchange(result[1], 2)],
                [SMEM, VMEM, VMEM],
                jax.ShapeDtypeStruct((2 * rows, part), BF16),
                VMEM,
            )
        latent = result[0]
        weights = next_weights


def solution(mesh):
    placed = (
        P("dom", "feat"),
        P(None, None, "feat"),
        P(None, None, "feat"),
        P(),
        P(None, None, "feat"),
        P(None, None, "feat"),
        P(),
        P(),
        P(None, None, "feat"),
        P(None, "feat"),
        P("dom", None),
        P("dom", None),
        P("dom", None, None),
        P("dom", None, None),
    )
    return jax.shard_map(
        per_device, mesh=mesh, in_specs=placed, out_specs=P("dom", "feat"), check_vma=False
    )
```

```python
import jax
import jax.numpy as jnp
from jax import lax
from jax.experimental import pallas as pl
from jax.experimental.pallas import tpu as pltpu
from jax.sharding import PartitionSpec as P

LAYERS = 2
EPSILON = 1e-05
BOTH = ("dom", "feat")
F32 = jnp.float32
BF16 = jnp.bfloat16
VECTOR_ROWS = 16
ORDER = (0, 2, 1, 3)
STRAIGHT = (0, 1, 2, 3)
FROM_NEXT = (3, 2, 1, 0)
FROM_BEYOND = (2, 3, 0, 1)
UNROLL = 4
LIST = 32
VMEM = pl.BlockSpec(memory_space=pltpu.VMEM)
SMEM = pl.BlockSpec(memory_space=pltpu.SMEM)
HBM = pl.BlockSpec(memory_space=pltpu.HBM)


def dot(a, b):
    return jnp.dot(a, b, preferred_element_type=F32)


def exchange(value, mask):
    total = lax.axis_size(BOTH)
    return lax.ppermute(value, BOTH, [(i, i ^ mask) for i in range(total)])


def swap_with(value, chips):
    total = lax.axis_size(BOTH)
    step = 2 * chips + 1
    pairs = [(i, i + (step if i % 2 == 0 else -step)) for i in range(total)]
    return lax.ppermute(value, BOTH, [(i, t) for i, t in pairs if 0 <= t < total])


def from_other_side(value):
    total = lax.axis_size(BOTH)
    pairs = []
    for i in range(total):
        column, low = divmod(i, 16)
        z, core = divmod(low, 2)
        z = (z + (1 if z % 2 else -1)) % 8
        pairs.append((i, column * 16 + z * 2 + core))
    return lax.ppermute(value, BOTH, pairs)


def prepare_kernel(place_ref, nbr_ref, count_ref, src_ref, dst_ref, gather_ref, collect_ref, degree_ref, meta_ref, turned):
    last, edges, _ = gather_ref.shape
    slots = nbr_ref.shape[1]
    blocks = last // slots
    core, first, base = place_ref[1], place_ref[2], place_ref[3]
    lanes = lax.broadcasted_iota(jnp.int32, (edges, edges), 1)
    rows = lax.broadcasted_iota(jnp.int32, (edges, edges), 0)
    for i in range(LIST):
        meta_ref[0, i] = last - 1
        meta_ref[1, i] = last - 1
        meta_ref[2, i] = 0
    near, far = jnp.int32(0), jnp.int32(0)
    turned[...] = jnp.zeros_like(turned)
    for j in range(blocks):
        turned[0:slots, :] = src_ref[first + j].astype(F32)
        turned[8 : 8 + slots, :] = dst_ref[first + j].astype(F32)
        columns = turned[...].T.astype(jnp.int32)
        to_row = dst_ref[first + j]
        degree = jnp.zeros((edges, edges), F32)
        for k in range(slots):
            s = j * slots + k
            gather_ref[s, :, :edges] = (columns[:, 8 + k : 9 + k] == lanes).astype(F32).astype(BF16)
            gather_ref[s, :, edges:] = (columns[:, k : k + 1] == lanes).astype(F32).astype(BF16)
            live = ((to_row[k : k + 1, :] == rows) & (lanes < count_ref[first + j, k])).astype(F32)
            collect_ref[s] = live.astype(BF16)
            degree = degree + live
            place = nbr_ref[first + j, k] - base
            step = (place + 2 * blocks) // blocks - 2
            hops = jnp.abs(step)
            meta_ref[2, s] = hops * blocks + place - step * blocks
            mine = jnp.where(step == 0, core == j // (blocks // 2), (step > 0) == (core == 0))
            is_far = mine & (hops == 2)
            is_near = mine & (hops < 2)

            @pl.when(is_near)
            def _():
                meta_ref[0, near] = s

            @pl.when(is_far)
            def _():
                meta_ref[1, far] = s

            near = near + is_near.astype(jnp.int32)
            far = far + is_far.astype(jnp.int32)
        degree_ref[j * edges : (j + 1) * edges, :] = jnp.broadcast_to(
            jnp.sum(degree, axis=1, keepdims=True), (edges, edges)
        )
    meta_ref[3, 0] = near
    meta_ref[3, 1] = far
    gather_ref[last - 1] = jnp.zeros(gather_ref.shape[1:], BF16)
    collect_ref[last - 1] = jnp.zeros(collect_ref.shape[1:], BF16)


def pack_kernel(src_ref, dst_ref, in_ref, out_w_ref, vec_ref, gain_ref, first_ref, next_ref, rows, sems):
    width = src_ref.shape[1]
    copies = []
    for layer, ref in enumerate((first_ref, next_ref)):
        for source, at in ((in_ref, 0), (out_w_ref, 2), (src_ref, 3), (dst_ref, 4)):
            count = source.shape[1]
            copies.append(
                pltpu.make_async_copy(
                    source.at[layer], ref.at[pl.ds(at * width, count), :], sems.at[len(copies)]
                )
            )
    for copy in copies:
        copy.start()
    rest = jnp.concatenate(
        [part for layer in range(LAYERS) for part in (vec_ref[layer], gain_ref[layer : layer + 1, :])]
        + [jnp.zeros((VECTOR_ROWS - 5 * LAYERS, src_ref.shape[2]), F32)],
        axis=0,
    )
    for i in range(3):
        piece = rest.astype(BF16)
        rows[i * VECTOR_ROWS : (i + 1) * VECTOR_ROWS, :] = piece
        rest = rest - piece.astype(F32)
    rows[3 * VECTOR_ROWS :, :] = jnp.zeros((VECTOR_ROWS, src_ref.shape[2]), BF16)
    last = pltpu.make_async_copy(
        rows, first_ref.at[pl.ds(5 * width, 4 * VECTOR_ROWS), :], sems.at[len(copies)]
    )
    last.start()
    for copy in copies:
        copy.wait()
    last.wait()


def wide(ref, order=STRAIGHT):
    return jnp.concatenate([ref[i] for i in order], axis=1)


def weight(shards, f, mixed):
    part = shards[0].shape[-1]
    rows = []
    for i in range(4):
        at = pl.ds(pl.multiple_of((f ^ ORDER[i]) * part, part) if mixed else i * part, part)
        rows.append(jnp.concatenate([w[at, :] for w in shards], axis=1))
    return jnp.concatenate(rows, axis=0)


def vector(vectors, layer, i):
    row = layer * 5 + i
    return jnp.concatenate([vectors[m, row : row + 1, :] for m in range(4)], axis=1)


def run_edges(which, shift, layer, f, meta_ref, receive, window, gather_ref, collect_ref, wmsg_ref, mvec_ref, hidden, normed, acc):
    slots = 6
    edges = gather_ref.shape[1]
    w_msg = jnp.concatenate([wmsg_ref[f ^ m] for m in range(4)], axis=0)
    bias = mvec_ref[layer, 0:1, :]

    def body(step, carry):
        ids = [meta_ref[which, step * UNROLL + u] for u in range(UNROLL)]
        blocks = [jnp.minimum(s // slots, 3) for s in ids]
        for u, (s, j) in enumerate(zip(ids, blocks)):
            at = meta_ref[2, s] - shift
            if which == 1:
                at = jnp.maximum(at, 0)
            to = receive[pl.ds(pl.multiple_of(j * edges, edges), edges), :]
            frm = window[pl.ds(pl.multiple_of(at * edges, edges), edges), :]
            terms = dot(gather_ref[s], jnp.concatenate([to, frm], axis=0))
            hidden[u * edges : (u + 1) * edges, :] = jnp.maximum(terms, 0.0).astype(BF16)
        for v in range(0, UNROLL, 2):
            rows = slice(v * edges, (v + 2) * edges)
            message = dot(hidden[rows, :], w_msg) + bias
            centred = message - jnp.mean(message, axis=1, keepdims=True)
            spread = jnp.mean(centred * centred, axis=1, keepdims=True)
            normed[rows, :] = (centred * lax.rsqrt(spread + EPSILON)).astype(BF16)
        for u, (s, j) in enumerate(zip(ids, blocks)):
            rows = pl.ds(pl.multiple_of(j * edges, edges), edges)
            acc[rows, :] = acc[rows, :] + dot(collect_ref[s], normed[u * edges : (u + 1) * edges, :])
        return carry

    lax.fori_loop(0, (meta_ref[3, which] + UNROLL - 1) // UNROLL, body, 0)


def near_kernel(layer, first, place_ref, meta_ref, h_ref, next_ref, wmsg_ref, mvec_ref, gather_ref, collect_ref, *refs):
    source, target, refs = refs[:4], refs[4:8], refs[8:]
    if first:
        shards, (acc, receive, vectors, window, hidden, normed) = refs[:4], refs[4:]
        for m, w in enumerate(shards):
            rows = w[...].astype(F32)
            vectors[m] = rows[:VECTOR_ROWS] + rows[VECTOR_ROWS : 2 * VECTOR_ROWS] + rows[2 * VECTOR_ROWS : 3 * VECTOR_ROWS]
    else:
        vectors, acc, receive, window, hidden, normed = refs
    f = place_ref[0]
    w_src = weight(source, f, True)
    own = wide(h_ref)
    block = own.shape[0]
    window[:block, :] = dot(own, w_src).astype(BF16)
    window[block:, :] = dot(wide(next_ref, FROM_NEXT), w_src).astype(BF16)
    receive[...] = (dot(own, weight(target, f, True)) + vector(vectors, layer, 0)).astype(BF16)
    acc[...] = jnp.zeros_like(acc)
    run_edges(0, 0, layer, f, meta_ref, receive, window, gather_ref, collect_ref, wmsg_ref, mvec_ref, hidden, normed, acc)


def far_kernel(layer, place_ref, meta_ref, after_ref, wmsg_ref, mvec_ref, gather_ref, collect_ref, acc_in, receive, w0, w1, w2, w3, out_ref, window, hidden, normed, acc):
    f = place_ref[0]
    window[...] = dot(wide(after_ref, FROM_BEYOND), weight((w0, w1, w2, w3), f, True)).astype(BF16)
    acc[...] = acc_in[...]
    run_edges(1, 8, layer, f, meta_ref, receive, window, gather_ref, collect_ref, wmsg_ref, mvec_ref, hidden, normed, acc)
    out_ref[...] = acc[...].astype(BF16)


def node_kernel(layer, final, place_ref, h_ref, part_a, part_b, degree_ref, vectors, mvec_ref, mgain_ref, *refs):
    f = place_ref[0]
    w_latent, w_sum, w_out, outs = refs[:4], refs[4:8], refs[8:12], refs[12:]
    part = h_ref.shape[-1]
    total = part_a[...].astype(F32) + part_b[...].astype(F32)
    agg = total * mgain_ref[layer : layer + 1, :] + degree_ref[:, 0:1] * mvec_ref[layer, 1:2, :]
    pre = dot(wide(h_ref), weight(w_latent, f, True))
    pre = pre + dot(agg.astype(BF16), weight(w_sum, f, False)) + vector(vectors, layer, 1)
    inner = jnp.maximum(pre, 0.0).astype(BF16)
    inner = jnp.concatenate([inner[:, m * part : (m + 1) * part] for m in ORDER], axis=1)
    node = dot(inner, weight(w_out, f, True)) + vector(vectors, layer, 2)
    centred = node - jnp.mean(node, axis=1, keepdims=True)
    spread = jnp.mean(centred * centred, axis=1, keepdims=True)
    change = centred * lax.rsqrt(spread + EPSILON) * vector(vectors, layer, 4) + vector(vectors, layer, 3)
    for i, m in enumerate(ORDER):
        if final and m not in (0, 2):
            continue
        new = (h_ref[i].astype(F32) + change[:, m * part : (m + 1) * part]).astype(BF16)
        if final:
            outs[m // 2][...] = new
        else:
            outs[0][i] = new


def join_kernel(place_ref, own_ref, other_ref, out_ref):
    rows = own_ref.shape[0]
    side = place_ref[4]
    out_ref[pl.ds(pl.multiple_of(side * rows, rows), rows), :] = own_ref[...]
    out_ref[pl.ds(pl.multiple_of((1 - side) * rows, rows), rows), :] = other_ref[...]


def rows_of(weights, at, count):
    return weights, [pl.BlockSpec((count, w.shape[-1]), lambda i: (at, 0)) for w in weights]


def call(kernel, name, inputs, spaces, outs, out_spaces, scratch=(), us=2, mib=32):
    return pl.pallas_call(
        kernel,
        out_shape=outs,
        grid=(1,),
        in_specs=spaces,
        out_specs=out_spaces,
        scratch_shapes=list(scratch),
        compiler_params=pltpu.CompilerParams(vmem_limit_bytes=mib * 1024 * 1024),
        cost_estimate=pl.CostEstimate(flops=int(us * 1e9), bytes_accessed=1 << 20, transcendentals=0),
        name=name,
    )(*inputs)


def per_device(
    node_state,
    w_dst,
    w_src,
    w_msg,
    w_node_in,
    w_node_out,
    msg_vectors,
    msg_gain,
    node_vectors,
    node_gain,
    nbr_blocks,
    edge_count,
    edge_src,
    edge_dst,
):
    width = w_msg.shape[1]
    part = width // 4
    block_count, slots = nbr_blocks.shape
    edges = edge_src.shape[2]
    mine = block_count // 2
    rows = mine * edges
    feat = lax.axis_index("feat")
    dom = lax.axis_index("dom")
    side = feat // 2
    place = jnp.stack([feat, feat % 2, side * mine, dom * block_count + side * mine, side]).astype(jnp.int32)
    barrier = lax.optimization_barrier

    halves = node_state.reshape(2, rows, part)
    own = lax.dynamic_index_in_dim(halves, side, 0, keepdims=False)
    other = lax.dynamic_index_in_dim(halves, 1 - side, 0, keepdims=False)
    pack, next_pack = call(
        pack_kernel,
        "packs",
        (w_src, w_dst, w_node_in, w_node_out, node_vectors, node_gain),
        [VMEM] * 6,
        (
            jax.ShapeDtypeStruct((5 * width + 4 * VECTOR_ROWS, part), BF16),
            jax.ShapeDtypeStruct((5 * width, part), BF16),
        ),
        (HBM, HBM),
        [pltpu.VMEM((4 * VECTOR_ROWS, part), BF16), pltpu.SemaphoreType.DMA((9,))],
        mib=60,
    )
    across = exchange(other, 2)
    pack_across = exchange(pack, 2)
    beside = exchange(pack, 1)
    next_share, beside = barrier((next_pack, beside))
    next_across = from_other_side(next_share)
    next_beside = exchange(next_share, 1)

    all_slots = mine * slots + 1
    gather, collect, degree, meta = call(
        prepare_kernel,
        "one_hots",
        (place, nbr_blocks, edge_count, edge_src, edge_dst),
        [SMEM] * 3 + [VMEM] * 2,
        (
            jax.ShapeDtypeStruct((all_slots, edges, 2 * edges), BF16),
            jax.ShapeDtypeStruct((all_slots, edges, edges), BF16),
            jax.ShapeDtypeStruct((rows, edges), F32),
            jax.ShapeDtypeStruct((4, LIST), jnp.int32),
        ),
        (VMEM, VMEM, VMEM, SMEM),
        [pltpu.VMEM((edges, edges), F32)],
        us=3,
    )
    pair = jnp.stack([own, across])
    latent = jnp.concatenate([pair, exchange(pair, 1)], axis=0)
    vectors = None
    messages = w_msg.reshape(LAYERS * 4, part, width)
    for layer in range(LAYERS):
        final = layer == LAYERS - 1
        after = swap_with(latent, 1)
        beyond = swap_with(latent, 2)
        if layer == 0:
            after, beyond, pack_across, next_across, beside, next_beside, meta = barrier(
                (after, beyond, pack_across, next_across, beside, next_beside, meta)
            )
            weights = (pack, beside, pack_across, exchange(pack_across, 1))
        message_spec = pl.BlockSpec((4, part, width), lambda i, layer=layer: (layer, 0, 0))
        edge_inputs = [messages, msg_vectors, gather, collect]
        edge_specs = [message_spec, VMEM, VMEM, VMEM]
        source, source_specs = rows_of(weights, 3, width)
        target, target_specs = rows_of(weights, 4, width)
        outs = [jax.ShapeDtypeStruct((rows, width), F32), jax.ShapeDtypeStruct((rows, width), BF16)]
        if layer == 0:
            outs.append(jax.ShapeDtypeStruct((4, VECTOR_ROWS, part), F32))
            extra, extra_specs = rows_of(weights, 5 * width // (4 * VECTOR_ROWS), 4 * VECTOR_ROWS)
        else:
            extra, extra_specs = (vectors,), [VMEM]
        result = call(
            lambda *refs, layer=layer: near_kernel(layer, layer == 0, *refs),
            f"near{layer}",
            [place, meta, latent, after, *edge_inputs, *source, *target, *extra],
            [SMEM, SMEM, VMEM, VMEM, *edge_specs, *source_specs, *target_specs, *extra_specs],
            outs,
            [VMEM] * len(outs),
            [
                pltpu.VMEM((2 * rows, width), BF16),
                pltpu.VMEM((UNROLL * edges, width), BF16),
                pltpu.VMEM((UNROLL * edges, width), BF16),
            ],
            us=5,
        )
        acc, receive = result[0], result[1]
        if layer == 0:
            vectors = result[2]
            next_across = barrier((next_across, acc))[0]
            next_weights = (next_pack, next_beside, next_across, exchange(next_across, 1))
        beyond, acc = barrier((beyond, acc))
        partial = call(
            lambda *refs, layer=layer: far_kernel(layer, *refs),
            f"far{layer}",
            [place, meta, beyond, *edge_inputs, acc, receive, *source],
            [SMEM, SMEM, VMEM, *edge_specs, VMEM, VMEM, *source_specs],
            jax.ShapeDtypeStruct((rows, width), BF16),
            VMEM,
            [
                pltpu.VMEM((rows, width), BF16),
                pltpu.VMEM((UNROLL * edges, width), BF16),
                pltpu.VMEM((UNROLL * edges, width), BF16),
                pltpu.VMEM((rows, width), F32),
            ],
            us=3,
        )
        theirs = exchange(partial, 1)
        if final:
            outs = [jax.ShapeDtypeStruct((rows, part), BF16)] * 2
        else:
            outs = [jax.ShapeDtypeStruct((4, rows, part), BF16)]
        matrices = [rows_of(weights, i, width) for i in range(3)]
        result = call(
            lambda *refs, layer=layer, final=final: node_kernel(layer, final, *refs),
            f"node{layer}",
            [place, latent, partial, theirs, degree, vectors, msg_vectors, msg_gain] + [w for group, _ in matrices for w in group],
            [SMEM] + [VMEM] * 7 + [spec for _, specs in matrices for spec in specs],
            outs,
            [VMEM] * len(outs),
        )
        if final:
            return call(
                join_kernel,
                "join",
                [place, result[0], exchange(result[1], 2)],
                [SMEM, VMEM, VMEM],
                jax.ShapeDtypeStruct((2 * rows, part), BF16),
                VMEM,
            )
        latent = result[0]
        weights = next_weights


def solution(mesh):
    placed = (
        P("dom", "feat"),
        P(None, None, "feat"),
        P(None, None, "feat"),
        P(),
        P(None, None, "feat"),
        P(None, None, "feat"),
        P(),
        P(),
        P(None, None, "feat"),
        P(None, "feat"),
        P("dom", None),
        P("dom", None),
        P("dom", None, None),
        P("dom", None, None),
    )
    return jax.shard_map(
        per_device, mesh=mesh, in_specs=placed, out_specs=P("dom", "feat"), check_vma=False
    )
```

```python
import jax
import jax.numpy as jnp
from jax import lax
from jax.experimental import pallas as pl
from jax.experimental.pallas import tpu as pltpu
from jax.sharding import PartitionSpec as P

LAYERS = 2
EPSILON = 1e-05
BOTH = ("dom", "feat")
F32 = jnp.float32
BF16 = jnp.bfloat16
VECTOR_ROWS = 16
ORDER = (0, 2, 1, 3)
STRAIGHT = (0, 1, 2, 3)
FROM_NEXT = (3, 2, 1, 0)
FROM_BEYOND = (2, 3, 0, 1)
UNROLL = 2
LIST = 32
VMEM = pl.BlockSpec(memory_space=pltpu.VMEM)
SMEM = pl.BlockSpec(memory_space=pltpu.SMEM)
HBM = pl.BlockSpec(memory_space=pltpu.HBM)


def dot(a, b):
    return jnp.dot(a, b, preferred_element_type=F32)


def exchange(value, mask):
    total = lax.axis_size(BOTH)
    return lax.ppermute(value, BOTH, [(i, i ^ mask) for i in range(total)])


def swap_with(value, chips):
    total = lax.axis_size(BOTH)
    step = 2 * chips + 1
    pairs = [(i, i + (step if i % 2 == 0 else -step)) for i in range(total)]
    return lax.ppermute(value, BOTH, [(i, t) for i, t in pairs if 0 <= t < total])


def from_other_side(value):
    total = lax.axis_size(BOTH)
    pairs = []
    for i in range(total):
        column, low = divmod(i, 16)
        z, core = divmod(low, 2)
        z = (z + (1 if z % 2 else -1)) % 8
        pairs.append((i, column * 16 + z * 2 + core))
    return lax.ppermute(value, BOTH, pairs)


def prepare_kernel(place_ref, nbr_ref, count_ref, src_ref, dst_ref, gather_ref, collect_ref, degree_ref, meta_ref, turned):
    last, edges, _ = gather_ref.shape
    slots = nbr_ref.shape[1]
    blocks = last // slots
    core, first, base = place_ref[1], place_ref[2], place_ref[3]
    lanes = lax.broadcasted_iota(jnp.int32, (edges, edges), 1)
    rows = lax.broadcasted_iota(jnp.int32, (edges, edges), 0)
    for i in range(LIST):
        meta_ref[0, i] = last - 1
        meta_ref[1, i] = last - 1
        meta_ref[2, i] = 0
    near, far = jnp.int32(0), jnp.int32(0)
    turned[...] = jnp.zeros_like(turned)
    for j in range(blocks):
        turned[0:slots, :] = src_ref[first + j].astype(F32)
        turned[8 : 8 + slots, :] = dst_ref[first + j].astype(F32)
        columns = turned[...].T.astype(jnp.int32)
        to_row = dst_ref[first + j]
        degree = jnp.zeros((edges, edges), F32)
        for k in range(slots):
            s = j * slots + k
            gather_ref[s, :, :edges] = (columns[:, 8 + k : 9 + k] == lanes).astype(F32).astype(BF16)
            gather_ref[s, :, edges:] = (columns[:, k : k + 1] == lanes).astype(F32).astype(BF16)
            live = ((to_row[k : k + 1, :] == rows) & (lanes < count_ref[first + j, k])).astype(F32)
            collect_ref[s] = live.astype(BF16)
            degree = degree + live
            place = nbr_ref[first + j, k] - base
            step = (place + 2 * blocks) // blocks - 2
            hops = jnp.abs(step)
            meta_ref[2, s] = hops * blocks + place - step * blocks
            mine = jnp.where(step == 0, core == j // (blocks // 2), (step > 0) == (core == 0))
            is_far = mine & (hops == 2)
            is_near = mine & (hops < 2)

            @pl.when(is_near)
            def _():
                meta_ref[0, near] = s

            @pl.when(is_far)
            def _():
                meta_ref[1, far] = s

            near = near + is_near.astype(jnp.int32)
            far = far + is_far.astype(jnp.int32)
        degree_ref[j * edges : (j + 1) * edges, :] = jnp.broadcast_to(
            jnp.sum(degree, axis=1, keepdims=True), (edges, edges)
        )
    meta_ref[3, 0] = near
    meta_ref[3, 1] = far
    gather_ref[last - 1] = jnp.zeros(gather_ref.shape[1:], BF16)
    collect_ref[last - 1] = jnp.zeros(collect_ref.shape[1:], BF16)


def pack_kernel(src_ref, dst_ref, in_ref, out_w_ref, vec_ref, gain_ref, first_ref, next_ref, rows, sems):
    width = src_ref.shape[1]
    copies = []
    for layer, ref in enumerate((first_ref, next_ref)):
        for source, at in ((in_ref, 0), (out_w_ref, 2), (src_ref, 3), (dst_ref, 4)):
            count = source.shape[1]
            copies.append(
                pltpu.make_async_copy(
                    source.at[layer], ref.at[pl.ds(at * width, count), :], sems.at[len(copies)]
                )
            )
    for copy in copies:
        copy.start()
    rest = jnp.concatenate(
        [part for layer in range(LAYERS) for part in (vec_ref[layer], gain_ref[layer : layer + 1, :])]
        + [jnp.zeros((VECTOR_ROWS - 5 * LAYERS, src_ref.shape[2]), F32)],
        axis=0,
    )
    for i in range(3):
        piece = rest.astype(BF16)
        rows[i * VECTOR_ROWS : (i + 1) * VECTOR_ROWS, :] = piece
        rest = rest - piece.astype(F32)
    rows[3 * VECTOR_ROWS :, :] = jnp.zeros((VECTOR_ROWS, src_ref.shape[2]), BF16)
    last = pltpu.make_async_copy(
        rows, first_ref.at[pl.ds(5 * width, 4 * VECTOR_ROWS), :], sems.at[len(copies)]
    )
    last.start()
    for copy in copies:
        copy.wait()
    last.wait()


def wide(ref, order=STRAIGHT):
    return jnp.concatenate([ref[i] for i in order], axis=1)


def weight(shards, f, mixed):
    part = shards[0].shape[-1]
    rows = []
    for i in range(4):
        at = pl.ds(pl.multiple_of((f ^ ORDER[i]) * part, part) if mixed else i * part, part)
        rows.append(jnp.concatenate([w[at, :] for w in shards], axis=1))
    return jnp.concatenate(rows, axis=0)


def vector(vectors, layer, i):
    row = layer * 5 + i
    return jnp.concatenate([vectors[m, row : row + 1, :] for m in range(4)], axis=1)


def run_edges(which, shift, layer, f, meta_ref, receive, window, gather_ref, collect_ref, wmsg_ref, mvec_ref, hidden, normed, acc):
    slots = 6
    edges = gather_ref.shape[1]
    w_msg = jnp.concatenate([wmsg_ref[f ^ m] for m in range(4)], axis=0)
    bias = mvec_ref[layer, 0:1, :]

    def body(step, carry):
        ids = [meta_ref[which, step * UNROLL + u] for u in range(UNROLL)]
        blocks = [jnp.minimum(s // slots, 3) for s in ids]
        for u, (s, j) in enumerate(zip(ids, blocks)):
            at = meta_ref[2, s] - shift
            if which == 1:
                at = jnp.maximum(at, 0)
            to = receive[pl.ds(pl.multiple_of(j * edges, edges), edges), :]
            frm = window[pl.ds(pl.multiple_of(at * edges, edges), edges), :]
            terms = dot(gather_ref[s], jnp.concatenate([to, frm], axis=0))
            hidden[u * edges : (u + 1) * edges, :] = jnp.maximum(terms, 0.0).astype(BF16)
        for v in range(0, UNROLL, 2):
            rows = slice(v * edges, (v + 2) * edges)
            message = dot(hidden[rows, :], w_msg) + bias
            centred = message - jnp.mean(message, axis=1, keepdims=True)
            spread = jnp.mean(centred * centred, axis=1, keepdims=True)
            normed[rows, :] = (centred * lax.rsqrt(spread + EPSILON)).astype(BF16)
        for u, (s, j) in enumerate(zip(ids, blocks)):
            rows = pl.ds(pl.multiple_of(j * edges, edges), edges)
            acc[rows, :] = acc[rows, :] + dot(collect_ref[s], normed[u * edges : (u + 1) * edges, :])
        return carry

    lax.fori_loop(0, (meta_ref[3, which] + UNROLL - 1) // UNROLL, body, 0)


def near_kernel(layer, first, place_ref, meta_ref, h_ref, next_ref, wmsg_ref, mvec_ref, gather_ref, collect_ref, *refs):
    source, target, refs = refs[:4], refs[4:8], refs[8:]
    if first:
        shards, (acc, receive, vectors, window, hidden, normed) = refs[:4], refs[4:]
        for m, w in enumerate(shards):
            rows = w[...].astype(F32)
            vectors[m] = rows[:VECTOR_ROWS] + rows[VECTOR_ROWS : 2 * VECTOR_ROWS] + rows[2 * VECTOR_ROWS : 3 * VECTOR_ROWS]
    else:
        vectors, acc, receive, window, hidden, normed = refs
    f = place_ref[0]
    w_src = weight(source, f, True)
    own = wide(h_ref)
    block = own.shape[0]
    window[:block, :] = dot(own, w_src).astype(BF16)
    window[block:, :] = dot(wide(next_ref, FROM_NEXT), w_src).astype(BF16)
    receive[...] = (dot(own, weight(target, f, True)) + vector(vectors, layer, 0)).astype(BF16)
    acc[...] = jnp.zeros_like(acc)
    run_edges(0, 0, layer, f, meta_ref, receive, window, gather_ref, collect_ref, wmsg_ref, mvec_ref, hidden, normed, acc)


def far_kernel(layer, place_ref, meta_ref, after_ref, wmsg_ref, mvec_ref, gather_ref, collect_ref, acc_in, receive, w0, w1, w2, w3, out_ref, window, hidden, normed, acc):
    f = place_ref[0]
    window[...] = dot(wide(after_ref, FROM_BEYOND), weight((w0, w1, w2, w3), f, True)).astype(BF16)
    acc[...] = acc_in[...]
    run_edges(1, 8, layer, f, meta_ref, receive, window, gather_ref, collect_ref, wmsg_ref, mvec_ref, hidden, normed, acc)
    out_ref[...] = acc[...].astype(BF16)


def node_kernel(layer, final, place_ref, h_ref, part_a, part_b, degree_ref, vectors, mvec_ref, mgain_ref, *refs):
    f = place_ref[0]
    w_latent, w_sum, w_out, outs = refs[:4], refs[4:8], refs[8:12], refs[12:]
    part = h_ref.shape[-1]
    total = part_a[...].astype(F32) + part_b[...].astype(F32)
    agg = total * mgain_ref[layer : layer + 1, :] + degree_ref[:, 0:1] * mvec_ref[layer, 1:2, :]
    pre = dot(wide(h_ref), weight(w_latent, f, True))
    pre = pre + dot(agg.astype(BF16), weight(w_sum, f, False)) + vector(vectors, layer, 1)
    inner = jnp.maximum(pre, 0.0).astype(BF16)
    inner = jnp.concatenate([inner[:, m * part : (m + 1) * part] for m in ORDER], axis=1)
    node = dot(inner, weight(w_out, f, True)) + vector(vectors, layer, 2)
    centred = node - jnp.mean(node, axis=1, keepdims=True)
    spread = jnp.mean(centred * centred, axis=1, keepdims=True)
    change = centred * lax.rsqrt(spread + EPSILON) * vector(vectors, layer, 4) + vector(vectors, layer, 3)
    for i, m in enumerate(ORDER):
        if final and m not in (0, 2):
            continue
        new = (h_ref[i].astype(F32) + change[:, m * part : (m + 1) * part]).astype(BF16)
        if final:
            outs[m // 2][...] = new
        else:
            outs[0][i] = new


def join_kernel(place_ref, own_ref, other_ref, out_ref):
    rows = own_ref.shape[0]
    side = place_ref[4]
    out_ref[pl.ds(pl.multiple_of(side * rows, rows), rows), :] = own_ref[...]
    out_ref[pl.ds(pl.multiple_of((1 - side) * rows, rows), rows), :] = other_ref[...]


def rows_of(weights, at, count):
    return weights, [pl.BlockSpec((count, w.shape[-1]), lambda i: (at, 0)) for w in weights]


def call(kernel, name, inputs, spaces, outs, out_spaces, scratch=(), us=2, mib=32):
    return pl.pallas_call(
        kernel,
        out_shape=outs,
        grid=(1,),
        in_specs=spaces,
        out_specs=out_spaces,
        scratch_shapes=list(scratch),
        compiler_params=pltpu.CompilerParams(vmem_limit_bytes=mib * 1024 * 1024),
        cost_estimate=pl.CostEstimate(flops=int(us * 1e9), bytes_accessed=1 << 20, transcendentals=0),
        name=name,
    )(*inputs)


def per_device(
    node_state,
    w_dst,
    w_src,
    w_msg,
    w_node_in,
    w_node_out,
    msg_vectors,
    msg_gain,
    node_vectors,
    node_gain,
    nbr_blocks,
    edge_count,
    edge_src,
    edge_dst,
):
    width = w_msg.shape[1]
    part = width // 4
    block_count, slots = nbr_blocks.shape
    edges = edge_src.shape[2]
    mine = block_count // 2
    rows = mine * edges
    feat = lax.axis_index("feat")
    dom = lax.axis_index("dom")
    side = feat // 2
    place = jnp.stack([feat, feat % 2, side * mine, dom * block_count + side * mine, side]).astype(jnp.int32)
    barrier = lax.optimization_barrier

    halves = node_state.reshape(2, rows, part)
    own = lax.dynamic_index_in_dim(halves, side, 0, keepdims=False)
    other = lax.dynamic_index_in_dim(halves, 1 - side, 0, keepdims=False)
    pack, next_pack = call(
        pack_kernel,
        "packs",
        (w_src, w_dst, w_node_in, w_node_out, node_vectors, node_gain),
        [VMEM] * 6,
        (
            jax.ShapeDtypeStruct((5 * width + 4 * VECTOR_ROWS, part), BF16),
            jax.ShapeDtypeStruct((5 * width, part), BF16),
        ),
        (HBM, HBM),
        [pltpu.VMEM((4 * VECTOR_ROWS, part), BF16), pltpu.SemaphoreType.DMA((9,))],
        mib=60,
    )
    across = exchange(other, 2)
    pack_across = exchange(pack, 2)
    beside = exchange(pack, 1)
    next_share, beside = barrier((next_pack, beside))
    next_across = from_other_side(next_share)
    next_beside = exchange(next_share, 1)

    all_slots = mine * slots + 1
    gather, collect, degree, meta = call(
        prepare_kernel,
        "one_hots",
        (place, nbr_blocks, edge_count, edge_src, edge_dst),
        [SMEM] * 3 + [VMEM] * 2,
        (
            jax.ShapeDtypeStruct((all_slots, edges, 2 * edges), BF16),
            jax.ShapeDtypeStruct((all_slots, edges, edges), BF16),
            jax.ShapeDtypeStruct((rows, edges), F32),
            jax.ShapeDtypeStruct((4, LIST), jnp.int32),
        ),
        (VMEM, VMEM, VMEM, SMEM),
        [pltpu.VMEM((edges, edges), F32)],
        us=3,
    )
    pair = jnp.stack([own, across])
    pair, pack_across, next_across, beside, next_beside, meta = barrier(
        (pair, pack_across, next_across, beside, next_beside, meta)
    )
    latent = jnp.concatenate([pair, exchange(pair, 1)], axis=0)
    pack_across = barrier((pack_across, latent))[0]
    weights = (pack, beside, pack_across, exchange(pack_across, 1))

    vectors = None
    messages = w_msg.reshape(LAYERS * 4, part, width)
    for layer in range(LAYERS):
        final = layer == LAYERS - 1
        after = swap_with(latent, 1)
        beyond = swap_with(latent, 2)
        message_spec = pl.BlockSpec((4, part, width), lambda i, layer=layer: (layer, 0, 0))
        edge_inputs = [messages, msg_vectors, gather, collect]
        edge_specs = [message_spec, VMEM, VMEM, VMEM]
        source, source_specs = rows_of(weights, 3, width)
        target, target_specs = rows_of(weights, 4, width)
        outs = [jax.ShapeDtypeStruct((rows, width), F32), jax.ShapeDtypeStruct((rows, width), BF16)]
        if layer == 0:
            outs.append(jax.ShapeDtypeStruct((4, VECTOR_ROWS, part), F32))
            extra, extra_specs = rows_of(weights, 5 * width // (4 * VECTOR_ROWS), 4 * VECTOR_ROWS)
        else:
            extra, extra_specs = (vectors,), [VMEM]
        result = call(
            lambda *refs, layer=layer: near_kernel(layer, layer == 0, *refs),
            f"near{layer}",
            [place, meta, latent, after, *edge_inputs, *source, *target, *extra],
            [SMEM, SMEM, VMEM, VMEM, *edge_specs, *source_specs, *target_specs, *extra_specs],
            outs,
            [VMEM] * len(outs),
            [
                pltpu.VMEM((2 * rows, width), BF16),
                pltpu.VMEM((UNROLL * edges, width), BF16),
                pltpu.VMEM((UNROLL * edges, width), BF16),
            ],
            us=5,
        )
        acc, receive = result[0], result[1]
        if layer == 0:
            vectors = result[2]
            next_across = barrier((next_across, acc))[0]
            next_weights = (next_pack, next_beside, next_across, exchange(next_across, 1))
        beyond, acc = barrier((beyond, acc))
        partial = call(
            lambda *refs, layer=layer: far_kernel(layer, *refs),
            f"far{layer}",
            [place, meta, beyond, *edge_inputs, acc, receive, *source],
            [SMEM, SMEM, VMEM, *edge_specs, VMEM, VMEM, *source_specs],
            jax.ShapeDtypeStruct((rows, width), BF16),
            VMEM,
            [
                pltpu.VMEM((rows, width), BF16),
                pltpu.VMEM((UNROLL * edges, width), BF16),
                pltpu.VMEM((UNROLL * edges, width), BF16),
                pltpu.VMEM((rows, width), F32),
            ],
            us=3,
        )
        theirs = exchange(partial, 1)
        if final:
            outs = [jax.ShapeDtypeStruct((rows, part), BF16)] * 2
        else:
            outs = [jax.ShapeDtypeStruct((4, rows, part), BF16)]
        matrices = [rows_of(weights, i, width) for i in range(3)]
        result = call(
            lambda *refs, layer=layer, final=final: node_kernel(layer, final, *refs),
            f"node{layer}",
            [place, latent, partial, theirs, degree, vectors, msg_vectors, msg_gain] + [w for group, _ in matrices for w in group],
            [SMEM] + [VMEM] * 7 + [spec for _, specs in matrices for spec in specs],
            outs,
            [VMEM] * len(outs),
        )
        if final:
            return call(
                join_kernel,
                "join",
                [place, result[0], exchange(result[1], 2)],
                [SMEM, VMEM, VMEM],
                jax.ShapeDtypeStruct((2 * rows, part), BF16),
                VMEM,
            )
        latent = result[0]
        weights = next_weights


def solution(mesh):
    placed = (
        P("dom", "feat"),
        P(None, None, "feat"),
        P(None, None, "feat"),
        P(),
        P(None, None, "feat"),
        P(None, None, "feat"),
        P(),
        P(),
        P(None, None, "feat"),
        P(None, "feat"),
        P("dom", None),
        P("dom", None),
        P("dom", None, None),
        P("dom", None, None),
    )
    return jax.shard_map(
        per_device, mesh=mesh, in_specs=placed, out_specs=P("dom", "feat"), check_vma=False
    )
```
